32 devices in a mesh: band: 8 (over z, x), col: 2 (over core), head: 2 (over y).
Axes of the slice: x: 2, y: 2, z: 4, core: 2. Of those that a mesh axis runs over, the one named last changes fastest.
Arguments:
- act_in: bfloat16 [80, 80, 512], P('band', ('col', 'head')), may hold values from -6 to 6
- ln_gain: float32 [2, 2, 512], replicated, may hold values from 0.1 to 1.9
- ln_bias: float32 [2, 2, 512], replicated, may hold values from -1.5 to 1.5
- w_qkv: bfloat16 [2, 512, 1536], P(None, None, 'head'), may hold values from -0.25 to 0.25
- b_qv: float32 [2, 1024], P(None, 'head'), may hold values from -1.5 to 1.5
- rel_table: float32 [2, 361, 16], P(None, None, 'head'), may hold values from -4 to 4
- w_proj: bfloat16 [2, 512, 512], P(None, 'head'), may hold values from -0.75 to 0.75
- b_proj: float32 [2, 512], replicated, may hold values from -1.5 to 1.5
- w_fc1: bfloat16 [2, 512, 2048], P(None, None, 'head'), may hold values from -0.25 to 0.25
- b_fc1: float32 [2, 2048], P(None, 'head'), may hold values from -1.5 to 1.5
- w_fc2: bfloat16 [2, 2048, 512], P(None, 'head'), may hold values from -0.125 to 0.125
- b_fc2: float32 [2, 512], replicated, may hold values from -1.5 to 1.5
- grad_out: float32 [80, 80, 512], P('band', ('col', 'head')), may hold values from -6 to 6
Outputs:
- act_out: float32 [80, 80, 512], P('band', ('col', 'head'))
- grad_in: float32 [80, 80, 512], P('band', ('col', 'head'))
- grad_ln_gain: float32 [2, 2, 512], replicated
- grad_ln_bias: float32 [2, 2, 512], replicated
- grad_w_qkv: float32 [2, 512, 1536], P(None, None, 'head')
- grad_b_qv: float32 [2, 1024], P(None, 'head')
- grad_rel_table: float32 [2, 361, 16], P(None, None, 'head')
- grad_w_proj: float32 [2, 512, 512], P(None, 'head')
- grad_b_proj: float32 [2, 512], replicated
- grad_w_fc1: float32 [2, 512, 2048], P(None, None, 'head')
- grad_b_fc1: float32 [2, 2048], P(None, 'head')
- grad_w_fc2: float32 [2, 2048, 512], P(None, 'head')
- grad_b_fc2: float32 [2, 512], replicated
The draws below stay inside these ranges and needn't reach their ends.
All inputs are finite; a program needn't handle non-finite values.
Results may differ from the reference program's by a relative error of at most 0.035.
Values may be sent and summed in bfloat16 or wider, within the bound.
No kernel may reach another device: no remote copies, remote signals or barrier semaphores. Data moves between devices by JAX's collectives and lax.ppermute only.
A program may use at most 128 MiB of HBM per device.

```python
import jax
import jax.numpy as jnp
from jax import lax

D = 512
HEADS = 16
HEAD_DIM = 32
FF = 2048
WIN = 10
SHIFT = 5
BLOCKS = 2
ROWS = 80
COLS = 80
TABLE = 361


def block_levels(key, shape, cuts, smallest, top_value):
    factor_of = 1.0
    for position, parts in cuts:
        steps = jax.random.uniform(jax.random.fold_in(jax.random.fold_in(key, 6), position), (parts,), jnp.float32, smallest / len(cuts), top_value / len(cuts))
        factor_of = factor_of * jnp.repeat(jnp.exp(steps), shape[position] // parts).reshape((-1,) + (1,) * (len(shape) - 1 - position))
    return factor_of


def centred(key, dims, deviation, bound, pieces=(), kind=jnp.bfloat16):
    factor_of = block_levels(key, dims, pieces, -0.22, 0.18) if pieces else 1.0
    values = jax.random.normal(key, dims, jnp.float32) * deviation * factor_of
    return jnp.minimum(jnp.maximum(values, -bound), bound).astype(kind)


def setup_inputs(seed: int = 0) -> dict:
    streams_of = jax.random.split(jax.random.key(seed), 14)
    act_in = centred(streams_of[0], (ROWS, COLS, D), 1.0, 6.0, ((0, 8), (1, 4)))
    ln_gain = jnp.clip(1.0 + 0.18 * jax.random.normal(streams_of[1], (BLOCKS, 2, D), jnp.float32), 0.1, 1.9)
    ln_bias = centred(streams_of[2], (BLOCKS, 2, D), 0.3, 1.5, (), jnp.float32)
    w_qkv = centred(streams_of[3], (BLOCKS, D, 3 * D), D ** -0.5, 0.25, ((2, 2),))
    b_qv = centred(streams_of[4], (BLOCKS, 2 * D), 0.3, 1.5, ((1, 2),), jnp.float32)
    rel_table = centred(streams_of[5], (BLOCKS, TABLE, HEADS), 1.0, 4.0, ((2, 2),), jnp.float32)
    w_proj = centred(streams_of[6], (BLOCKS, D, D), (D // 8) ** -0.5, 0.75, ((1, 2),))
    b_proj = centred(streams_of[7], (BLOCKS, D), 0.3, 1.5, (), jnp.float32)
    w_fc1 = centred(streams_of[8], (BLOCKS, D, FF), D ** -0.5, 0.25, ((2, 2),))
    b_fc1 = centred(streams_of[9], (BLOCKS, FF), 0.3, 1.5, ((1, 2),), jnp.float32)
    w_fc2 = centred(streams_of[10], (BLOCKS, FF, D), FF ** -0.5, 0.125, ((1, 2),))
    b_fc2 = centred(streams_of[11], (BLOCKS, D), 0.3, 1.5, (), jnp.float32)
    grad_out = centred(streams_of[12], (ROWS, COLS, D), 1.0, 6.0, ((0, 8), (1, 4)), jnp.float32)
    return {"act_in": act_in, "ln_gain": ln_gain, "ln_bias": ln_bias, "w_qkv": w_qkv, "b_qv": b_qv, "rel_table": rel_table, "w_proj": w_proj, "b_proj": b_proj, "w_fc1": w_fc1, "b_fc1": b_fc1, "w_fc2": w_fc2, "b_fc2": b_fc2, "grad_out": grad_out}


@jax.custom_vjp
def low(v):
    return lax.optimization_barrier(v.astype(jnp.bfloat16)).astype(jnp.float32)

@jax.custom_vjp
def low_back(v):
    return v

def low_keep(v):
    return (low(v), None)

def low_pass(kept, grad):
    return (grad,)

def back_keep(v):
    return (v, None)

def back_low(kept, grad):
    return (low(grad),)
low.defvjp(low_keep, low_pass)
low_back.defvjp(back_keep, back_low)
EPSILON = 1e-05
HIGHEST = lax.Precision.HIGHEST

def layer_norm(array, gain_row, bias_row):
    centre = array - lax.optimization_barrier(jnp.mean(array, axis=-1, keepdims=True))
    spread = lax.optimization_barrier(jnp.mean(centre * centre, axis=-1, keepdims=True))
    return centre * lax.rsqrt(spread + EPSILON) * gain_row + bias_row

def offsets(window):
    places = jnp.arange(window, dtype=jnp.int32)
    spread = jnp.arange(2 * window - 1, dtype=jnp.int32)
    return (spread[None, None, :] == places[:, None, None] - places[None, :, None] + window - 1).astype(jnp.float32)

def position_bias(table, window):
    head_count = table.shape[-1]
    table_grid = table.reshape(2 * window - 1, 2 * window - 1, head_count)
    onehot = offsets(window)
    full = jnp.einsum('ika,jlb,abh->hijkl', onehot, onehot, table_grid, precision=HIGHEST)
    return full.reshape(head_count, window * window, window * window)

def partition(array, window):
    height, breadth = (array.shape[0], array.shape[1])
    others = array.shape[2:]
    split = array.reshape((height // window, window, breadth // window, window) + others)
    split = jnp.moveaxis(split, 2, 1)
    return split.reshape((height // window, breadth // window, window * window) + others)

def unpartition(array, window):
    row_count, col_count = (array.shape[0], array.shape[1])
    others = array.shape[3:]
    split = array.reshape((row_count, col_count, window, window) + others)
    split = jnp.moveaxis(split, 1, 2)
    return split.reshape((row_count * window, col_count * window) + others)

def region_ids(places, extent):
    return (places >= extent - WIN).astype(jnp.int32) + (places >= extent - SHIFT).astype(jnp.int32)

def shift_mask(height, breadth):
    rows_id = region_ids(jnp.arange(height, dtype=jnp.int32), height)
    cols_id = region_ids(jnp.arange(breadth, dtype=jnp.int32), breadth)
    region = 3 * rows_id[:, None] + cols_id[None, :]
    windows = partition(region, WIN)
    return jnp.where(windows[..., :, None] != windows[..., None, :], -100.0, 0.0).astype(jnp.float32)

def attend(queries, key_rows, values, region_mask, offset):
    logits = jnp.einsum('cqhd,ckhd->chqk', queries, key_rows, precision=HIGHEST) * HEAD_DIM ** (-0.5)
    logits = low_back(logits + offset[None] + region_mask[:, None])
    largest = lax.optimization_barrier(jnp.max(logits, axis=-1, keepdims=True))
    expval = jnp.exp(logits - largest)
    probs = low(expval / lax.optimization_barrier(jnp.sum(expval, axis=-1, keepdims=True)))
    return jnp.einsum('chqk,ckhd->cqhd', probs, values, precision=HIGHEST)

def swin_block(residual, weights, shifted, region_mask):
    norm_gain, norm_bias, w_qkv, b_qv, table, w_proj, b_proj, w_fc1, b_fc1, w_fc2, b_fc2 = weights
    normed = low(layer_norm(residual, norm_gain[0], norm_bias[0]))
    if shifted:
        normed = jnp.roll(low_back(normed), (-SHIFT, -SHIFT), (0, 1))
    windows = partition(normed, WIN)
    row_count, col_count = (windows.shape[0], windows.shape[1])
    projected = jnp.einsum('rctd,de->rcte', windows, w_qkv, precision=HIGHEST)
    projected = projected.reshape(row_count, col_count, WIN * WIN, HEADS, 3, HEAD_DIM)
    qv_bias = b_qv.reshape(HEADS, 2, HEAD_DIM)
    queries = low_back(low(projected[..., 0, :] + qv_bias[:, 0]))
    key_rows = low_back(low(projected[..., 1, :]))
    values = low_back(low(projected[..., 2, :] + qv_bias[:, 1]))
    offset = position_bias(table, WIN)
    masks = region_mask if shifted else jnp.zeros_like(region_mask)
    context = lax.map(lambda items: jax.checkpoint(attend)(items[0], items[1], items[2], items[3], offset), (queries, key_rows, values, masks))
    context = low_back(low(context)).reshape(row_count, col_count, WIN * WIN, HEADS * HEAD_DIM)
    branch = low_back(jnp.einsum('rctd,de->rcte', context, w_proj, precision=HIGHEST) + b_proj)
    if shifted:
        branch = low(branch)
    branch = unpartition(branch, WIN)
    if shifted:
        branch = jnp.roll(branch, (SHIFT, SHIFT), (0, 1))
    middle = residual + branch
    second = low(layer_norm(middle, norm_gain[1], norm_bias[1]))
    hidden = low_back(jnp.einsum('rcd,df->rcf', second, w_fc1, precision=HIGHEST) + b_fc1)
    active = low(jax.nn.gelu(hidden, approximate=False))
    return middle + low_back(jnp.einsum('rcf,fd->rcd', active, w_fc2, precision=HIGHEST) + b_fc2)

def forward(residual, *weights):
    region_mask = shift_mask(residual.shape[0], residual.shape[1])
    for block_id in range(BLOCKS):
        layer_weights = tuple((member[block_id] for member in weights))
        residual = swin_block(residual, layer_weights, block_id % 2 == 1, region_mask)
    return residual

def reference(act_in, ln_gain, ln_bias, w_qkv, b_qv, rel_table, w_proj, b_proj, w_fc1, b_fc1, w_fc2, b_fc2, grad_out):
    inputs = (act_in.astype(jnp.float32), ln_gain.astype(jnp.float32), ln_bias.astype(jnp.float32), w_qkv.astype(jnp.float32), b_qv.astype(jnp.float32), rel_table.astype(jnp.float32), w_proj.astype(jnp.float32), b_proj.astype(jnp.float32), w_fc1.astype(jnp.float32), b_fc1.astype(jnp.float32), w_fc2.astype(jnp.float32), b_fc2.astype(jnp.float32))
    result, pull = jax.vjp(forward, *inputs)
    grads = pull(grad_out.astype(jnp.float32))
    return (result, grads[0], grads[1], grads[2], grads[3], grads[4], grads[5], grads[6], grads[7], grads[8], grads[9], grads[10], grads[11])
```

```python
from functools import partial

import jax
import jax.numpy as jnp
import numpy as np
from jax import lax
from jax.experimental import pallas as pl
from jax.experimental.pallas import tpu as pltpu
from jax.sharding import PartitionSpec as P

HEAD_DIM = 32
WIN = 10
SHIFT = 5
BLOCKS = 2


EPSILON = 1e-05
HIGHEST = lax.Precision.HIGHEST


def shifted_2(value, axis, steps):
    count = lax.axis_size(axis)
    pairs = [(source, (source + steps) % count) for source in range(count)]
    return lax.ppermute(value, axis, pairs)


def layer_norm(array, gain_row, bias_row):
    centre = array - jnp.mean(array, axis=-1, keepdims=True)
    spread = jnp.mean(centre * centre, axis=-1, keepdims=True)
    return centre * lax.rsqrt(spread + EPSILON) * gain_row + bias_row


def offsets(window):
    places = jnp.arange(window, dtype=jnp.int32)
    spread = jnp.arange(2 * window - 1, dtype=jnp.int32)
    return (
        spread[None, None, :] == places[:, None, None] - places[None, :, None] + window - 1
    ).astype(jnp.float32)


def position_bias(table):
    head_count = table.shape[-1]
    table_grid = table.reshape(2 * WIN - 1, 2 * WIN - 1, head_count)
    onehot = offsets(WIN)
    full = jnp.einsum("ika,jlb,abh->hijkl", onehot, onehot, table_grid, precision=HIGHEST)
    return full.reshape(head_count, WIN * WIN, WIN * WIN)


def table_grad(grad_offset):
    head_count = grad_offset.shape[0]
    onehot = offsets(WIN)
    spread = grad_offset.reshape(head_count, WIN, WIN, WIN, WIN)
    full = jnp.einsum("ika,jlb,hijkl->abh", onehot, onehot, spread, precision=HIGHEST)
    return full.reshape((2 * WIN - 1) * (2 * WIN - 1), head_count)


def gather_tile(array):
    return lax.all_gather(array, "head", axis=1, tiled=True)


def sum_tile(array):
    return lax.psum_scatter(
        array.astype(jnp.bfloat16), "head", scatter_dimension=1, tiled=True
    ).astype(jnp.float32)


def gather_grad(array):
    return lax.all_gather(array, "head", axis=1, tiled=True)


def sum_grad(array):
    return lax.psum_scatter(
        array.astype(jnp.bfloat16), "head", scatter_dimension=1, tiled=True
    ).astype(jnp.float32)


def roll_ahead(array):
    upper = shifted_2(array[:SHIFT], "band", -1)
    array = jnp.concatenate([array[SHIFT:], upper], axis=0)
    leftmost = shifted_2(array[:, :SHIFT], ("col", "head"), -1)
    return jnp.concatenate([array[:, SHIFT:], leftmost], axis=1)


def roll_behind(array):
    lower = shifted_2(array[-SHIFT:], "band", 1)
    array = jnp.concatenate([lower, array[:-SHIFT]], axis=0)
    rightmost = shifted_2(array[:, -SHIFT:], ("col", "head"), 1)
    return jnp.concatenate([rightmost, array[:, :-SHIFT]], axis=1)


def pack_members(members):
    group = lax.axis_size("band") * lax.axis_size("col")
    flat = jnp.concatenate([member.reshape(-1) for member in members])
    padding = -flat.shape[0] % group
    return jnp.concatenate([flat, jnp.zeros((padding,), jnp.float32)])


def unpack_members(flat, members):
    result = []
    start = 0
    for member in members:
        count = member.size
        result.append(flat[start : start + count].reshape(member.shape))
        start = start + count
    return tuple(result)


def to_windows(tile_rows):
    height, breadth, depth = tile_rows.shape
    window_count = breadth // height
    split = tile_rows.reshape(height, window_count, height, depth).transpose(1, 0, 2, 3)
    return split.reshape(window_count * height * height, depth)


def from_windows(flat_rows, height):
    window_count = flat_rows.shape[0] // (height * height)
    depth = flat_rows.shape[1]
    split = flat_rows.reshape(window_count, height, height, depth).transpose(1, 0, 2, 3)
    return split.reshape(height, window_count * height, depth)


def region_ids(places, extent):
    return (places >= extent - WIN).astype(jnp.int32) + (places >= extent - SHIFT).astype(jnp.int32)


def shift_mask(breadth):
    rows_all = WIN * lax.axis_size("band")
    cols_all = breadth * lax.axis_size("col")
    rows_here = WIN * lax.axis_index("band") + jnp.arange(WIN, dtype=jnp.int32)
    cols_here = breadth * lax.axis_index("col") + jnp.arange(breadth, dtype=jnp.int32)
    region = 3 * region_ids(rows_here, rows_all)[:, None] + region_ids(cols_here, cols_all)[None, :]
    window_count = breadth // WIN
    labels = to_windows(region[:, :, None])[:, 0].reshape(window_count, WIN * WIN)
    return jnp.where(labels[:, :, None] != labels[:, None, :], -100.0, 0.0).astype(jnp.float32)


def scores(queries, key_rows, offset, region_mask):
    logits = jnp.einsum("wqhd,wkhd->whqk", queries, key_rows, preferred_element_type=jnp.float32)
    logits = logits * HEAD_DIM ** (-0.5) + offset[None]
    if region_mask is not None:
        logits = logits + region_mask[:, None]
    return logits


def forward_block(source, weights, shifted):
    norm_gain, norm_bias, w_qkv, b_qv, table, w_proj, b_proj, w_fc1, b_fc1, w_fc2, b_fc2 = weights
    height = source.shape[0]
    heads_here = table.shape[-1]
    normed = layer_norm(source, norm_gain[0], norm_bias[0]).astype(jnp.bfloat16)
    if shifted:
        normed = roll_ahead(normed)
    gathered = gather_tile(normed)
    window_count = gathered.shape[1] // height
    flat_rows = to_windows(gathered)
    projected = jnp.dot(flat_rows, w_qkv, preferred_element_type=jnp.float32)
    projected = projected.reshape(window_count, height * height, heads_here, 3, HEAD_DIM)
    qv_bias = b_qv.reshape(heads_here, 2, HEAD_DIM)
    queries = (projected[..., 0, :] + qv_bias[:, 0]).astype(jnp.bfloat16)
    key_rows = projected[..., 1, :].astype(jnp.bfloat16)
    values = (projected[..., 2, :] + qv_bias[:, 1]).astype(jnp.bfloat16)
    offset = position_bias(table)
    region_mask = shift_mask(gathered.shape[1]) if shifted else None
    logits = scores(queries, key_rows, offset, region_mask)
    log_total = jax.nn.logsumexp(logits, axis=-1)
    probs_low = jnp.exp(logits - log_total[..., None]).astype(jnp.bfloat16)
    context = jnp.einsum("whqk,wkhd->wqhd", probs_low, values, preferred_element_type=jnp.float32)
    context = context.astype(jnp.bfloat16).reshape(
        window_count * height * height, heads_here * HEAD_DIM
    )
    partial_out = from_windows(jnp.dot(context, w_proj, preferred_element_type=jnp.float32), height)
    branch = sum_tile(partial_out) + b_proj
    if shifted:
        branch = roll_behind(branch.astype(jnp.bfloat16)).astype(jnp.float32)
    middle = source + branch
    second = layer_norm(middle, norm_gain[1], norm_bias[1]).astype(jnp.bfloat16)
    second_tile = gather_tile(second)
    mlp_rows = second_tile.reshape(-1, second_tile.shape[-1])
    hidden = jnp.dot(mlp_rows, w_fc1, preferred_element_type=jnp.float32) + b_fc1
    active = jax.nn.gelu(hidden, approximate=False).astype(jnp.bfloat16)
    out_part = jnp.dot(active, w_fc2, preferred_element_type=jnp.float32).reshape(second_tile.shape)
    result = middle + sum_tile(out_part) + b_fc2
    saved_state = (
        source,
        middle,
        flat_rows,
        queries,
        key_rows,
        values,
        log_total,
        context,
        mlp_rows,
        hidden,
        offset,
        region_mask,
    )
    return (result, saved_state)


def backward_block(upstream, weights, saved_state, shifted):
    norm_gain, norm_bias, w_qkv, b_qv, table, w_proj, b_proj, w_fc1, b_fc1, w_fc2, b_fc2 = weights
    (
        source,
        middle,
        flat_rows,
        queries,
        key_rows,
        values,
        log_total,
        context,
        mlp_rows,
        hidden,
        offset,
        region_mask,
    ) = saved_state
    height = source.shape[0]
    window_count, window_len, heads_here, _ = queries.shape
    grad_low = upstream.astype(jnp.bfloat16)
    grad_tile = gather_grad(grad_low)
    grad_rows = grad_tile.reshape(-1, grad_tile.shape[-1])
    active = jax.nn.gelu(hidden, approximate=False).astype(jnp.bfloat16)
    g_fc2 = jnp.dot(active.T, grad_rows, preferred_element_type=jnp.float32)
    g_bfc2 = jnp.sum(grad_low.astype(jnp.float32), axis=(0, 1))
    g_active = jnp.dot(grad_rows, w_fc2.T, preferred_element_type=jnp.float32)
    g_hidden = jax.vjp(partial(jax.nn.gelu, approximate=False), hidden)[1](g_active)[0].astype(
        jnp.bfloat16
    )
    g_bfc1 = jnp.sum(g_hidden.astype(jnp.float32), axis=0)
    g_fc1 = jnp.dot(mlp_rows.T, g_hidden, preferred_element_type=jnp.float32)
    g_second = sum_grad(
        jnp.dot(g_hidden, w_fc1.T, preferred_element_type=jnp.float32).reshape(grad_tile.shape)
    )
    pull_second = jax.vjp(layer_norm, middle, norm_gain[1], norm_bias[1])[1]
    g_mid_norm, g_gain2, g_bias2 = pull_second(g_second)
    g_middle = upstream + g_mid_norm
    g_branch = g_middle.astype(jnp.bfloat16)
    if shifted:
        g_branch = roll_ahead(g_branch)
    g_bproj = jnp.sum(g_branch.astype(jnp.float32), axis=(0, 1))
    g_output = to_windows(gather_grad(g_branch))
    g_proj = jnp.dot(context.T, g_output, preferred_element_type=jnp.float32)
    g_context = jnp.dot(g_output, w_proj.T, preferred_element_type=jnp.float32).astype(jnp.bfloat16)
    g_context = g_context.reshape(window_count, window_len, heads_here, HEAD_DIM)
    logits = scores(queries, key_rows, offset, region_mask)
    probs = jnp.exp(logits - log_total[..., None])
    probs_low = probs.astype(jnp.bfloat16)
    g_values = jnp.einsum(
        "whqk,wqhd->wkhd", probs_low, g_context, preferred_element_type=jnp.float32
    ).astype(jnp.bfloat16)
    g_probs = jnp.einsum("wqhd,wkhd->whqk", g_context, values, preferred_element_type=jnp.float32)
    centre = jnp.sum(probs * g_probs, axis=-1, keepdims=True)
    g_logits = (probs * (g_probs - centre)).astype(jnp.bfloat16)
    g_table = table_grad(jnp.sum(g_logits.astype(jnp.float32), axis=0))
    inv_root = HEAD_DIM ** (-0.5)
    g_queries = (
        jnp.einsum("whqk,wkhd->wqhd", g_logits, key_rows, preferred_element_type=jnp.float32)
        * inv_root
    ).astype(jnp.bfloat16)
    g_keys = (
        jnp.einsum("whqk,wqhd->wkhd", g_logits, queries, preferred_element_type=jnp.float32)
        * inv_root
    ).astype(jnp.bfloat16)
    g_mixed = jnp.stack([g_queries, g_keys, g_values], axis=3).reshape(
        window_count * window_len, heads_here * 3 * HEAD_DIM
    )
    g_bqv = jnp.stack(
        [
            jnp.sum(g_queries.astype(jnp.float32), axis=(0, 1)),
            jnp.sum(g_values.astype(jnp.float32), axis=(0, 1)),
        ],
        axis=1,
    ).reshape(-1)
    g_qkv = jnp.dot(flat_rows.T, g_mixed, preferred_element_type=jnp.float32)
    g_first = sum_grad(
        from_windows(jnp.dot(g_mixed, w_qkv.T, preferred_element_type=jnp.float32), height)
    )
    if shifted:
        g_first = roll_behind(g_first.astype(jnp.bfloat16)).astype(jnp.float32)
    pull_first = jax.vjp(layer_norm, source, norm_gain[0], norm_bias[0])[1]
    g_source, g_gain1, g_bias1 = pull_first(g_first)
    g_input = g_middle + g_source
    sharded = (g_qkv, g_bqv, g_table, g_proj, g_fc1, g_bfc1, g_fc2)
    shared = (jnp.stack([g_gain1, g_gain2]), jnp.stack([g_bias1, g_bias2]), g_bproj, g_bfc2)
    return (g_input, sharded, shared)


def on_device(
    act_in,
    ln_gain,
    ln_bias,
    w_qkv,
    b_qv,
    rel_table,
    w_proj,
    b_proj,
    w_fc1,
    b_fc1,
    w_fc2,
    b_fc2,
    grad_out,
):
    params = (ln_gain, ln_bias, w_qkv, b_qv, rel_table, w_proj, b_proj, w_fc1, b_fc1, w_fc2, b_fc2)
    layers = [tuple((member[block_id] for member in params)) for block_id in range(BLOCKS)]
    residual = act_in.astype(jnp.float32)
    layer_inputs = []
    stored = []
    for block_id in range(BLOCKS):
        layer_inputs.append(residual)
        residual, saved_state = forward_block(residual, layers[block_id], block_id % 2 == 1)
        stored.append(saved_state)
    upstream = grad_out
    sharded_all = [None] * BLOCKS
    shared_all = [None] * BLOCKS
    for block_id in reversed(range(BLOCKS)):
        saved_state = forward_block(layer_inputs[block_id], layers[block_id], block_id % 2 == 1)[1]
        upstream, sharded, shared = backward_block(
            upstream, layers[block_id], saved_state, block_id % 2 == 1
        )
        sharded_all[block_id] = sharded
        shared_all[block_id] = shared
    sharded_stack = tuple(
        (jnp.stack([entry[member] for entry in sharded_all]) for member in range(7))
    )
    shared_stack = tuple(
        (jnp.stack([entry[member] for entry in shared_all]) for member in range(4))
    )
    packed_all = pack_members(sharded_stack)
    packed_part = lax.psum_scatter(
        packed_all.astype(jnp.bfloat16), ("band", "col"), scatter_dimension=0, tiled=True
    ).astype(jnp.float32)
    packed_all = lax.all_gather(
        packed_part.astype(jnp.bfloat16), ("band", "col"), axis=0, tiled=True
    ).astype(packed_part.dtype)
    sharded_stack = unpack_members(packed_all, sharded_stack)
    shared_stack = lax.psum(shared_stack, ("band", "col", "head"))
    return (
        residual,
        upstream,
        shared_stack[0],
        shared_stack[1],
        sharded_stack[0],
        sharded_stack[1],
        sharded_stack[2],
        sharded_stack[3],
        shared_stack[2],
        sharded_stack[4],
        sharded_stack[5],
        sharded_stack[6],
        shared_stack[3],
    )


F32 = jnp.float32
BF16 = jnp.bfloat16
WIDTH = 512
QUAD = 32
LIVE = SHIFT * SHIFT
UNIT = 2 * QUAD
TOK = 2 * UNIT
TILE = 4 * UNIT
PAIR = 2 * TILE
GROUP = 8
SPAN = GROUP * HEAD_DIM
KEYS = GROUP * TOK
OFFSETS = 2 * WIN - 1
ENTRIES = 384
SCALE = HEAD_DIM ** (-0.5)
FAR = -1e30
ROOT_HALF = 0.5 ** 0.5
ROOT_TWO_PI = (2.0 * np.pi) ** (-0.5)
VMEM = pl.BlockSpec(memory_space=pltpu.VMEM)
SMEM = pl.BlockSpec(memory_space=pltpu.SMEM)
ROWS_QKV = 3 * 512
ROWS_ATT = ROWS_QKV + 512
ROWS_MLP = 4096


def shape_of(shape, kind):
    return jax.ShapeDtypeStruct(shape, kind)


def layer_spec(array, layer):
    rest = array.shape[1:]
    return pl.BlockSpec((1,) + rest, lambda _: (layer,) + (0,) * len(rest), pipeline_mode=pl.Buffered(1))


def run_kernel(kernel, operands, outs, scratch=(), limit=40, specs=None, aliases=None, out_specs=None, flops=0):
    specs = specs or {}
    in_specs = [specs.get(place, VMEM) for place in range(len(operands))]
    return pl.pallas_call(
        kernel,
        grid=(1,),
        in_specs=in_specs,
        out_specs=out_specs or [VMEM] * len(outs),
        out_shape=list(outs),
        scratch_shapes=list(scratch),
        input_output_aliases=aliases or {},
        cost_estimate=pl.CostEstimate(flops=flops, bytes_accessed=1 << 20, transcendentals=0),
        compiler_params=pltpu.CompilerParams(vmem_limit_bytes=limit << 20),
    )(*operands)


def mm(left, right):
    return lax.dot_general(left, right, (((1,), (0,)), ((), ())), preferred_element_type=F32)


def mm_nt(left, right):
    return lax.dot_general(left, right, (((1,), (1,)), ((), ())), preferred_element_type=F32)


def mm_tn(left, right):
    return lax.dot_general(left, right, (((0,), (0,)), ((), ())), preferred_element_type=F32)


def halves_of(value):
    high = value.astype(BF16)
    return high, (value - high.astype(F32)).astype(BF16)


def norm_parts(value):
    centre = value - jnp.mean(value, axis=-1, keepdims=True)
    inverse = lax.rsqrt(jnp.mean(centre * centre, axis=-1, keepdims=True) + EPSILON)
    return centre * inverse, inverse


def norm_back(grad, gain, unit, inverse):
    scaled = grad * gain
    return (
        scaled
        - jnp.mean(scaled, axis=-1, keepdims=True)
        - unit * jnp.mean(scaled * unit, axis=-1, keepdims=True)
    ) * inverse


def column_sum(value):
    return jnp.sum(value, axis=0, keepdims=True)


def put_row(ref, row, value):
    for part in range(value.shape[1] // 256):
        ref[row + part : row + part + 1, :] = value[:, 256 * part : 256 * (part + 1)]


def token_place(row, col):
    return ((col // SHIFT) * 2 + row // SHIFT) * QUAD + (row % SHIFT) * SHIFT + col % SHIFT


def constants():
    row_map = np.zeros((TOK, 160), np.float32)
    col_map = np.zeros((TOK, TOK), np.float32)
    token_row = np.zeros((TOK,), np.int32)
    token_col = np.zeros((TOK,), np.int32)
    for row in range(WIN):
        for col in range(WIN):
            place = token_place(row, col)
            row_map[place, row * 16 + col] = 1.0
            col_map[row * WIN + col, place] = 1.0
            token_row[place] = row
            token_col[place] = col
    base = np.full((1, 256), -4000, np.int32)
    for lane in range(OFFSETS * WIN):
        base[0, lane] = (OFFSETS - 1 - lane // WIN) * OFFSETS - lane % WIN + WIN - 1
    order = np.zeros((768, 768), np.float32)
    for head in range(GROUP):
        for part in range(3):
            for place in range(HEAD_DIM):
                order[head * 96 + part * 32 + place, part * SPAN + head * HEAD_DIM + place] = 1.0
    heads = np.zeros((KEYS, SPAN), np.float32)
    for head in range(GROUP):
        heads[head * TOK : (head + 1) * TOK, head * HEAD_DIM : (head + 1) * HEAD_DIM] = 1.0
    return (
        jnp.asarray(row_map, BF16),
        jnp.asarray(col_map, BF16),
        jnp.asarray(base),
        jnp.asarray(order, BF16),
        jnp.asarray(heads, BF16),
        token_row,
        token_col,
    )


def enter_kernel(in_ref, out_ref, buf):
    buf[...] = jnp.zeros(buf.shape, F32)
    for row in range(WIN):
        line = in_ref[row].astype(F32)
        for unit in range(4):
            start = unit * UNIT + (row // SHIFT) * QUAD + (row % SHIFT) * SHIFT
            buf[start : start + SHIFT, :] = line[unit * SHIFT : (unit + 1) * SHIFT, :]
    out_ref[...] = buf[...].astype(BF16)


def enter_units(tile):
    return run_kernel(
        enter_kernel, [tile], [shape_of((TILE, WIDTH), BF16)], [pltpu.VMEM((TILE, WIDTH), F32)]
    )[0]


def leave_rows(value_ref, out_ref):
    for row in range(WIN):
        for unit in range(4):
            start = unit * UNIT + (row // SHIFT) * QUAD + (row % SHIFT) * SHIFT
            out_ref[row, unit * SHIFT : (unit + 1) * SHIFT, :] = value_ref[start : start + SHIFT, :]


def leave_kernel(in_ref, out_ref, buf):
    buf[...] = in_ref[...].astype(F32)
    leave_rows(buf, out_ref)


def leave_units(rows):
    return run_kernel(
        leave_kernel, [rows], [shape_of((WIN, 2 * WIN, WIDTH), F32)], [pltpu.VMEM((TILE, WIDTH), F32)]
    )[0]


def entry_onehot(base_ref, col):
    entry = lax.broadcasted_iota(jnp.int32, (ENTRIES, 256), 0)
    return (entry == base_ref[...] + col).astype(F32).astype(BF16)


def bias_body(table_ref, base_ref, row_map_ref, col_map_ref, out_ref, left, right, strip):
    high, low = halves_of(table_ref[...])
    left[...] = jnp.zeros(left.shape, F32)
    right[...] = jnp.zeros(right.shape, F32)
    for col in range(WIN):
        onehot = entry_onehot(base_ref, col)
        line = mm(high, onehot) + mm(low, onehot)
        left[GROUP * col : GROUP * (col + 1), :] = line[:, :128]
        right[GROUP * col : GROUP * (col + 1), :] = line[:, 128:]
    for head in range(GROUP):
        wide = jnp.concatenate(
            [left[pl.ds(head, 16, stride=GROUP), :], right[pl.ds(head, 16, stride=GROUP), :]], axis=1
        )
        for row in range(WIN):
            start = (WIN - 1 - row) * WIN
            strip[16 * row : 16 * (row + 1), TOK * head : TOK * (head + 1)] = wide[:, start : start + TOK]
    high, low = halves_of(strip[...])
    rows = mm(row_map_ref[...], high) + mm(row_map_ref[...], low)
    live = lax.broadcasted_iota(jnp.int32, (TOK, TOK), 1) % QUAD < LIVE
    for head in range(GROUP):
        high, low = halves_of(rows[:, TOK * head : TOK * (head + 1)])
        value = mm(high, col_map_ref[...]) + mm(low, col_map_ref[...])
        out_ref[:, TOK * head : TOK * (head + 1)] = jnp.where(live, value, FAR)


BIAS_SCRATCH = (
    pltpu.VMEM((16 * GROUP, 128), F32),
    pltpu.VMEM((16 * GROUP, 128), F32),
    pltpu.VMEM((160, KEYS), F32),
)


def table_body(sum_ref, base_ref, row_map_ref, col_map_ref, out_ref, row, left, right, strip):
    for head in range(GROUP):
        high, low = halves_of(sum_ref[:, TOK * head : TOK * (head + 1)])
        back = mm_nt(high, col_map_ref[...]) + mm_nt(low, col_map_ref[...])
        high, low = halves_of(back)
        strip[:, TOK * head : TOK * (head + 1)] = mm_tn(row_map_ref[...], high) + mm_tn(row_map_ref[...], low)
    for head in range(GROUP):
        total = jnp.zeros((16, 256), F32)
        for line in range(WIN):
            block = strip[16 * line : 16 * (line + 1), TOK * head : TOK * (head + 1)]
            wide = jnp.concatenate([block, jnp.zeros((16, 128), F32)], axis=1)
            start = (WIN - 1 - line) * WIN
            total = total + (pltpu.roll(wide, start, 1) if start else wide)
        left[pl.ds(head, 16, stride=GROUP), :] = total[:, :128]
        right[pl.ds(head, 16, stride=GROUP), :] = total[:, 128:]
    table = jnp.zeros((GROUP, ENTRIES), F32)
    for col in range(WIN):
        onehot = entry_onehot(base_ref, col)
        lines = slice(GROUP * col, GROUP * (col + 1))
        high, low = halves_of(jnp.concatenate([left[lines, :], right[lines, :]], axis=1))
        table = table + mm_nt(high, onehot) + mm_nt(low, onehot)
    out_ref[row : row + GROUP, :] = table[:, :256]
    out_ref[row + GROUP : row + 2 * GROUP, :] = jnp.concatenate(
        [table[:, 256:], jnp.zeros((GROUP, 128), F32)], axis=1
    )


def pack_kernel(w_qkv_ref, w_proj_ref, order_ref, out_ref):
    mixed = mm(w_qkv_ref[0], order_ref[...]).astype(BF16)
    for part in range(3):
        out_ref[512 * part : 512 * (part + 1), :] = mixed[:, 256 * part : 256 * (part + 1)]
    for part in range(2):
        out_ref[ROWS_QKV + 256 * part : ROWS_QKV + 256 * (part + 1), :] = w_proj_ref[
            0, :, 256 * part : 256 * (part + 1)
        ]


def pack_weights(w_qkv, w_proj, order, layer):
    return run_kernel(
        pack_kernel,
        [w_qkv, w_proj, order],
        [shape_of((ROWS_ATT, 256), BF16)],
        specs={0: layer_spec(w_qkv, layer), 1: layer_spec(w_proj, layer)},
    )[0]


def bias_of(table, base, row_map, col_map):
    return run_kernel(
        bias_body,
        [table, base, row_map, col_map],
        [shape_of((TOK, KEYS), F32)],
        BIAS_SCRATCH,
    )[0]


def project(normed, pack_ref, qv_ref):
    parts = [mm(normed, pack_ref[512 * part : 512 * (part + 1), :]) for part in range(3)]
    return (
        (parts[0] + qv_ref[0:1, :]).astype(BF16),
        parts[1].astype(BF16),
        (parts[2] + qv_ref[1:2, :]).astype(BF16),
    )


def spread_heads(ref, value, heads_ref):
    for head in range(GROUP):
        lines = slice(TOK * head, TOK * (head + 1))
        ref[lines, :] = value * heads_ref[lines, :]


def attend(qkv_ref, base, bias_ref, region, heads_ref, probs_ref, probs_base, stack, wide):
    rows = pl.ds(base, TOK)
    spread_heads(stack, qkv_ref[rows, 256:512], heads_ref)
    logits = mm_nt(qkv_ref[rows, 0:256], stack[...])
    for head in range(GROUP):
        lanes = slice(TOK * head, TOK * (head + 1))
        score = logits[:, lanes] * SCALE + bias_ref[:, lanes]
        if region is not None:
            score = score + region
        grown = jnp.exp(score - jnp.max(score, axis=-1, keepdims=True))
        probs = (grown / jnp.sum(grown, axis=-1, keepdims=True)).astype(BF16)
        wide[:, lanes] = probs
        probs_ref[pl.ds(probs_base + TOK * head, TOK), :] = probs
    spread_heads(stack, qkv_ref[rows, 512:768], heads_ref)
    return mm(wide[...], stack[...]).astype(BF16)


def attend_back(qkv_ref, base, grad, heads_ref, probs_ref, probs_base, total_ref, stack, wide, tall, mixed_ref):
    rows = pl.ds(base, TOK)
    spread_heads(stack, qkv_ref[rows, 512:768], heads_ref)
    grad_probs = mm_nt(grad, stack[...])
    for head in range(GROUP):
        lanes = slice(TOK * head, TOK * (head + 1))
        probs = probs_ref[pl.ds(probs_base + TOK * head, TOK), :].astype(F32)
        part = grad_probs[:, lanes]
        centre = jnp.sum(probs * part, axis=-1, keepdims=True)
        inner = (probs * (part - centre)).astype(BF16)
        wide[:, lanes] = inner
        tall[lanes, :] = inner
        total_ref[:, lanes] = total_ref[:, lanes] + inner.astype(F32)
    spread_heads(stack, grad, heads_ref)
    mixed_ref[rows, 512:768] = mm_tn(probs_ref[pl.ds(probs_base, KEYS), :], stack[...]).astype(BF16)
    spread_heads(stack, qkv_ref[rows, 256:512], heads_ref)
    mixed_ref[rows, 0:256] = (mm(wide[...], stack[...]) * SCALE).astype(BF16)
    spread_heads(stack, qkv_ref[rows, 0:256], heads_ref)
    mixed_ref[rows, 256:512] = (mm_tn(tall[...], stack[...]) * SCALE).astype(BF16)


def project_out(context, pack_ref):
    return jnp.concatenate(
        [mm(context, pack_ref[ROWS_QKV + 256 * part : ROWS_QKV + 256 * (part + 1), :]) for part in range(2)],
        axis=1,
    )


def project_out_back(grad, pack_ref):
    return (
        mm_nt(grad[:, :256], pack_ref[ROWS_QKV : ROWS_QKV + 256, :])
        + mm_nt(grad[:, 256:], pack_ref[ROWS_QKV + 256 : ROWS_ATT, :])
    ).astype(BF16)


def project_back(mixed_ref, pack_ref):
    total = mm_nt(mixed_ref[:, 0:256], pack_ref[0:512, :])
    for part in range(1, 3):
        total = total + mm_nt(mixed_ref[:, 256 * part : 256 * (part + 1)], pack_ref[512 * part : 512 * (part + 1), :])
    return total


ATTEND_SCRATCH = (pltpu.VMEM((KEYS, SPAN), BF16), pltpu.VMEM((TOK, KEYS), BF16))


def attention_plain_kernel(
    side, own, other, gain, bias, pack, qv, offset, heads, whole, normed_out, qkv, probs, context, part_out, stack, wide
):
    here = side[0]
    whole[pl.ds(here * TILE, TILE), :] = own[...]
    whole[pl.ds((1 - here) * TILE, TILE), :] = other[...]
    unit, _ = norm_parts(whole[...].astype(F32))
    normed_out[...] = (unit * gain[...] + bias[...]).astype(BF16)
    for part, value in enumerate(project(normed_out[...], pack, qv)):
        qkv[:, 256 * part : 256 * (part + 1)] = value

    def window(place, carry):
        base = pl.multiple_of(place * TOK, TOK)
        context[pl.ds(base, TOK), :] = attend(
            qkv, base, offset, None, heads, probs, pl.multiple_of(place * KEYS, KEYS), stack, wide
        )
        return carry

    lax.fori_loop(0, PAIR // TOK, window, 0)
    part_out[...] = project_out(context[...], pack).astype(BF16)


def attention_shifted_kernel(
    keep, gain, bias, gain2, bias2, pack_a, pack_b, qv_a, qv_b, off_a, off_b, ids_q, ids_k, heads, b_proj,
    normed_out, qkv_a, qkv_b, probs_a, probs_b, context_a, context_b, middle_out, second_out, stack, wide,
):
    unit, _ = norm_parts(keep[...].astype(F32))
    normed_out[...] = (unit * gain[...] + bias[...]).astype(BF16)
    total = keep[...].astype(F32) + b_proj[...]
    for pack, qv, off, qkv, probs, context in (
        (pack_a, qv_a, off_a, qkv_a, probs_a, context_a),
        (pack_b, qv_b, off_b, qkv_b, probs_b, context_b),
    ):
        for part, value in enumerate(project(normed_out[...], pack, qv)):
            qkv[:, 256 * part : 256 * (part + 1)] = value

        def window(place, carry):
            base = pl.multiple_of(place * TOK, TOK)
            region = jnp.where(ids_q[pl.ds(base, TOK), :] != ids_k[place], -100.0, 0.0)
            context[pl.ds(base, TOK), :] = attend(
                qkv, base, off, region, heads, probs, pl.multiple_of(place * KEYS, KEYS), stack, wide
            )
            return carry

        lax.fori_loop(0, TILE // TOK, window, 0)
        total = total + project_out(context[...], pack)
    middle_out[...] = total
    unit, _ = norm_parts(total)
    second_out[...] = (unit * gain2[...] + bias2[...]).astype(BF16)


def gelu_parts(hidden):
    chance = 0.5 * (1.0 + lax.erf(hidden * ROOT_HALF))
    slope = chance + hidden * (jnp.exp(-0.5 * hidden * hidden) * ROOT_TWO_PI)
    return (hidden * chance).astype(BF16), slope.astype(BF16)


CHUNK = 256


def mlp_plain_kernel(
    side, whole, part_own, part_other, b_proj, gain, bias, w_fc1, b_fc1, w_fc2, b_fc2,
    middle, second, active, slope, keep, send, spun,
):
    here = side[0]
    middle[...] = (
        whole[...].astype(F32) + (part_own[...].astype(F32) + part_other[...].astype(F32)) + b_proj[...]
    )
    unit, _ = norm_parts(middle[...])
    second[...] = (unit * gain[...] + bias[...]).astype(BF16)
    for place in range(1024 // CHUNK):
        lanes = slice(CHUNK * place, CHUNK * (place + 1))
        hidden = mm(second[...], w_fc1[0, :, lanes]) + b_fc1[:, lanes]
        active[:, lanes], slope[:, lanes] = gelu_parts(hidden)
    out = mm(active[...], w_fc2[0])
    spun[0 : PAIR - UNIT, :] = out[UNIT:, :]
    spun[PAIR - UNIT :, :] = out[:UNIT, :]
    send[...] = spun[pl.ds((1 - here) * TILE, TILE), :].astype(BF16)
    spun[0 : PAIR - UNIT, :] = spun[0 : PAIR - UNIT, :] + middle[UNIT:, :]
    spun[PAIR - UNIT :, :] = spun[PAIR - UNIT :, :] + middle[:UNIT, :]
    keep[...] = spun[pl.ds(here * TILE, TILE), :] + b_fc2[...]


def mlp_shifted_kernel(
    side, own, other, grad, w_fc1, b_fc1, w_fc2,
    second, active, inner, keep, send, back_keep, back_send, small, slope,
):
    here = side[0]
    mine = pl.ds(here * TILE, TILE)
    theirs = pl.ds((1 - here) * TILE, TILE)
    second[mine, :] = own[...]
    second[theirs, :] = other[...]
    for place in range(1024 // CHUNK):
        lanes = slice(CHUNK * place, CHUNK * (place + 1))
        hidden = mm(second[...], w_fc1[0, :, lanes]) + b_fc1[:, lanes]
        active[:, lanes], slope[:, lanes] = gelu_parts(hidden)
    for place in range(1024 // CHUNK):
        lanes = slice(CHUNK * place, CHUNK * (place + 1))
        back = mm_nt(grad[...], w_fc2[0, lanes, :]) * slope[:, lanes].astype(F32)
        inner[:, lanes] = back.astype(BF16)
    back_keep[...] = mm_nt(inner[mine, :], w_fc1[0])
    back_send[...] = mm_nt(inner[theirs, :], w_fc1[0]).astype(BF16)
    keep[...] = mm(active[mine, :], w_fc2[0])
    send[...] = mm(active[theirs, :], w_fc2[0]).astype(BF16)
    put_row(small, 0, column_sum(inner[...].astype(F32)))
    small[4:, :] = jnp.zeros((4, 256), F32)


def mlp_plain_back_kernel(spun, slope, w_fc1, w_fc2, grad, inner, back):
    grad[0:UNIT, :] = spun[PAIR - UNIT :, :]
    grad[UNIT:, :] = spun[0 : PAIR - UNIT, :]
    for place in range(1024 // CHUNK):
        lanes = slice(CHUNK * place, CHUNK * (place + 1))
        value = mm_nt(grad[...], w_fc2[0, lanes, :]) * slope[:, lanes].astype(F32)
        inner[:, lanes] = value.astype(BF16)
    back[...] = mm_nt(inner[...], w_fc1[0]).astype(BF16)


def mlp_weights_kernel(second, active, grad, inner, out):
    for place in range(4):
        lanes = slice(256 * place, 256 * (place + 1))
        out[512 * place : 512 * (place + 1), :] = mm_tn(second[...], inner[:, lanes]).astype(BF16)
    for place in range(2):
        lanes = slice(256 * place, 256 * (place + 1))
        start = 2048 + 1024 * place
        out[start : start + 1024, :] = mm_tn(active[...], grad[:, lanes]).astype(BF16)


def mlp_weights(second, active, grad, inner):
    return run_kernel(
        mlp_weights_kernel, [second, active, grad, inner], [shape_of((ROWS_MLP, 256), BF16)]
    )[0]


def attention_shifted_back_kernel(
    side, grad_all, back_own, back_other, middle, entry, gain, gain2, qkv_a, qkv_b, probs_a, probs_b,
    pack_a, pack_b, heads,
    grad_low, mixed_a, mixed_b, total_a, total_b, below, small, stack, wide, tall, grad_context,
):
    here = side[0]
    upstream = grad_all[pl.ds(here * TILE, TILE), :].astype(F32)
    back = back_own[...] + back_other[...].astype(F32)
    unit, inverse = norm_parts(middle[...])
    put_row(small, 0, column_sum(back * unit))
    put_row(small, 2, column_sum(back))
    put_row(small, 4, column_sum(upstream))
    grad_middle = upstream + norm_back(back, gain2[...], unit, inverse)
    grad_low[...] = grad_middle.astype(BF16)
    put_row(small, 6, column_sum(grad_low[...].astype(F32)))
    first = jnp.zeros((TILE, WIDTH), F32)
    for pack, qkv, probs, mixed, total in (
        (pack_a, qkv_a, probs_a, mixed_a, total_a),
        (pack_b, qkv_b, probs_b, mixed_b, total_b),
    ):
        grad_context[...] = project_out_back(grad_low[...], pack)
        total[...] = jnp.zeros((TOK, KEYS), F32)

        def window(place, carry):
            base = pl.multiple_of(place * TOK, TOK)
            attend_back(
                qkv, base, grad_context[pl.ds(base, TOK), :], heads, probs, pl.multiple_of(place * KEYS, KEYS),
                total, stack, wide, tall, mixed,
            )
            return carry

        lax.fori_loop(0, TILE // TOK, window, 0)
        first = first + project_back(mixed, pack)
    unit, inverse = norm_parts(entry[...].astype(F32))
    put_row(small, 8, column_sum(first * unit))
    put_row(small, 10, column_sum(first))
    put_row(small, 12, column_sum(mixed_a[...].astype(F32)))
    small[15:16, :] = jnp.zeros((1, 256), F32)
    put_row(small, 16, column_sum(mixed_b[...].astype(F32)))
    small[19:24, :] = jnp.zeros((5, 256), F32)
    below[...] = (grad_middle + norm_back(first, gain[...], unit, inverse)).astype(BF16)


def attention_plain_back_kernel(
    side, grad, back_own, back_other, middle, whole, gain, gain2, qkv, probs, pack, heads, inner,
    grad_low, mixed, total, first_keep, first_send, kept, small, stack, wide, tall, grad_context, first,
):
    here = side[0]
    mine = pl.ds(here * TILE, TILE)
    theirs = pl.ds((1 - here) * TILE, TILE)
    back = back_own[...].astype(F32) + back_other[...].astype(F32)
    unit, inverse = norm_parts(middle[...])
    share = back_own[...].astype(F32)
    put_row(small, 0, column_sum(share * unit))
    put_row(small, 2, column_sum(share))
    put_row(small, 4, column_sum(grad[mine, :].astype(F32)))
    first[...] = grad[...].astype(F32) + norm_back(back, gain2[...], unit, inverse)
    kept[...] = first[mine, :]
    grad_low[...] = first[...].astype(BF16)
    put_row(small, 6, column_sum(grad_low[mine, :].astype(F32)))
    grad_context[...] = project_out_back(grad_low[...], pack)
    total[...] = jnp.zeros((TOK, KEYS), F32)

    def window(place, carry):
        base = pl.multiple_of(place * TOK, TOK)
        attend_back(
            qkv, base, grad_context[pl.ds(base, TOK), :], heads, probs, pl.multiple_of(place * KEYS, KEYS),
            total, stack, wide, tall, mixed,
        )
        return carry

    lax.fori_loop(0, PAIR // TOK, window, 0)
    first[...] = project_back(mixed, pack)
    first_keep[...] = first[mine, :]
    first_send[...] = first[theirs, :].astype(BF16)
    unit, _ = norm_parts(whole[...].astype(F32))
    put_row(small, 8, column_sum(first[...] * unit))
    put_row(small, 10, column_sum(first[...]))
    put_row(small, 12, column_sum(mixed[...].astype(F32)))
    small[15:16, :] = jnp.zeros((1, 256), F32)
    put_row(small, 16, column_sum(inner[...].astype(F32)))
    small[20:24, :] = jnp.zeros((4, 256), F32)


def attention_weights_body(normed, mixed, context, grad_low, order, out, start):
    turned = [mm_tn(normed[...], mixed[:, 256 * part : 256 * (part + 1)]).astype(BF16) for part in range(3)]
    canon = mm_nt(jnp.concatenate(turned, axis=1), order[...]).astype(BF16)
    for part in range(3):
        out[start + 512 * part : start + 512 * (part + 1), :] = canon[:, 256 * part : 256 * (part + 1)]
    for part in range(2):
        lines = slice(start + ROWS_QKV + 256 * part, start + ROWS_QKV + 256 * (part + 1))
        out[lines, :] = mm_tn(context[...], grad_low[:, 256 * part : 256 * (part + 1)]).astype(BF16)


def attention_weights_plain_kernel(normed, mixed, context, grad_low, order, out):
    attention_weights_body(normed, mixed, context, grad_low, order, out, 0)


def table_kernel(total, base, row_map, col_map, out, left, right, strip):
    table_body(total, base, row_map, col_map, out, 0, left, right, strip)


def table_of(total, base, row_map, col_map):
    return run_kernel(
        table_kernel, [total, base, row_map, col_map], [shape_of((2 * GROUP, 256), F32)], BIAS_SCRATCH
    )[0]


def attention_weights(normed, mixed, context, grad_low, order):
    return run_kernel(
        attention_weights_plain_kernel,
        [normed, mixed, context, grad_low, order],
        [shape_of((ROWS_ATT, 256), BF16)],
    )[0]


def last_kernel(side, whole, gain, keep, other, kept, out, buf):
    here = side[0]
    unit, inverse = norm_parts(whole[pl.ds(here * TILE, TILE), :].astype(F32))
    buf[...] = kept[...] + norm_back(keep[...] + other[...].astype(F32), gain[...], unit, inverse)
    leave_rows(buf, out)


def steps_of(place_band, place_col):
    def pairs(first, second):
        return [
            (band * 2 + col, (band ^ (first if col == 0 else second)) * 2 + col) for band in range(8) for col in range(2)
        ]

    digit = [(place_band >> power) & 1 for power in range(3)]
    return [
        ([(band * 2 + col, band * 2 + 1 - col) for band in range(8) for col in range(2)], place_col),
        (pairs(1, 2), jnp.where(place_col == 0, digit[0], digit[1])),
        (pairs(2, 4), jnp.where(place_col == 0, digit[1], digit[2])),
        (pairs(4, 1), jnp.where(place_col == 0, digit[2], digit[0])),
    ]


def sum_page(value, steps):
    for pairs, bit in steps:
        half = value.shape[0] // 2
        kept = lax.dynamic_slice_in_dim(value, bit * half, half, 0)
        sent = lax.dynamic_slice_in_dim(value, (1 - bit) * half, half, 0)
        come = lax.ppermute(sent, ("band", "col"), pairs)
        value = (kept.astype(F32) + come.astype(F32)).astype(BF16)
    for pairs, bit in steps[::-1]:
        come = lax.ppermute(value, ("band", "col"), pairs)
        half = value.shape[0]
        whole = jnp.zeros((2 * half, value.shape[1]), BF16)
        whole = lax.dynamic_update_slice_in_dim(whole, value, bit * half, 0)
        value = lax.dynamic_update_slice_in_dim(whole, come, (1 - bit) * half, 0)
    return value


def unpack_body(att, mlp, qkv, proj, fc1, fc2):
    for part in range(3):
        qkv[0, :, 256 * part : 256 * (part + 1)] = att[512 * part : 512 * (part + 1), :].astype(F32)
    for part in range(2):
        lanes = slice(256 * part, 256 * (part + 1))
        start = ROWS_QKV + 256 * part
        proj[0, :, lanes] = att[start : start + 256, :].astype(F32)
        start = 2048 + 1024 * part
        fc2[0, :, lanes] = mlp[start : start + 1024, :].astype(F32)
    for part in range(4):
        fc1[0, :, 256 * part : 256 * (part + 1)] = mlp[512 * part : 512 * (part + 1), :].astype(F32)


def unpack_first_kernel(att, mlp, qkv, proj, fc1, fc2):
    unpack_body(att, mlp, qkv, proj, fc1, fc2)


def unpack_last_kernel(att, mlp, qkv_in, proj_in, fc1_in, fc2_in, qkv, proj, fc1, fc2):
    unpack_body(att, mlp, qkv, proj, fc1, fc2)


def unpack(att, mlp, layer, before=None):
    shapes = [(2, 512, 768), (2, 256, 512), (2, 512, 1024), (2, 1024, 512)]
    outs = [shape_of(shape, F32) for shape in shapes]
    out_specs = [layer_spec(out, layer) for out in outs]
    if before is None:
        return run_kernel(unpack_first_kernel, [att, mlp], outs, out_specs=out_specs)
    return run_kernel(
        unpack_last_kernel,
        [att, mlp, *before],
        outs,
        specs={place: pl.BlockSpec(memory_space=pl.ANY) for place in range(2, 6)},
        out_specs=out_specs,
        aliases={2: 0, 3: 1, 4: 2, 5: 3},
    )


def swap_head(value):
    return lax.ppermute(value, "head", [(0, 1), (1, 0)])


def fast_device(
    act_in, ln_gain, ln_bias, w_qkv, b_qv, rel_table, w_proj, b_proj, w_fc1, b_fc1, w_fc2, b_fc2, grad_out
):
    row_map, col_map, base, order, heads, token_row, token_col = constants()
    band = lax.axis_index("band")
    col = lax.axis_index("col")
    head = lax.axis_index("head")
    bands = lax.axis_size("band")
    cols = lax.axis_size("col")
    side = head.reshape(1).astype(jnp.int32)
    band_up = [(place, (place - 1) % bands) for place in range(bands)]
    band_down = [(place, (place + 1) % bands) for place in range(bands)]
    col_left = [(place, (place - 1) % cols) for place in range(cols)]
    edge_left = [(place * 2 + 1, (place - 1) % cols * 2 + 1) for place in range(cols)]
    edge_right = [(place * 2 + 1, (place + 1) % cols * 2 + 1) for place in range(cols)]
    gain = [[ln_gain[layer, place][None] for place in range(2)] for layer in range(2)]
    bias = [[ln_bias[layer, place][None] for place in range(2)] for layer in range(2)]
    row_proj = [b_proj[layer][None] for layer in range(2)]
    row_fc1 = [b_fc1[layer][None] for layer in range(2)]
    row_fc2 = [b_fc2[layer][None] for layer in range(2)]
    qv = b_qv.reshape(2, GROUP, 2, HEAD_DIM).transpose(0, 2, 1, 3).reshape(2, 2, SPAN)
    tables = jnp.pad(rel_table, ((0, 0), (0, ENTRIES - rel_table.shape[1]), (0, 0))).transpose(0, 2, 1)

    def lines(value, places):
        return jnp.concatenate([value[place] for place in places], axis=0)

    def at_edge(value, pairs):
        come = lax.ppermute(value[3 * UNIT :], ("col", "head"), pairs)
        return jnp.concatenate([value[: 3 * UNIT], jnp.where(head == 1, come, value[3 * UNIT :])], axis=0)

    def quads(value):
        return value.reshape(-1, 2, QUAD, WIDTH)

    def flat(value):
        return value.reshape(-1, WIDTH)

    def go_ahead(value):
        grid = quads(value)
        come = lax.ppermute(grid[:, 0], "band", band_up)
        return flat(jnp.stack([grid[:, 1], come], axis=1))

    def go_back(value):
        grid = quads(value)
        come = lax.ppermute(grid[:, 1], "band", band_down)
        return flat(jnp.stack([come, grid[:, 0]], axis=1))

    x_own = enter_units(act_in)
    x_other = swap_head(x_own)
    pack0 = pack_weights(w_qkv, w_proj, order, 0)
    off0 = bias_of(tables[0], base, row_map, col_map)
    whole, normed0, qkv0, probs0, context0, part0 = run_kernel(
        attention_plain_kernel,
        [side, x_own, x_other, gain[0][0], bias[0][0], pack0, qv[0], off0, heads],
        [
            shape_of((PAIR, WIDTH), BF16),
            shape_of((PAIR, WIDTH), BF16),
            shape_of((PAIR, 768), BF16),
            shape_of((4 * KEYS, TOK), BF16),
            shape_of((PAIR, SPAN), BF16),
            shape_of((PAIR, WIDTH), BF16),
        ],
        ATTEND_SCRATCH,
        specs={0: SMEM},
    )
    part0_other = swap_head(part0)
    middle0, second0, active0, slope0, x1_keep, x1_send = run_kernel(
        mlp_plain_kernel,
        [
            side, whole, part0, part0_other, row_proj[0], gain[0][1], bias[0][1], w_fc1, row_fc1[0], w_fc2,
            row_fc2[0],
        ],
        [
            shape_of((PAIR, WIDTH), F32),
            shape_of((PAIR, WIDTH), BF16),
            shape_of((PAIR, 1024), BF16),
            shape_of((PAIR, 1024), BF16),
            shape_of((TILE, WIDTH), F32),
            shape_of((TILE, WIDTH), BF16),
        ],
        [pltpu.VMEM((PAIR, WIDTH), F32)],
        specs={0: SMEM, 7: layer_spec(w_fc1, 0), 9: layer_spec(w_fc2, 0)},
    )
    x1 = (x1_keep + swap_head(x1_send).astype(F32)).astype(BF16)
    x1 = go_ahead(at_edge(x1, edge_left))

    pack1 = pack_weights(w_qkv, w_proj, order, 1)
    half = ROWS_ATT // 2
    mine = swap_head(lax.dynamic_slice_in_dim(pack1, col * half, half, 0))
    theirs = lax.ppermute(mine, "col", [(0, 1), (1, 0)])
    pack1_other = jnp.where(
        col == 0, jnp.concatenate([mine, theirs], axis=0), jnp.concatenate([theirs, mine], axis=0)
    )
    small1 = jnp.concatenate([tables[1], jnp.pad(qv[1], ((0, 6), (0, ENTRIES - SPAN)))], axis=0)
    small1_other = swap_head(small1)
    off1 = bias_of(tables[1], base, row_map, col_map)
    off1_other = bias_of(small1_other[:GROUP], base, row_map, col_map)
    qv1_other = small1_other[GROUP : GROUP + 2, :SPAN]

    grad_own = enter_units(grad_out)
    grad_other = swap_head(grad_own)
    grad_all = jnp.where(
        head == 0,
        jnp.concatenate([grad_own, grad_other], axis=0),
        jnp.concatenate([grad_other, grad_own], axis=0),
    )
    grad_all = jnp.concatenate([grad_all[UNIT:], lax.ppermute(grad_all[:UNIT], "col", col_left)], axis=0)
    grad_all = go_ahead(grad_all)

    rows_id = region_ids(WIN * band + jnp.asarray(token_row), WIN * bands)
    cols_id = region_ids(
        2 * WIN * (2 * col + head) + WIN * jnp.arange(2, dtype=jnp.int32)[:, None] + jnp.asarray(token_col)[None],
        4 * WIN * cols,
    )
    ids = (3 * rows_id[None] + cols_id).astype(F32)
    normed1, qkv1a, qkv1b, probs1a, probs1b, context1a, context1b, middle1, second1_own = run_kernel(
        attention_shifted_kernel,
        [
            x1, gain[1][0], bias[1][0], gain[1][1], bias[1][1], pack1, pack1_other, qv[1], qv1_other, off1,
            off1_other, ids.reshape(TILE, 1), ids.reshape(2, 1, TOK), heads, row_proj[1],
        ],
        [
            shape_of((TILE, WIDTH), BF16),
            shape_of((TILE, 768), BF16),
            shape_of((TILE, 768), BF16),
            shape_of((2 * KEYS, TOK), BF16),
            shape_of((2 * KEYS, TOK), BF16),
            shape_of((TILE, SPAN), BF16),
            shape_of((TILE, SPAN), BF16),
            shape_of((TILE, WIDTH), F32),
            shape_of((TILE, WIDTH), BF16),
        ],
        ATTEND_SCRATCH,
    )
    second1_other = swap_head(second1_own)
    second1, active1, inner1, x2_keep, x2_send, back1_keep, back1_send, small_mlp1 = run_kernel(
        mlp_shifted_kernel,
        [side, second1_own, second1_other, grad_all, w_fc1, row_fc1[1], w_fc2],
        [
            shape_of((PAIR, WIDTH), BF16),
            shape_of((PAIR, 1024), BF16),
            shape_of((PAIR, 1024), BF16),
            shape_of((TILE, WIDTH), F32),
            shape_of((TILE, WIDTH), BF16),
            shape_of((TILE, WIDTH), F32),
            shape_of((TILE, WIDTH), BF16),
            shape_of((8, 256), F32),
        ],
        [pltpu.VMEM((PAIR, 1024), BF16)],
        specs={0: SMEM, 4: layer_spec(w_fc1, 1), 6: layer_spec(w_fc2, 1)},
    )
    back1_other = swap_head(back1_send)
    weights_mlp1 = mlp_weights(second1, active1, grad_all, inner1)
    grad_low1, mixed1a, mixed1b, total1a, total1b, below, small_att1 = run_kernel(
        attention_shifted_back_kernel,
        [
            side, grad_all, back1_keep, back1_other, middle1, x1, gain[1][0], gain[1][1], qkv1a, qkv1b, probs1a,
            probs1b, pack1, pack1_other, heads,
        ],
        [
            shape_of((TILE, WIDTH), BF16),
            shape_of((TILE, 768), BF16),
            shape_of((TILE, 768), BF16),
            shape_of((TOK, KEYS), F32),
            shape_of((TOK, KEYS), F32),
            shape_of((TILE, WIDTH), BF16),
            shape_of((24, 256), F32),
        ],
        ATTEND_SCRATCH + (pltpu.VMEM((KEYS, TOK), BF16), pltpu.VMEM((TILE, SPAN), BF16)),
        specs={0: SMEM},
    )

    spun = at_edge(go_back(below), edge_right)
    spun_other = swap_head(spun)
    spun_all = jnp.where(
        head == 0, jnp.concatenate([spun, spun_other], axis=0), jnp.concatenate([spun_other, spun], axis=0)
    )
    grad0, inner0, back0 = run_kernel(
        mlp_plain_back_kernel,
        [spun_all, slope0, w_fc1, w_fc2],
        [shape_of((PAIR, WIDTH), BF16), shape_of((PAIR, 1024), BF16), shape_of((PAIR, WIDTH), BF16)],
        specs={2: layer_spec(w_fc1, 0), 3: layer_spec(w_fc2, 0)},
    )
    back0_other = swap_head(back0)
    weights_mlp0 = mlp_weights(second0, active0, grad0, inner0)
    grad_low0, mixed0, total0, first_keep, first_send, kept0, small_att0 = run_kernel(
        attention_plain_back_kernel,
        [
            side, grad0, back0, back0_other, middle0, whole, gain[0][0], gain[0][1], qkv0, probs0, pack0, heads,
            inner0,
        ],
        [
            shape_of((PAIR, WIDTH), BF16),
            shape_of((PAIR, 768), BF16),
            shape_of((TOK, KEYS), F32),
            shape_of((TILE, WIDTH), F32),
            shape_of((TILE, WIDTH), BF16),
            shape_of((TILE, WIDTH), F32),
            shape_of((24, 256), F32),
        ],
        ATTEND_SCRATCH
        + (
            pltpu.VMEM((KEYS, TOK), BF16),
            pltpu.VMEM((PAIR, SPAN), BF16),
            pltpu.VMEM((PAIR, WIDTH), F32),
        ),
        specs={0: SMEM},
    )
    first_other = swap_head(first_send)
    grad_in = run_kernel(
        last_kernel,
        [side, whole, gain[0][0], first_keep, first_other, kept0],
        [shape_of((WIN, 2 * WIN, WIDTH), F32)],
        [pltpu.VMEM((TILE, WIDTH), F32)],
        specs={0: SMEM},
    )[0]

    weights_att1 = attention_weights(normed1, mixed1a, context1a, grad_low1, order)
    weights_att1_send = attention_weights(normed1, mixed1b, context1b, grad_low1, order)
    weights_att1 = weights_att1.astype(F32) + swap_head(weights_att1_send).astype(F32)
    table1 = table_of(total1a, base, row_map, col_map)
    table1_send = table_of(total1b, base, row_map, col_map)
    weights_att0 = attention_weights(normed0, mixed0, context0, grad_low0, order)
    table0 = table_of(total0, base, row_map, col_map)
    shared = jnp.concatenate([small_att0[:12], small_att1[:12]], axis=0)
    come = swap_head(jnp.concatenate([shared, small_att1[16:24], table1_send], axis=0))
    shared = shared + come[:24]
    smalls = jnp.concatenate(
        [
            shared,
            small_att1[12:16] + come[24:28],
            small_att0[12:20],
            small_mlp1[:4],
            table0,
            table1 + come[32:48],
        ],
        axis=0,
    )
    smalls = jnp.pad(smalls.astype(BF16), ((0, 256 - smalls.shape[0]), (0, 0)))
    steps = steps_of(band, col)
    sum1 = sum_page(jnp.concatenate([weights_mlp1, weights_att1.astype(BF16)], axis=0), steps)
    sum0_mlp = sum_page(weights_mlp0, steps)
    sum0_att = sum_page(jnp.concatenate([weights_att0, smalls], axis=0), steps)
    before = unpack(sum1[ROWS_MLP:], sum1[:ROWS_MLP], 1)
    g_qkv, g_proj, g_fc1, g_fc2 = unpack(sum0_att[:ROWS_ATT], sum0_mlp, 0, before)
    sums = sum0_att[ROWS_ATT:].astype(F32)

    def row_at(place, count):
        return sums[place : place + count].reshape(-1)

    g_gain = jnp.stack([row_at(8, 2), row_at(0, 2), row_at(20, 2), row_at(12, 2)]).reshape(2, 2, WIDTH)
    g_bias = jnp.stack([row_at(10, 2), row_at(2, 2), row_at(22, 2), row_at(14, 2)]).reshape(2, 2, WIDTH)
    g_bfc2 = jnp.stack([row_at(4, 2), row_at(16, 2)])
    g_bproj = jnp.stack([row_at(6, 2), row_at(18, 2)])
    g_qv = jnp.stack([sums[28:31], sums[24:27]])[:, ::2].reshape(2, 2, GROUP, HEAD_DIM)
    g_qv = g_qv.transpose(0, 2, 1, 3).reshape(2, 2 * SPAN)
    g_bfc1 = jnp.stack([row_at(32, 4), row_at(36, 4)])

    def table_rows(place):
        full = jnp.concatenate([sums[place : place + GROUP], sums[place + GROUP : place + 2 * GROUP]], axis=1)
        return full[:, : rel_table.shape[1]].T

    g_table = jnp.stack([table_rows(40), table_rows(56)])

    x2 = (x2_keep + swap_head(x2_send).astype(F32) + middle1 + row_fc2[1]).astype(BF16)
    x2 = at_edge(go_back(x2), edge_right)
    x2 = jnp.concatenate([swap_head(x2[3 * UNIT :]), x2[: 3 * UNIT]], axis=0)
    x2 = jnp.where(head == 0, x2, jnp.concatenate([x2[:UNIT], x2[UNIT:]], axis=0))
    act_out = leave_units(x2)
    return (
        act_out, grad_in, g_gain, g_bias, g_qkv, g_qv, g_table, g_proj, g_bproj, g_fc1, g_bfc1, g_fc2, g_bfc2,
    )


def fits(mesh):
    return dict(mesh.shape) == {"band": 8, "col": 2, "head": 2}


def solution(mesh):
    placed = (
        P("band", ("col", "head"), None),
        P(),
        P(),
        P(None, None, "head"),
        P(None, "head"),
        P(None, None, "head"),
        P(None, "head", None),
        P(),
        P(None, None, "head"),
        P(None, "head"),
        P(None, "head", None),
        P(),
        P("band", ("col", "head"), None),
    )
    return jax.shard_map(
        fast_device if fits(mesh) else on_device,
        mesh=mesh,
        in_specs=placed,
        out_specs=(
            P("band", ("col", "head"), None),
            P("band", ("col", "head"), None),
            P(),
            P(),
            P(None, None, "head"),
            P(None, "head"),
            P(None, None, "head"),
            P(None, "head", None),
            P(),
            P(None, None, "head"),
            P(None, "head"),
            P(None, "head", None),
            P(),
        ),
        check_vma=False,
    )
```

```python
from functools import partial

import jax
import jax.numpy as jnp
import numpy as np
from jax import lax
from jax.experimental import pallas as pl
from jax.experimental.pallas import tpu as pltpu
from jax.sharding import PartitionSpec as P

HEAD_DIM = 32
WIN = 10
SHIFT = 5
BLOCKS = 2


EPSILON = 1e-05
HIGHEST = lax.Precision.HIGHEST


def shifted_2(value, axis, steps):
    count = lax.axis_size(axis)
    pairs = [(source, (source + steps) % count) for source in range(count)]
    return lax.ppermute(value, axis, pairs)


def layer_norm(array, gain_row, bias_row):
    centre = array - jnp.mean(array, axis=-1, keepdims=True)
    spread = jnp.mean(centre * centre, axis=-1, keepdims=True)
    return centre * lax.rsqrt(spread + EPSILON) * gain_row + bias_row


def offsets(window):
    places = jnp.arange(window, dtype=jnp.int32)
    spread = jnp.arange(2 * window - 1, dtype=jnp.int32)
    return (
        spread[None, None, :] == places[:, None, None] - places[None, :, None] + window - 1
    ).astype(jnp.float32)


def position_bias(table):
    head_count = table.shape[-1]
    table_grid = table.reshape(2 * WIN - 1, 2 * WIN - 1, head_count)
    onehot = offsets(WIN)
    full = jnp.einsum("ika,jlb,abh->hijkl", onehot, onehot, table_grid, precision=HIGHEST)
    return full.reshape(head_count, WIN * WIN, WIN * WIN)


def table_grad(grad_offset):
    head_count = grad_offset.shape[0]
    onehot = offsets(WIN)
    spread = grad_offset.reshape(head_count, WIN, WIN, WIN, WIN)
    full = jnp.einsum("ika,jlb,hijkl->abh", onehot, onehot, spread, precision=HIGHEST)
    return full.reshape((2 * WIN - 1) * (2 * WIN - 1), head_count)


def gather_tile(array):
    return lax.all_gather(array, "head", axis=1, tiled=True)


def sum_tile(array):
    return lax.psum_scatter(
        array.astype(jnp.bfloat16), "head", scatter_dimension=1, tiled=True
    ).astype(jnp.float32)


def gather_grad(array):
    return lax.all_gather(array, "head", axis=1, tiled=True)


def sum_grad(array):
    return lax.psum_scatter(
        array.astype(jnp.bfloat16), "head", scatter_dimension=1, tiled=True
    ).astype(jnp.float32)


def roll_ahead(array):
    upper = shifted_2(array[:SHIFT], "band", -1)
    array = jnp.concatenate([array[SHIFT:], upper], axis=0)
    leftmost = shifted_2(array[:, :SHIFT], ("col", "head"), -1)
    return jnp.concatenate([array[:, SHIFT:], leftmost], axis=1)


def roll_behind(array):
    lower = shifted_2(array[-SHIFT:], "band", 1)
    array = jnp.concatenate([lower, array[:-SHIFT]], axis=0)
    rightmost = shifted_2(array[:, -SHIFT:], ("col", "head"), 1)
    return jnp.concatenate([rightmost, array[:, :-SHIFT]], axis=1)


def pack_members(members):
    group = lax.axis_size("band") * lax.axis_size("col")
    flat = jnp.concatenate([member.reshape(-1) for member in members])
    padding = -flat.shape[0] % group
    return jnp.concatenate([flat, jnp.zeros((padding,), jnp.float32)])


def unpack_members(flat, members):
    result = []
    start = 0
    for member in members:
        count = member.size
        result.append(flat[start : start + count].reshape(member.shape))
        start = start + count
    return tuple(result)


def to_windows(tile_rows):
    height, breadth, depth = tile_rows.shape
    window_count = breadth // height
    split = tile_rows.reshape(height, window_count, height, depth).transpose(1, 0, 2, 3)
    return split.reshape(window_count * height * height, depth)


def from_windows(flat_rows, height):
    window_count = flat_rows.shape[0] // (height * height)
    depth = flat_rows.shape[1]
    split = flat_rows.reshape(window_count, height, height, depth).transpose(1, 0, 2, 3)
    return split.reshape(height, window_count * height, depth)


def region_ids(places, extent):
    return (places >= extent - WIN).astype(jnp.int32) + (places >= extent - SHIFT).astype(jnp.int32)


def shift_mask(breadth):
    rows_all = WIN * lax.axis_size("band")
    cols_all = breadth * lax.axis_size("col")
    rows_here = WIN * lax.axis_index("band") + jnp.arange(WIN, dtype=jnp.int32)
    cols_here = breadth * lax.axis_index("col") + jnp.arange(breadth, dtype=jnp.int32)
    region = 3 * region_ids(rows_here, rows_all)[:, None] + region_ids(cols_here, cols_all)[None, :]
    window_count = breadth // WIN
    labels = to_windows(region[:, :, None])[:, 0].reshape(window_count, WIN * WIN)
    return jnp.where(labels[:, :, None] != labels[:, None, :], -100.0, 0.0).astype(jnp.float32)


def scores(queries, key_rows, offset, region_mask):
    logits = jnp.einsum("wqhd,wkhd->whqk", queries, key_rows, preferred_element_type=jnp.float32)
    logits = logits * HEAD_DIM ** (-0.5) + offset[None]
    if region_mask is not None:
        logits = logits + region_mask[:, None]
    return logits


def forward_block(source, weights, shifted):
    norm_gain, norm_bias, w_qkv, b_qv, table, w_proj, b_proj, w_fc1, b_fc1, w_fc2, b_fc2 = weights
    height = source.shape[0]
    heads_here = table.shape[-1]
    normed = layer_norm(source, norm_gain[0], norm_bias[0]).astype(jnp.bfloat16)
    if shifted:
        normed = roll_ahead(normed)
    gathered = gather_tile(normed)
    window_count = gathered.shape[1] // height
    flat_rows = to_windows(gathered)
    projected = jnp.dot(flat_rows, w_qkv, preferred_element_type=jnp.float32)
    projected = projected.reshape(window_count, height * height, heads_here, 3, HEAD_DIM)
    qv_bias = b_qv.reshape(heads_here, 2, HEAD_DIM)
    queries = (projected[..., 0, :] + qv_bias[:, 0]).astype(jnp.bfloat16)
    key_rows = projected[..., 1, :].astype(jnp.bfloat16)
    values = (projected[..., 2, :] + qv_bias[:, 1]).astype(jnp.bfloat16)
    offset = position_bias(table)
    region_mask = shift_mask(gathered.shape[1]) if shifted else None
    logits = scores(queries, key_rows, offset, region_mask)
    log_total = jax.nn.logsumexp(logits, axis=-1)
    probs_low = jnp.exp(logits - log_total[..., None]).astype(jnp.bfloat16)
    context = jnp.einsum("whqk,wkhd->wqhd", probs_low, values, preferred_element_type=jnp.float32)
    context = context.astype(jnp.bfloat16).reshape(
        window_count * height * height, heads_here * HEAD_DIM
    )
    partial_out = from_windows(jnp.dot(context, w_proj, preferred_element_type=jnp.float32), height)
    branch = sum_tile(partial_out) + b_proj
    if shifted:
        branch = roll_behind(branch.astype(jnp.bfloat16)).astype(jnp.float32)
    middle = source + branch
    second = layer_norm(middle, norm_gain[1], norm_bias[1]).astype(jnp.bfloat16)
    second_tile = gather_tile(second)
    mlp_rows = second_tile.reshape(-1, second_tile.shape[-1])
    hidden = jnp.dot(mlp_rows, w_fc1, preferred_element_type=jnp.float32) + b_fc1
    active = jax.nn.gelu(hidden, approximate=False).astype(jnp.bfloat16)
    out_part = jnp.dot(active, w_fc2, preferred_element_type=jnp.float32).reshape(second_tile.shape)
    result = middle + sum_tile(out_part) + b_fc2
    saved_state = (
        source,
        middle,
        flat_rows,
        queries,
        key_rows,
        values,
        log_total,
        context,
        mlp_rows,
        hidden,
        offset,
        region_mask,
    )
    return (result, saved_state)


def backward_block(upstream, weights, saved_state, shifted):
    norm_gain, norm_bias, w_qkv, b_qv, table, w_proj, b_proj, w_fc1, b_fc1, w_fc2, b_fc2 = weights
    (
        source,
        middle,
        flat_rows,
        queries,
        key_rows,
        values,
        log_total,
        context,
        mlp_rows,
        hidden,
        offset,
        region_mask,
    ) = saved_state
    height = source.shape[0]
    window_count, window_len, heads_here, _ = queries.shape
    grad_low = upstream.astype(jnp.bfloat16)
    grad_tile = gather_grad(grad_low)
    grad_rows = grad_tile.reshape(-1, grad_tile.shape[-1])
    active = jax.nn.gelu(hidden, approximate=False).astype(jnp.bfloat16)
    g_fc2 = jnp.dot(active.T, grad_rows, preferred_element_type=jnp.float32)
    g_bfc2 = jnp.sum(grad_low.astype(jnp.float32), axis=(0, 1))
    g_active = jnp.dot(grad_rows, w_fc2.T, preferred_element_type=jnp.float32)
    g_hidden = jax.vjp(partial(jax.nn.gelu, approximate=False), hidden)[1](g_active)[0].astype(
        jnp.bfloat16
    )
    g_bfc1 = jnp.sum(g_hidden.astype(jnp.float32), axis=0)
    g_fc1 = jnp.dot(mlp_rows.T, g_hidden, preferred_element_type=jnp.float32)
    g_second = sum_grad(
        jnp.dot(g_hidden, w_fc1.T, preferred_element_type=jnp.float32).reshape(grad_tile.shape)
    )
    pull_second = jax.vjp(layer_norm, middle, norm_gain[1], norm_bias[1])[1]
    g_mid_norm, g_gain2, g_bias2 = pull_second(g_second)
    g_middle = upstream + g_mid_norm
    g_branch = g_middle.astype(jnp.bfloat16)
    if shifted:
        g_branch = roll_ahead(g_branch)
    g_bproj = jnp.sum(g_branch.astype(jnp.float32), axis=(0, 1))
    g_output = to_windows(gather_grad(g_branch))
    g_proj = jnp.dot(context.T, g_output, preferred_element_type=jnp.float32)
    g_context = jnp.dot(g_output, w_proj.T, preferred_element_type=jnp.float32).astype(jnp.bfloat16)
    g_context = g_context.reshape(window_count, window_len, heads_here, HEAD_DIM)
    logits = scores(queries, key_rows, offset, region_mask)
    probs = jnp.exp(logits - log_total[..., None])
    probs_low = probs.astype(jnp.bfloat16)
    g_values = jnp.einsum(
        "whqk,wqhd->wkhd", probs_low, g_context, preferred_element_type=jnp.float32
    ).astype(jnp.bfloat16)
    g_probs = jnp.einsum("wqhd,wkhd->whqk", g_context, values, preferred_element_type=jnp.float32)
    centre = jnp.sum(probs * g_probs, axis=-1, keepdims=True)
    g_logits = (probs * (g_probs - centre)).astype(jnp.bfloat16)
    g_table = table_grad(jnp.sum(g_logits.astype(jnp.float32), axis=0))
    inv_root = HEAD_DIM ** (-0.5)
    g_queries = (
        jnp.einsum("whqk,wkhd->wqhd", g_logits, key_rows, preferred_element_type=jnp.float32)
        * inv_root
    ).astype(jnp.bfloat16)
    g_keys = (
        jnp.einsum("whqk,wqhd->wkhd", g_logits, queries, preferred_element_type=jnp.float32)
        * inv_root
    ).astype(jnp.bfloat16)
    g_mixed = jnp.stack([g_queries, g_keys, g_values], axis=3).reshape(
        window_count * window_len, heads_here * 3 * HEAD_DIM
    )
    g_bqv = jnp.stack(
        [
            jnp.sum(g_queries.astype(jnp.float32), axis=(0, 1)),
            jnp.sum(g_values.astype(jnp.float32), axis=(0, 1)),
        ],
        axis=1,
    ).reshape(-1)
    g_qkv = jnp.dot(flat_rows.T, g_mixed, preferred_element_type=jnp.float32)
    g_first = sum_grad(
        from_windows(jnp.dot(g_mixed, w_qkv.T, preferred_element_type=jnp.float32), height)
    )
    if shifted:
        g_first = roll_behind(g_first.astype(jnp.bfloat16)).astype(jnp.float32)
    pull_first = jax.vjp(layer_norm, source, norm_gain[0], norm_bias[0])[1]
    g_source, g_gain1, g_bias1 = pull_first(g_first)
    g_input = g_middle + g_source
    sharded = (g_qkv, g_bqv, g_table, g_proj, g_fc1, g_bfc1, g_fc2)
    shared = (jnp.stack([g_gain1, g_gain2]), jnp.stack([g_bias1, g_bias2]), g_bproj, g_bfc2)
    return (g_input, sharded, shared)


def on_device(
    act_in,
    ln_gain,
    ln_bias,
    w_qkv,
    b_qv,
    rel_table,
    w_proj,
    b_proj,
    w_fc1,
    b_fc1,
    w_fc2,
    b_fc2,
    grad_out,
):
    params = (ln_gain, ln_bias, w_qkv, b_qv, rel_table, w_proj, b_proj, w_fc1, b_fc1, w_fc2, b_fc2)
    layers = [tuple((member[block_id] for member in params)) for block_id in range(BLOCKS)]
    residual = act_in.astype(jnp.float32)
    layer_inputs = []
    stored = []
    for block_id in range(BLOCKS):
        layer_inputs.append(residual)
        residual, saved_state = forward_block(residual, layers[block_id], block_id % 2 == 1)
        stored.append(saved_state)
    upstream = grad_out
    sharded_all = [None] * BLOCKS
    shared_all = [None] * BLOCKS
    for block_id in reversed(range(BLOCKS)):
        saved_state = forward_block(layer_inputs[block_id], layers[block_id], block_id % 2 == 1)[1]
        upstream, sharded, shared = backward_block(
            upstream, layers[block_id], saved_state, block_id % 2 == 1
        )
        sharded_all[block_id] = sharded
        shared_all[block_id] = shared
    sharded_stack = tuple(
        (jnp.stack([entry[member] for entry in sharded_all]) for member in range(7))
    )
    shared_stack = tuple(
        (jnp.stack([entry[member] for entry in shared_all]) for member in range(4))
    )
    packed_all = pack_members(sharded_stack)
    packed_part = lax.psum_scatter(
        packed_all.astype(jnp.bfloat16), ("band", "col"), scatter_dimension=0, tiled=True
    ).astype(jnp.float32)
    packed_all = lax.all_gather(
        packed_part.astype(jnp.bfloat16), ("band", "col"), axis=0, tiled=True
    ).astype(packed_part.dtype)
    sharded_stack = unpack_members(packed_all, sharded_stack)
    shared_stack = lax.psum(shared_stack, ("band", "col", "head"))
    return (
        residual,
        upstream,
        shared_stack[0],
        shared_stack[1],
        sharded_stack[0],
        sharded_stack[1],
        sharded_stack[2],
        sharded_stack[3],
        shared_stack[2],
        sharded_stack[4],
        sharded_stack[5],
        sharded_stack[6],
        shared_stack[3],
    )


F32 = jnp.float32
BF16 = jnp.bfloat16
WIDTH = 512
QUAD = 32
LIVE = SHIFT * SHIFT
UNIT = 2 * QUAD
TOK = 2 * UNIT
TILE = 4 * UNIT
PAIR = 2 * TILE
GROUP = 8
SPAN = GROUP * HEAD_DIM
KEYS = GROUP * TOK
OFFSETS = 2 * WIN - 1
ENTRIES = 384
SCALE = HEAD_DIM ** (-0.5)
FAR = -1e30
ROOT_HALF = 0.5 ** 0.5
ROOT_TWO_PI = (2.0 * np.pi) ** (-0.5)
VMEM = pl.BlockSpec(memory_space=pltpu.VMEM)
SMEM = pl.BlockSpec(memory_space=pltpu.SMEM)
ROWS_QKV = 3 * 512
ROWS_ATT = ROWS_QKV + 512
ROWS_MLP = 4096
HALF_ATT = ROWS_ATT // 2
HEAD, COL = 0, 1


def shape_of(shape, kind):
    return jax.ShapeDtypeStruct(shape, kind)


def layer_spec(array, layer):
    rest = array.shape[1:]
    return pl.BlockSpec((1,) + rest, lambda _: (layer,) + (0,) * len(rest), pipeline_mode=pl.Buffered(1))


COSTS = {
    "attention_plain_kernel": 6.0,
    "mlp_plain_kernel": 4.5,
    "attention_shifted_kernel": 5.5,
    "mlp_shifted_kernel": 5.0,
    "attention_shifted_back_kernel": 6.0,
    "mlp_plain_back_kernel": 2.0,
    "attention_plain_back_kernel": 6.0,
    "mlp_weights_kernel": 2.0,
    "attention_weights_plain_kernel": 2.0,
    "attention_weights_shifted_kernel": 2.7,
    "table_kernel": 1.2,
    "bias_body": 1.2,
    "pack_kernel": 1.5,
    "unpack_mlp_kernel": 3.0,
    "unpack_att_kernel": 3.5,
}


def run_kernel(kernel, operands, outs, scratch=(), limit=24, specs=None, aliases=None, out_specs=None):
    specs = specs or {}
    name = getattr(kernel, "func", kernel).__name__
    in_specs = [specs.get(place, VMEM) for place in range(len(operands))]
    return pl.pallas_call(
        kernel,
        grid=(1,),
        in_specs=in_specs,
        out_specs=out_specs or [VMEM] * len(outs),
        out_shape=list(outs),
        scratch_shapes=list(scratch),
        input_output_aliases=aliases or {},
        cost_estimate=pl.CostEstimate(
            flops=int(COSTS.get(name, 0.7) * 16.0 * 1.15e9), bytes_accessed=1 << 10, transcendentals=0
        ),
        compiler_params=pltpu.CompilerParams(vmem_limit_bytes=limit << 20),
        name=name,
    )(*operands)


def mm(left, right):
    return lax.dot_general(left, right, (((1,), (0,)), ((), ())), preferred_element_type=F32)


def mm_nt(left, right):
    return lax.dot_general(left, right, (((1,), (1,)), ((), ())), preferred_element_type=F32)


def mm_tn(left, right):
    return lax.dot_general(left, right, (((0,), (0,)), ((), ())), preferred_element_type=F32)


def halves_of(value):
    high = value.astype(BF16)
    return high, (value - high.astype(F32)).astype(BF16)


def norm_parts(value):
    centre = value - jnp.mean(value, axis=-1, keepdims=True)
    inverse = lax.rsqrt(jnp.mean(centre * centre, axis=-1, keepdims=True) + EPSILON)
    return centre * inverse, inverse


def norm_back(grad, gain, unit, inverse):
    scaled = grad * gain
    return (
        scaled
        - jnp.mean(scaled, axis=-1, keepdims=True)
        - unit * jnp.mean(scaled * unit, axis=-1, keepdims=True)
    ) * inverse


def column_sum(value):
    return jnp.sum(value, axis=0, keepdims=True)


def put_row(ref, row, value):
    for part in range(value.shape[1] // 256):
        ref[row + part : row + part + 1, :] = value[:, 256 * part : 256 * (part + 1)]


def token_place(row, col):
    return ((col // SHIFT) * 2 + row // SHIFT) * QUAD + (row % SHIFT) * SHIFT + col % SHIFT


def constants():
    row_map = np.zeros((TOK, 160), np.float32)
    col_map = np.zeros((TOK, TOK), np.float32)
    token_row = np.zeros((TOK,), np.int32)
    token_col = np.zeros((TOK,), np.int32)
    for row in range(WIN):
        for col in range(WIN):
            place = token_place(row, col)
            row_map[place, row * 16 + col] = 1.0
            col_map[row * WIN + col, place] = 1.0
            token_row[place] = row
            token_col[place] = col
    base = np.full((1, 256), -4000, np.int32)
    for lane in range(OFFSETS * WIN):
        base[0, lane] = (OFFSETS - 1 - lane // WIN) * OFFSETS - lane % WIN + WIN - 1
    order = np.zeros((768, 768), np.float32)
    for head in range(GROUP):
        for part in range(3):
            for place in range(HEAD_DIM):
                order[head * 96 + part * 32 + place, part * SPAN + head * HEAD_DIM + place] = 1.0
    heads = np.zeros((KEYS, SPAN), np.float32)
    for head in range(GROUP):
        heads[head * TOK : (head + 1) * TOK, head * HEAD_DIM : (head + 1) * HEAD_DIM] = 1.0
    return (
        jnp.asarray(row_map, BF16),
        jnp.asarray(row_map.T, BF16),
        jnp.asarray(col_map, BF16),
        jnp.asarray(base),
        jnp.asarray(order, BF16),
        jnp.asarray(heads, BF16),
        token_row,
        token_col,
    )


def enter_rows(in_ref, buf, start):
    for row in range(WIN):
        line = in_ref[row].astype(F32)
        for unit in range(4):
            first = unit * UNIT + (row // SHIFT) * QUAD + (row % SHIFT) * SHIFT
            buf[start + first : start + first + SHIFT, :] = line[unit * SHIFT : (unit + 1) * SHIFT, :]


def enter_kernel(in_ref, out_ref, buf):
    buf[...] = jnp.zeros(buf.shape, F32)
    enter_rows(in_ref, buf, 0)
    out_ref[...] = buf[...].astype(BF16)


def enter_units(tile):
    return run_kernel(
        enter_kernel, [tile], [shape_of((TILE, WIDTH), BF16)], [pltpu.VMEM((TILE, WIDTH), F32)]
    )[0]


def leave_rows(value_ref, out_ref):
    for row in range(WIN):
        for unit in range(4):
            start = unit * UNIT + (row // SHIFT) * QUAD + (row % SHIFT) * SHIFT
            out_ref[row, unit * SHIFT : (unit + 1) * SHIFT, :] = value_ref[start : start + SHIFT, :]


def leave_kernel(first, stay, come, out_ref, buf):
    buf[0:UNIT, :] = first[...].astype(F32)
    for unit in range(3):
        lines = slice(QUAD * unit, QUAD * (unit + 1))
        start = UNIT * (unit + 1)
        buf[start : start + QUAD, :] = come[lines, :].astype(F32)
        buf[start + QUAD : start + UNIT, :] = stay[lines, :].astype(F32)
    leave_rows(buf, out_ref)


def part_quads(value, upper, lower, units):
    for unit in range(units):
        lines = slice(QUAD * unit, QUAD * (unit + 1))
        upper[lines, :] = value[UNIT * unit : UNIT * unit + QUAD, :].astype(upper.dtype)
        lower[lines, :] = value[UNIT * unit + QUAD : UNIT * (unit + 1), :].astype(lower.dtype)


def join_quads(out, start, upper, lower, units):
    for unit in range(units):
        lines = slice(QUAD * unit, QUAD * (unit + 1))
        first = start + UNIT * unit
        out[first : first + QUAD, :] = upper[lines, :]
        out[first + QUAD : first + UNIT, :] = lower[lines, :]


def enter_entry_kernel(keep, come, stay_main, send_main, edge, buf):
    buf[...] = keep[...] + come[...].astype(F32)
    part_quads(buf, send_main, stay_main, 3)
    edge[...] = buf[3 * UNIT :, :].astype(BF16)


def edge_kernel(place, own, come, upper, lower):
    taken = jnp.where(place[0] == 1, come[...], own[...])
    upper[...] = taken[:QUAD, :]
    lower[...] = taken[QUAD:, :]


def grad_join_kernel(place, own, other, send, stay, buf):
    here = place[0]
    buf[pl.ds(pl.multiple_of(here * TILE, TILE), TILE), :] = own[...]
    buf[pl.ds(pl.multiple_of((1 - here) * TILE, TILE), TILE), :] = other[...]
    part_quads(buf, send, stay, 8)


def last_entry_kernel(keep, come, middle, b_fc2, send, stay, buf):
    buf[...] = keep[...] + come[...].astype(F32) + middle[...] + b_fc2[...]
    part_quads(buf, stay, send, 4)


def entry_onehot(base_ref):
    entry = lax.broadcasted_iota(jnp.int32, (ENTRIES, 256), 0)
    return (entry == base_ref[...]).astype(F32).astype(BF16)


LINES = WIN * GROUP


def bias_body(table_ref, base_ref, row_map_ref, col_map_ref, out_ref, left, right, strip):
    table = table_ref[...]
    turned = jnp.concatenate([pltpu.roll(table, ENTRIES - col, 1) if col else table for col in range(WIN)], axis=0)
    high, low = halves_of(turned)
    onehot = entry_onehot(base_ref)
    spread = mm(high, onehot) + mm(low, onehot)
    left[0:LINES, :] = spread[:, :128]
    right[0:LINES, :] = spread[:, 128:]
    left[LINES:, :] = jnp.zeros((16 * GROUP - LINES, 128), F32)
    right[LINES:, :] = jnp.zeros((16 * GROUP - LINES, 128), F32)
    for head in range(GROUP):
        wide = jnp.concatenate(
            [left[pl.ds(head, 16, stride=GROUP), :], right[pl.ds(head, 16, stride=GROUP), :]], axis=1
        )
        for row in range(WIN):
            start = (WIN - 1 - row) * WIN
            strip[16 * row : 16 * (row + 1), TOK * head : TOK * (head + 1)] = wide[:, start : start + TOK]
    high, low = halves_of(strip[...])
    rows = mm(row_map_ref[...], high) + mm(row_map_ref[...], low)
    live = lax.broadcasted_iota(jnp.int32, (TOK, TOK), 1) % QUAD < LIVE
    for head in range(GROUP):
        high, low = halves_of(rows[:, TOK * head : TOK * (head + 1)])
        value = mm(high, col_map_ref[...]) + mm(low, col_map_ref[...])
        out_ref[:, TOK * head : TOK * (head + 1)] = jnp.where(live, value, FAR)


BIAS_SCRATCH = (
    pltpu.VMEM((16 * GROUP, 128), F32),
    pltpu.VMEM((16 * GROUP, 128), F32),
    pltpu.VMEM((160, KEYS), F32),
)


def table_body(sum_ref, base_ref, row_back_ref, col_map_ref, out_ref, row, left, right, strip):
    high, low = halves_of(sum_ref[...])
    turned = [
        mm_nt(high[:, TOK * head : TOK * (head + 1)], col_map_ref[...])
        + mm_nt(low[:, TOK * head : TOK * (head + 1)], col_map_ref[...])
        for head in range(GROUP)
    ]
    high, low = halves_of(jnp.concatenate(turned, axis=1))
    strip[...] = mm(row_back_ref[...], high) + mm(row_back_ref[...], low)
    for head in range(GROUP):
        total = jnp.zeros((16, 256), F32)
        for line in range(WIN):
            block = strip[16 * line : 16 * (line + 1), TOK * head : TOK * (head + 1)]
            wide = jnp.concatenate([block, jnp.zeros((16, 128), F32)], axis=1)
            start = (WIN - 1 - line) * WIN
            total = total + (pltpu.roll(wide, start, 1) if start else wide)
        left[pl.ds(head, 16, stride=GROUP), :] = total[:, :128]
        right[pl.ds(head, 16, stride=GROUP), :] = total[:, 128:]
    onehot = entry_onehot(base_ref)
    high, low = halves_of(jnp.concatenate([left[0:LINES, :], right[0:LINES, :]], axis=1))
    spread = mm_nt(high, onehot) + mm_nt(low, onehot)
    table = spread[0:GROUP, :]
    for col in range(1, WIN):
        table = table + pltpu.roll(spread[GROUP * col : GROUP * (col + 1), :], col, 1)
    out_ref[row : row + GROUP, :] = table[:, :256]
    out_ref[row + GROUP : row + 2 * GROUP, :] = jnp.concatenate(
        [table[:, 256:], jnp.zeros((GROUP, 128), F32)], axis=1
    )


def pack_kernel(place, w_qkv_ref, w_proj_ref, order_ref, out_ref, half_ref=None):
    mixed = mm(w_qkv_ref[0], order_ref[...]).astype(BF16)
    for part in range(3):
        out_ref[512 * part : 512 * (part + 1), :] = mixed[:, 256 * part : 256 * (part + 1)]
    for part in range(2):
        out_ref[ROWS_QKV + 256 * part : ROWS_QKV + 256 * (part + 1), :] = w_proj_ref[
            0, :, 256 * part : 256 * (part + 1)
        ]
    if half_ref is not None:
        half_ref[...] = out_ref[pl.ds(pl.multiple_of(place[COL] * HALF_ATT, HALF_ATT), HALF_ATT), :]


def pack_weights(place, w_qkv, w_proj, order, layer, rows):
    return run_kernel(
        pack_kernel,
        [place, w_qkv, w_proj, order],
        [shape_of((count, 256), BF16) for count in rows],
        specs={0: SMEM, 1: layer_spec(w_qkv, layer), 2: layer_spec(w_proj, layer)},
    )


def pack_join_kernel(place, mine, theirs, out_ref):
    here = place[COL]
    out_ref[pl.ds(pl.multiple_of(here * HALF_ATT, HALF_ATT), HALF_ATT), :] = mine[...]
    out_ref[pl.ds(pl.multiple_of((1 - here) * HALF_ATT, HALF_ATT), HALF_ATT), :] = theirs[...]


def bias_of(table, base, row_map, col_map):
    return run_kernel(
        bias_body,
        [table, base, row_map, col_map],
        [shape_of((TOK, KEYS), F32)],
        BIAS_SCRATCH,
    )[0]


def project(normed, pack_ref, qv_ref):
    parts = [mm(normed, pack_ref[512 * part : 512 * (part + 1), :]) for part in range(3)]
    return (
        (parts[0] + qv_ref[0:1, :]).astype(BF16),
        parts[1].astype(BF16),
        (parts[2] + qv_ref[1:2, :]).astype(BF16),
    )


def spread_heads(ref, value, heads_ref):
    for head in range(GROUP):
        lines = slice(TOK * head, TOK * (head + 1))
        ref[lines, :] = value * heads_ref[lines, :]


def attend(qkv_ref, base, bias_ref, region, heads_ref, probs_ref, probs_base, stack, wide):
    rows = pl.ds(base, TOK)
    spread_heads(stack, qkv_ref[rows, 256:512], heads_ref)
    logits = mm_nt(qkv_ref[rows, 0:256], stack[...])
    for head in range(GROUP):
        lanes = slice(TOK * head, TOK * (head + 1))
        score = logits[:, lanes] * SCALE + bias_ref[:, lanes]
        if region is not None:
            score = score + region
        grown = jnp.exp(score - jnp.max(score, axis=-1, keepdims=True))
        probs = (grown / jnp.sum(grown, axis=-1, keepdims=True)).astype(BF16)
        wide[:, lanes] = probs
        probs_ref[pl.ds(probs_base + TOK * head, TOK), :] = probs
    spread_heads(stack, qkv_ref[rows, 512:768], heads_ref)
    return mm(wide[...], stack[...]).astype(BF16)


def attend_back(qkv_ref, base, grad, heads_ref, probs_ref, probs_base, total_ref, stack, wide, tall, mixed_ref):
    rows = pl.ds(base, TOK)
    spread_heads(stack, qkv_ref[rows, 512:768], heads_ref)
    grad_probs = mm_nt(grad, stack[...])
    for head in range(GROUP):
        lanes = slice(TOK * head, TOK * (head + 1))
        probs = probs_ref[pl.ds(probs_base + TOK * head, TOK), :].astype(F32)
        part = grad_probs[:, lanes]
        centre = jnp.sum(probs * part, axis=-1, keepdims=True)
        inner = (probs * (part - centre)).astype(BF16)
        wide[:, lanes] = inner
        tall[lanes, :] = inner
        total_ref[:, lanes] = total_ref[:, lanes] + inner.astype(F32)
    spread_heads(stack, grad, heads_ref)
    mixed_ref[rows, 512:768] = mm_tn(probs_ref[pl.ds(probs_base, KEYS), :], stack[...]).astype(BF16)
    spread_heads(stack, qkv_ref[rows, 256:512], heads_ref)
    mixed_ref[rows, 0:256] = (mm(wide[...], stack[...]) * SCALE).astype(BF16)
    spread_heads(stack, qkv_ref[rows, 0:256], heads_ref)
    mixed_ref[rows, 256:512] = (mm_tn(tall[...], stack[...]) * SCALE).astype(BF16)


def project_out(context, pack_ref):
    return jnp.concatenate(
        [mm(context, pack_ref[ROWS_QKV + 256 * part : ROWS_QKV + 256 * (part + 1), :]) for part in range(2)],
        axis=1,
    )


def project_out_back(grad, pack_ref):
    return (
        mm_nt(grad[:, :256], pack_ref[ROWS_QKV : ROWS_QKV + 256, :])
        + mm_nt(grad[:, 256:], pack_ref[ROWS_QKV + 256 : ROWS_ATT, :])
    ).astype(BF16)


def project_back(mixed_ref, pack_ref):
    total = mm_nt(mixed_ref[:, 0:256], pack_ref[0:512, :])
    for part in range(1, 3):
        total = total + mm_nt(mixed_ref[:, 256 * part : 256 * (part + 1)], pack_ref[512 * part : 512 * (part + 1), :])
    return total


ATTEND_SCRATCH = (pltpu.VMEM((KEYS, SPAN), BF16), pltpu.VMEM((TOK, KEYS), BF16))


def attention_plain_kernel(
    place_ref, own, other, gain, bias, pack, qv, offset, heads,
    whole, normed_out, qkv, probs, context, part_out, stack, wide, buf,
):
    here = place_ref[HEAD]
    buf[...] = jnp.zeros(buf.shape, F32)
    enter_rows(own, buf, 0)
    enter_rows(other, buf, TILE)
    whole[pl.ds(pl.multiple_of(here * TILE, TILE), TILE), :] = buf[:TILE, :].astype(BF16)
    whole[pl.ds(pl.multiple_of((1 - here) * TILE, TILE), TILE), :] = buf[TILE:, :].astype(BF16)
    unit, _ = norm_parts(whole[...].astype(F32))
    normed_out[...] = (unit * gain[...] + bias[...]).astype(BF16)
    for part, value in enumerate(project(normed_out[...], pack, qv)):
        qkv[:, 256 * part : 256 * (part + 1)] = value

    def window(place, carry):
        base = pl.multiple_of(place * TOK, TOK)
        context[pl.ds(base, TOK), :] = attend(
            qkv, base, offset, None, heads, probs, pl.multiple_of(place * KEYS, KEYS), stack, wide
        )
        return carry

    lax.fori_loop(0, PAIR // TOK, window, 0)
    part_out[...] = project_out(context[...], pack).astype(BF16)


def attention_shifted_kernel(
    stay_main, come_main, stay_edge, come_edge, gain, bias, gain2, bias2, pack_a, pack_b, qv_a, qv_b, off_a, off_b,
    ids_q, ids_k, heads, b_proj,
    keep, normed_out, qkv_a, qkv_b, probs_a, probs_b, context_a, context_b, middle_out, second_out, stack, wide,
):
    join_quads(keep, 0, stay_main, come_main, 3)
    join_quads(keep, 3 * UNIT, stay_edge, come_edge, 1)
    unit, _ = norm_parts(keep[...].astype(F32))
    normed_out[...] = (unit * gain[...] + bias[...]).astype(BF16)
    total = keep[...].astype(F32) + b_proj[...]
    for pack, qv, off, qkv, probs, context in (
        (pack_a, qv_a, off_a, qkv_a, probs_a, context_a),
        (pack_b, qv_b, off_b, qkv_b, probs_b, context_b),
    ):
        for part, value in enumerate(project(normed_out[...], pack, qv)):
            qkv[:, 256 * part : 256 * (part + 1)] = value

        def window(place, carry):
            base = pl.multiple_of(place * TOK, TOK)
            region = jnp.where(ids_q[pl.ds(base, TOK), :] != ids_k[place], -100.0, 0.0)
            context[pl.ds(base, TOK), :] = attend(
                qkv, base, off, region, heads, probs, pl.multiple_of(place * KEYS, KEYS), stack, wide
            )
            return carry

        lax.fori_loop(0, TILE // TOK, window, 0)
        total = total + project_out(context[...], pack)
    middle_out[...] = total
    unit, _ = norm_parts(total)
    second_out[...] = (unit * gain2[...] + bias2[...]).astype(BF16)


def gelu_parts(hidden):
    chance = 0.5 * (1.0 + lax.erf(hidden * ROOT_HALF))
    slope = chance + hidden * (jnp.exp(-0.5 * hidden * hidden) * ROOT_TWO_PI)
    return (hidden * chance).astype(BF16), slope.astype(BF16)


CHUNK = 256


def mlp_plain_kernel(
    place_ref, whole, part_own, part_other, b_proj, gain, bias, w_fc1, b_fc1, w_fc2, b_fc2,
    middle, second, active, slope, keep, send, spun,
):
    here = place_ref[HEAD]
    middle[...] = (
        whole[...].astype(F32) + (part_own[...].astype(F32) + part_other[...].astype(F32)) + b_proj[...]
    )
    unit, _ = norm_parts(middle[...])
    second[...] = (unit * gain[...] + bias[...]).astype(BF16)
    for place in range(1024 // CHUNK):
        lanes = slice(CHUNK * place, CHUNK * (place + 1))
        hidden = mm(second[...], w_fc1[0, :, lanes]) + b_fc1[:, lanes]
        active[:, lanes], slope[:, lanes] = gelu_parts(hidden)
    out = mm(active[...], w_fc2[0])
    spun[0 : PAIR - UNIT, :] = out[UNIT:, :]
    spun[PAIR - UNIT :, :] = out[:UNIT, :]
    send[...] = spun[pl.ds((1 - here) * TILE, TILE), :].astype(BF16)
    spun[0 : PAIR - UNIT, :] = spun[0 : PAIR - UNIT, :] + middle[UNIT:, :]
    spun[PAIR - UNIT :, :] = spun[PAIR - UNIT :, :] + middle[:UNIT, :]
    keep[...] = spun[pl.ds(here * TILE, TILE), :] + b_fc2[...]


def mlp_shifted_kernel(
    place_ref, own, other, grad_stay, grad_come, grad_far, w_fc1, b_fc1, w_fc2,
    second, grad, active, inner, keep, send, back_keep, back_send, small, slope,
):
    here = place_ref[HEAD]
    mine = pl.ds(pl.multiple_of(here * TILE, TILE), TILE)
    theirs = pl.ds(pl.multiple_of((1 - here) * TILE, TILE), TILE)
    for unit in range(1, 8):
        lines = slice(QUAD * unit, QUAD * (unit + 1))
        first = UNIT * (unit - 1)
        grad[first : first + QUAD, :] = grad_stay[lines, :]
        grad[first + QUAD : first + UNIT, :] = grad_come[lines, :]
    grad[7 * UNIT :, :] = grad_far[...]
    second[mine, :] = own[...]
    second[theirs, :] = other[...]
    for place in range(1024 // CHUNK):
        lanes = slice(CHUNK * place, CHUNK * (place + 1))
        hidden = mm(second[...], w_fc1[0, :, lanes]) + b_fc1[:, lanes]
        active[:, lanes], slope[:, lanes] = gelu_parts(hidden)
    for place in range(1024 // CHUNK):
        lanes = slice(CHUNK * place, CHUNK * (place + 1))
        back = mm_nt(grad[...], w_fc2[0, lanes, :]) * slope[:, lanes].astype(F32)
        inner[:, lanes] = back.astype(BF16)
    back_keep[...] = mm_nt(inner[mine, :], w_fc1[0])
    back_send[...] = mm_nt(inner[theirs, :], w_fc1[0]).astype(BF16)
    keep[...] = mm(active[mine, :], w_fc2[0])
    send[...] = mm(active[theirs, :], w_fc2[0]).astype(BF16)
    put_row(small, 0, column_sum(inner[...].astype(F32)))
    small[4:, :] = jnp.zeros((4, 256), F32)


def mlp_plain_back_kernel(
    place_ref, stay_own, stay_other, come_own, come_other, edge_own, edge_other, slope, w_fc1, w_fc2,
    grad, inner, back, spun,
):
    for which, (stay, come, edge) in enumerate(
        ((stay_own, come_own, edge_own), (stay_other, come_other, edge_other))
    ):
        here = place_ref[HEAD] if which == 0 else 1 - place_ref[HEAD]
        start = pl.multiple_of(here * TILE, TILE)
        for unit in range(3):
            lines = slice(QUAD * unit, QUAD * (unit + 1))
            spun[pl.ds(start + UNIT * unit, QUAD), :] = come[lines, :]
            spun[pl.ds(start + UNIT * unit + QUAD, QUAD), :] = stay[lines, :]
        spun[pl.ds(start + 3 * UNIT, UNIT), :] = edge[...]
    grad[0:UNIT, :] = spun[PAIR - UNIT :, :]
    grad[UNIT:, :] = spun[0 : PAIR - UNIT, :]
    for place in range(1024 // CHUNK):
        lanes = slice(CHUNK * place, CHUNK * (place + 1))
        value = mm_nt(grad[...], w_fc2[0, lanes, :]) * slope[:, lanes].astype(F32)
        inner[:, lanes] = value.astype(BF16)
    back[...] = mm_nt(inner[...], w_fc1[0]).astype(BF16)


def deal_halves(place_ref, whole, keep, send, half, base=0, start=0):
    mine = pl.multiple_of(place_ref[COL] * half, half)
    theirs = pl.multiple_of((1 - place_ref[COL]) * half, half)
    keep[start : start + half, :] = whole[pl.ds(base + mine, half), :]
    send[start : start + half, :] = whole[pl.ds(base + theirs, half), :]


def mlp_weights_kernel(place_ref, second, active, grad, inner, keep, send, out):
    for place in range(4):
        lanes = slice(256 * place, 256 * (place + 1))
        out[512 * place : 512 * (place + 1), :] = mm_tn(second[...], inner[:, lanes]).astype(BF16)
    for place in range(2):
        lanes = slice(256 * place, 256 * (place + 1))
        start = 2048 + 1024 * place
        out[start : start + 1024, :] = mm_tn(active[...], grad[:, lanes]).astype(BF16)
    deal_halves(place_ref, out, keep, send, ROWS_MLP // 2)


def mlp_weights(place, second, active, grad, inner):
    return run_kernel(
        mlp_weights_kernel,
        [place, second, active, grad, inner],
        [shape_of((ROWS_MLP // 2, 256), BF16)] * 2,
        [pltpu.VMEM((ROWS_MLP, 256), BF16)],
        specs={0: SMEM},
    )


def attention_shifted_back_kernel(
    place_ref, grad_all, back_own, back_other, middle, entry, gain, gain2, qkv_a, qkv_b, probs_a, probs_b,
    pack_a, pack_b, heads,
    grad_low, mixed_a, mixed_b, total_a, total_b, stay_main, send_main, edge, small,
    stack, wide, tall, grad_context, below,
):
    here = place_ref[HEAD]
    upstream = grad_all[pl.ds(pl.multiple_of(here * TILE, TILE), TILE), :].astype(F32)
    back = back_own[...] + back_other[...].astype(F32)
    unit, inverse = norm_parts(middle[...])
    put_row(small, 0, column_sum(back * unit))
    put_row(small, 2, column_sum(back))
    put_row(small, 4, column_sum(upstream))
    grad_middle = upstream + norm_back(back, gain2[...], unit, inverse)
    grad_low[...] = grad_middle.astype(BF16)
    put_row(small, 6, column_sum(grad_low[...].astype(F32)))
    first = jnp.zeros((TILE, WIDTH), F32)
    for pack, qkv, probs, mixed, total in (
        (pack_a, qkv_a, probs_a, mixed_a, total_a),
        (pack_b, qkv_b, probs_b, mixed_b, total_b),
    ):
        grad_context[...] = project_out_back(grad_low[...], pack)
        total[...] = jnp.zeros((TOK, KEYS), F32)

        def window(place, carry):
            base = pl.multiple_of(place * TOK, TOK)
            attend_back(
                qkv, base, grad_context[pl.ds(base, TOK), :], heads, probs, pl.multiple_of(place * KEYS, KEYS),
                total, stack, wide, tall, mixed,
            )
            return carry

        lax.fori_loop(0, TILE // TOK, window, 0)
        first = first + project_back(mixed, pack)
    unit, inverse = norm_parts(entry[...].astype(F32))
    put_row(small, 8, column_sum(first * unit))
    put_row(small, 10, column_sum(first))
    put_row(small, 12, column_sum(mixed_a[...].astype(F32)))
    small[15:16, :] = jnp.zeros((1, 256), F32)
    put_row(small, 16, column_sum(mixed_b[...].astype(F32)))
    small[19:24, :] = jnp.zeros((5, 256), F32)
    below[...] = grad_middle + norm_back(first, gain[...], unit, inverse)
    part_quads(below, stay_main, send_main, 3)
    edge[...] = below[3 * UNIT :, :].astype(BF16)


def attention_plain_back_kernel(
    place_ref, grad, back_own, back_other, middle, whole, gain, gain2, qkv, probs, pack, heads, inner,
    grad_low, mixed, total, first_keep, first_send, kept, small, stack, wide, tall, grad_context, first,
):
    here = place_ref[HEAD]
    mine = pl.ds(pl.multiple_of(here * TILE, TILE), TILE)
    theirs = pl.ds(pl.multiple_of((1 - here) * TILE, TILE), TILE)
    back = back_own[...].astype(F32) + back_other[...].astype(F32)
    unit, inverse = norm_parts(middle[...])
    share = back_own[...].astype(F32)
    put_row(small, 0, column_sum(share * unit))
    put_row(small, 2, column_sum(share))
    put_row(small, 4, column_sum(grad[mine, :].astype(F32)))
    first[...] = grad[...].astype(F32) + norm_back(back, gain2[...], unit, inverse)
    kept[...] = first[mine, :]
    grad_low[...] = first[...].astype(BF16)
    put_row(small, 6, column_sum(grad_low[mine, :].astype(F32)))
    grad_context[...] = project_out_back(grad_low[...], pack)
    total[...] = jnp.zeros((TOK, KEYS), F32)

    def window(place, carry):
        base = pl.multiple_of(place * TOK, TOK)
        attend_back(
            qkv, base, grad_context[pl.ds(base, TOK), :], heads, probs, pl.multiple_of(place * KEYS, KEYS),
            total, stack, wide, tall, mixed,
        )
        return carry

    lax.fori_loop(0, PAIR // TOK, window, 0)
    first[...] = project_back(mixed, pack)
    first_keep[...] = first[mine, :]
    first_send[...] = first[theirs, :].astype(BF16)
    unit, _ = norm_parts(whole[...].astype(F32))
    put_row(small, 8, column_sum(first[...] * unit))
    put_row(small, 10, column_sum(first[...]))
    put_row(small, 12, column_sum(mixed[...].astype(F32)))
    small[15:16, :] = jnp.zeros((1, 256), F32)
    put_row(small, 16, column_sum(inner[...].astype(F32)))
    small[20:24, :] = jnp.zeros((4, 256), F32)


def attention_weights_body(normed, mixed, context, grad_low, order, out, start):
    turned = [mm_tn(normed[...], mixed[:, 256 * part : 256 * (part + 1)]).astype(BF16) for part in range(3)]
    canon = mm_nt(jnp.concatenate(turned, axis=1), order[...]).astype(BF16)
    for part in range(3):
        out[start + 512 * part : start + 512 * (part + 1), :] = canon[:, 256 * part : 256 * (part + 1)]
    for part in range(2):
        lines = slice(start + ROWS_QKV + 256 * part, start + ROWS_QKV + 256 * (part + 1))
        out[lines, :] = mm_tn(context[...], grad_low[:, 256 * part : 256 * (part + 1)]).astype(BF16)


def attention_weights_plain_kernel(place_ref, normed, mixed, context, grad_low, order, keep, send, out):
    attention_weights_body(normed, mixed, context, grad_low, order, out, 0)
    deal_halves(place_ref, out, keep, send, HALF_ATT)


def attention_weights_shifted_kernel(
    place_ref, normed, mixed_a, mixed_b, context_a, context_b, grad_low, order, keep, send, out
):
    attention_weights_body(normed, mixed_a, context_a, grad_low, order, out, 0)
    attention_weights_body(normed, mixed_b, context_b, grad_low, order, out, ROWS_ATT)
    deal_halves(place_ref, out, keep, send, HALF_ATT)
    deal_halves(place_ref, out, keep, send, HALF_ATT, ROWS_ATT, HALF_ATT)


def table_kernel(total, base, row_back, col_map, out, left, right, strip):
    table_body(total, base, row_back, col_map, out, 0, left, right, strip)


def table_of(total, base, row_back, col_map):
    return run_kernel(
        table_kernel, [total, base, row_back, col_map], [shape_of((2 * GROUP, 256), F32)], BIAS_SCRATCH
    )[0]


def last_kernel(place_ref, whole, gain, keep, other, kept, out, buf):
    here = place_ref[HEAD]
    unit, inverse = norm_parts(whole[pl.ds(pl.multiple_of(here * TILE, TILE), TILE), :].astype(F32))
    buf[...] = kept[...] + norm_back(keep[...] + other[...].astype(F32), gain[...], unit, inverse)
    leave_rows(buf, out)


def band_pairs(first, second):
    return [(band * 2 + col, (band ^ (first if col == 0 else second)) * 2 + col) for band in range(8) for col in range(2)]


STEP_PAIRS = (
    [(band * 2 + col, band * 2 + 1 - col) for band in range(8) for col in range(2)],
    band_pairs(1, 2),
    band_pairs(2, 4),
    band_pairs(4, 1),
)


def exchange(value, step):
    return lax.ppermute(value, ("band", "col"), STEP_PAIRS[step])


def halve_kernel(place_ref, kept, come, keep, send, *, step):
    half = keep.shape[0]
    mine = pl.ds(pl.multiple_of(place_ref[COL + step] * half, half), half)
    theirs = pl.ds(pl.multiple_of((1 - place_ref[COL + step]) * half, half), half)
    keep[...] = (kept[mine, :].astype(F32) + come[mine, :].astype(F32)).astype(BF16)
    send[...] = (kept[theirs, :].astype(F32) + come[theirs, :].astype(F32)).astype(BF16)


def halve(place, kept, come, step):
    half = kept.shape[0] // 2
    return run_kernel(
        partial(halve_kernel, step=step), [place, kept, come], [shape_of((half, 256), BF16)] * 2, specs={0: SMEM}
    )


def both_kernel(kept, come, out):
    out[...] = (kept[...].astype(F32) + come[...].astype(F32)).astype(BF16)


def both(kept, come):
    return run_kernel(both_kernel, [kept, come], [shape_of(kept.shape, BF16)])[0]


def across_kernel(kept, come, keep, send):
    total = (kept[...].astype(F32) + come[...].astype(F32)).astype(BF16)
    keep[...] = total[:HALF_ATT, :]
    send[...] = total[HALF_ATT:, :]


def double_kernel(place_ref, mine, come, out, *, step):
    half = mine.shape[0]
    out[pl.ds(pl.multiple_of(place_ref[COL + step] * half, half), half), :] = mine[...]
    out[pl.ds(pl.multiple_of((1 - place_ref[COL + step]) * half, half), half), :] = come[...]


def double(place, mine, come, step):
    return run_kernel(
        partial(double_kernel, step=step),
        [place, mine, come],
        [shape_of((2 * mine.shape[0], 256), BF16)],
        specs={0: SMEM},
    )[0]


def after(value, *others):
    return lax.optimization_barrier((value,) + others)[0]


def halve_pair_kernel(place_ref, kept_a, come_a, kept_b, come_b, keep, send):
    first = kept_a[...].astype(F32) + come_a[...].astype(F32)
    second = kept_b[...].astype(F32) + come_b[...].astype(F32)
    lower = place_ref[COL + 1] == 0
    keep[...] = jnp.where(lower, first, second).astype(BF16)
    send[...] = jnp.where(lower, second, first).astype(BF16)


class PageSum:
    def __init__(self, place, kept, come):
        self.place, self.kept, self.come, self.stage = place, kept, come, 0
        self.sent = kept

    def tie(self, *others):
        self.kept = after(self.kept, *others)

    def advance(self, other=None):
        self.stage += 1
        stage = self.stage
        if other is not None:
            half = self.kept.shape[0]
            self.kept, self.sent = run_kernel(
                halve_pair_kernel,
                [self.place, self.kept, self.come, *other],
                [shape_of((half, 256), BF16)] * 2,
                specs={0: SMEM},
            )
            self.come = exchange(self.sent, 1)
        elif stage < 4:
            self.kept, self.sent = halve(self.place, self.kept, self.come, stage)
            self.come = exchange(self.sent, stage)
        else:
            if stage == 4:
                self.kept = both(self.kept, self.come)
            else:
                self.kept = double(self.place, self.kept, self.come, 8 - stage)
            self.sent = self.kept
            self.come = exchange(self.sent, 7 - stage)

    @property
    def halves(self):
        return self.kept, self.come


def settle(chains, extras=()):
    flat = [item for chain in chains for item in chain.halves] + list(extras)
    flat = lax.optimization_barrier(tuple(flat))
    for number, chain in enumerate(chains):
        chain.kept, chain.come = flat[2 * number : 2 * number + 2]
    return list(flat[2 * len(chains) :])


def join_halves(place_ref, whole, mine, come):
    half = mine.shape[0]
    whole[pl.ds(pl.multiple_of(place_ref[COL] * half, half), half), :] = mine[...]
    whole[pl.ds(pl.multiple_of((1 - place_ref[COL]) * half, half), half), :] = come[...]


def unpack_att_kernel(place_ref, mine, come, qkv, proj, whole):
    join_halves(place_ref, whole, mine, come)
    for layer in range(2):
        for part in range(3):
            for half in range(2):
                start = 2 * HALF_ATT * half + HALF_ATT * layer
                first = 512 * part - HALF_ATT * half
                begin, end = max(first, 0), min(first + 512, HALF_ATT)
                if begin < end:
                    lines = slice(begin - first, end - first)
                    qkv[layer, lines, 256 * part : 256 * (part + 1)] = whole[
                        start + begin : start + end, :
                    ].astype(F32)
        for part in range(2):
            start = 2 * HALF_ATT + HALF_ATT * layer + ROWS_QKV - HALF_ATT + 256 * part
            proj[layer, :, 256 * part : 256 * (part + 1)] = whole[start : start + 256, :].astype(F32)


def unpack_mlp_kernel(place_ref, mine, come, *refs):
    fc1, fc2, whole = refs[-3:]
    join_halves(place_ref, whole, mine, come)
    for part in range(4):
        fc1[0, :, 256 * part : 256 * (part + 1)] = whole[512 * part : 512 * (part + 1), :].astype(F32)
    for part in range(2):
        start = 2048 + 1024 * part
        fc2[0, :, 256 * part : 256 * (part + 1)] = whole[start : start + 1024, :].astype(F32)


def unpack(kernel, place, halves, shapes, layer, before=()):
    outs = [shape_of(shape, F32) for shape in shapes]
    specs = {3 + number: pl.BlockSpec(memory_space=pl.ANY) for number in range(len(before))}
    return run_kernel(
        kernel,
        [place, *halves, *before],
        outs,
        [pltpu.VMEM((2 * halves[0].shape[0], 256), BF16)],
        specs={0: SMEM, **specs},
        out_specs=None if layer is None else [layer_spec(out, layer) for out in outs],
        aliases={3 + number: number for number in range(len(before))},
    )


def swap_head(value):
    return lax.ppermute(value, "head", [(0, 1), (1, 0)])


def fast_device(
    act_in, ln_gain, ln_bias, w_qkv, b_qv, rel_table, w_proj, b_proj, w_fc1, b_fc1, w_fc2, b_fc2, grad_out
):
    row_map, row_back, col_map, base, order, heads, token_row, token_col = constants()
    band = lax.axis_index("band")
    col = lax.axis_index("col")
    head = lax.axis_index("head")
    bands = lax.axis_size("band")
    cols = lax.axis_size("col")
    digit = [(band >> power) & 1 for power in range(3)]
    place = jnp.stack(
        [
            head,
            col,
            jnp.where(col == 0, digit[0], digit[1]),
            jnp.where(col == 0, digit[1], digit[2]),
            jnp.where(col == 0, digit[2], digit[0]),
        ]
    ).astype(jnp.int32)
    band_up = [(here, (here - 1) % bands) for here in range(bands)]
    band_down = [(here, (here + 1) % bands) for here in range(bands)]
    col_left = [(here, (here - 1) % cols) for here in range(cols)]
    edge_left = [(here * 2 + 1, (here - 1) % cols * 2 + 1) for here in range(cols)]
    edge_right = [(here * 2 + 1, (here + 1) % cols * 2 + 1) for here in range(cols)]
    gain = [[ln_gain[layer, which][None] for which in range(2)] for layer in range(2)]
    bias = [[ln_bias[layer, which][None] for which in range(2)] for layer in range(2)]
    row_proj = [b_proj[layer][None] for layer in range(2)]
    row_fc1 = [b_fc1[layer][None] for layer in range(2)]
    row_fc2 = [b_fc2[layer][None] for layer in range(2)]
    qv = b_qv.reshape(2, GROUP, 2, HEAD_DIM).transpose(0, 2, 1, 3).reshape(2, 2, SPAN)
    tables = jnp.pad(rel_table, ((0, 0), (0, ENTRIES - rel_table.shape[1]), (0, 0))).transpose(0, 2, 1)

    def edges(value, pairs):
        come = lax.ppermute(value, ("col", "head"), pairs)
        return run_kernel(edge_kernel, [place, value, come], [shape_of((QUAD, WIDTH), BF16)] * 2, specs={0: SMEM})

    def rows_bf(count, width=WIDTH):
        return shape_of((count, width), BF16)

    def rows_f32(count, width=WIDTH):
        return shape_of((count, width), F32)

    x_other = swap_head(act_in)
    pack1, pack1_half = pack_weights(place, w_qkv, w_proj, order, 1, (ROWS_ATT, HALF_ATT))
    pack1_mine = swap_head(pack1_half)
    (pack0,) = pack_weights(place, w_qkv, w_proj, order, 0, (ROWS_ATT,))
    off0 = bias_of(tables[0], base, row_map, col_map)
    whole, normed0, qkv0, probs0, context0, part0 = run_kernel(
        attention_plain_kernel,
        [place, act_in, x_other, gain[0][0], bias[0][0], pack0, qv[0], off0, heads],
        [
            rows_bf(PAIR), rows_bf(PAIR), rows_bf(PAIR, 768), rows_bf(4 * KEYS, TOK), rows_bf(PAIR, SPAN),
            rows_bf(PAIR),
        ],
        ATTEND_SCRATCH + (pltpu.VMEM((PAIR, WIDTH), F32),),
        specs={0: SMEM},
    )
    part0_other = swap_head(part0)

    small1 = jnp.concatenate([tables[1], jnp.pad(qv[1], ((0, 6), (0, ENTRIES - SPAN)))], axis=0)
    small1_other = swap_head(after(small1, part0))
    off1 = bias_of(after(tables[1], part0), base, row_map, col_map)
    grad_own = enter_units(after(grad_out, part0))
    pack1_mine = after(pack1_mine, part0)
    pack1_theirs = lax.ppermute(pack1_mine, "col", [(0, 1), (1, 0)])
    grad_other = swap_head(after(grad_own, part0_other))

    middle0, second0, active0, slope0, x1_keep, x1_send = run_kernel(
        mlp_plain_kernel,
        [
            place, whole, part0, part0_other, row_proj[0], gain[0][1], bias[0][1], w_fc1, row_fc1[0], w_fc2,
            row_fc2[0],
        ],
        [rows_f32(PAIR), rows_bf(PAIR), rows_bf(PAIR, 1024), rows_bf(PAIR, 1024), rows_f32(TILE), rows_bf(TILE)],
        [pltpu.VMEM((PAIR, WIDTH), F32)],
        specs={0: SMEM, 7: layer_spec(w_fc1, 0), 9: layer_spec(w_fc2, 0)},
    )
    x1_come = swap_head(x1_send)
    off1_other = bias_of(after(small1_other[:GROUP], x1_send), base, row_map, col_map)
    qv1_other = small1_other[GROUP : GROUP + 2, :SPAN]
    (pack1_other,) = run_kernel(
        pack_join_kernel, [place, after(pack1_mine, x1_send), pack1_theirs], [rows_bf(ROWS_ATT, 256)], specs={0: SMEM}
    )
    grad_send, grad_stay = run_kernel(
        grad_join_kernel,
        [place, after(grad_own, x1_send), grad_other],
        [rows_bf(8 * QUAD)] * 2,
        [pltpu.VMEM((PAIR, WIDTH), BF16)],
        specs={0: SMEM},
    )

    stay_main, send_main, edge = run_kernel(
        enter_entry_kernel,
        [x1_keep, x1_come],
        [rows_bf(3 * QUAD), rows_bf(3 * QUAD), rows_bf(UNIT)],
        [pltpu.VMEM((TILE, WIDTH), F32)],
    )
    come_main = lax.ppermute(send_main, "band", band_up)
    send_edge, stay_edge = edges(edge, edge_left)
    come_edge = lax.ppermute(send_edge, "band", band_up)
    grad_come = lax.ppermute(after(grad_send, send_edge), "band", band_up)

    rows_id = region_ids(WIN * band + jnp.asarray(token_row), WIN * bands)
    cols_id = region_ids(
        2 * WIN * (2 * col + head) + WIN * jnp.arange(2, dtype=jnp.int32)[:, None] + jnp.asarray(token_col)[None],
        4 * WIN * cols,
    )
    ids = (3 * rows_id[None] + cols_id).astype(F32)
    x1, normed1, qkv1a, qkv1b, probs1a, probs1b, context1a, context1b, middle1, second1_own = run_kernel(
        attention_shifted_kernel,
        [
            stay_main, come_main, stay_edge, come_edge, gain[1][0], bias[1][0], gain[1][1], bias[1][1], pack1,
            pack1_other, qv[1], qv1_other, off1, off1_other, ids.reshape(TILE, 1), ids.reshape(2, 1, TOK), heads,
            row_proj[1],
        ],
        [
            rows_bf(TILE), rows_bf(TILE), rows_bf(TILE, 768), rows_bf(TILE, 768), rows_bf(2 * KEYS, TOK),
            rows_bf(2 * KEYS, TOK), rows_bf(TILE, SPAN), rows_bf(TILE, SPAN), rows_f32(TILE), rows_bf(TILE),
        ],
        ATTEND_SCRATCH,
    )
    second1_other = swap_head(second1_own)
    grad_far = jnp.concatenate([after(grad_stay, second1_own)[:QUAD], grad_come[:QUAD]], axis=0)
    grad_far = lax.ppermute(grad_far, "col", col_left)
    second1, grad_all, active1, inner1, x2_keep, x2_send, back1_keep, back1_send, small_mlp1 = run_kernel(
        mlp_shifted_kernel,
        [place, second1_own, second1_other, grad_stay, grad_come, grad_far, w_fc1, row_fc1[1], w_fc2],
        [
            rows_bf(PAIR), rows_bf(PAIR), rows_bf(PAIR, 1024), rows_bf(PAIR, 1024), rows_f32(TILE), rows_bf(TILE),
            rows_f32(TILE), rows_bf(TILE), rows_f32(8, 256),
        ],
        [pltpu.VMEM((PAIR, 1024), BF16)],
        specs={0: SMEM, 6: layer_spec(w_fc1, 1), 8: layer_spec(w_fc2, 1)},
    )
    back1_other = swap_head(back1_send)
    mlp1_keep, mlp1_send = mlp_weights(place, second1, active1, grad_all, inner1)
    mlp1 = PageSum(place, mlp1_keep, exchange(mlp1_send, 0))
    mlp1.advance()
    back1_keep = after(back1_keep, mlp1.sent)
    grad_low1, mixed1a, mixed1b, total1a, total1b, stay_main, send_main, edge, small_att1 = run_kernel(
        attention_shifted_back_kernel,
        [
            place, grad_all, back1_keep, back1_other, middle1, x1, gain[1][0], gain[1][1], qkv1a, qkv1b, probs1a,
            probs1b, pack1, pack1_other, heads,
        ],
        [
            rows_bf(TILE), rows_bf(TILE, 768), rows_bf(TILE, 768), rows_f32(TOK, KEYS), rows_f32(TOK, KEYS),
            rows_bf(3 * QUAD), rows_bf(3 * QUAD), rows_bf(UNIT), rows_f32(24, 256),
        ],
        ATTEND_SCRATCH
        + (pltpu.VMEM((KEYS, TOK), BF16), pltpu.VMEM((TILE, SPAN), BF16), pltpu.VMEM((TILE, WIDTH), F32)),
        specs={0: SMEM},
    )

    come_main = lax.ppermute(send_main, "band", band_down)
    stay_edge, send_edge = edges(edge, edge_right)
    come_edge = lax.ppermute(send_edge, "band", band_down)
    stay_main_other = swap_head(stay_main)
    edge_own = jnp.concatenate([come_edge, stay_edge], axis=0)
    come_main_other = swap_head(come_main)
    edge_other = swap_head(edge_own)
    mlp1.tie(edge)
    mlp1.advance()
    att1_keep, att1_send = run_kernel(
        attention_weights_shifted_kernel,
        [place, after(normed1, mlp1.sent), mixed1a, mixed1b, context1a, context1b, grad_low1, order],
        [rows_bf(ROWS_ATT, 256)] * 2,
        [pltpu.VMEM((2 * ROWS_ATT, 256), BF16)],
        specs={0: SMEM},
    )
    att1_come = exchange(att1_send, 0)
    slope0 = after(slope0, att1_send)
    grad0, inner0, back0 = run_kernel(
        mlp_plain_back_kernel,
        [
            place, stay_main, stay_main_other, come_main, come_main_other, edge_own, edge_other, slope0, w_fc1,
            w_fc2,
        ],
        [rows_bf(PAIR), rows_bf(PAIR, 1024), rows_bf(PAIR)],
        [pltpu.VMEM((PAIR, WIDTH), BF16)],
        specs={0: SMEM, 8: layer_spec(w_fc1, 0), 9: layer_spec(w_fc2, 0)},
    )
    back0_other = swap_head(back0)
    mlp1.tie(back0)
    mlp1.advance()
    mlp0_keep, mlp0_send = mlp_weights(place, after(second0, mlp1.sent), active0, grad0, inner0)
    mlp0 = PageSum(place, mlp0_keep, exchange(mlp0_send, 0))
    mlp1.tie(mlp0_send)
    mlp1.advance()
    mlp0.tie(mlp1.sent)
    mlp0.advance()
    att1_keep, att1_send = run_kernel(
        across_kernel, [after(att1_keep, back0_other, mlp0.sent), att1_come], [rows_bf(HALF_ATT, 256)] * 2
    )
    att1_come = swap_head(att1_send)
    back0 = after(back0, att1_send)
    grad_low0, mixed0, total0, first_keep, first_send, kept0, small_att0 = run_kernel(
        attention_plain_back_kernel,
        [
            place, grad0, back0, back0_other, middle0, whole, gain[0][0], gain[0][1], qkv0, probs0, pack0, heads,
            inner0,
        ],
        [
            rows_bf(PAIR), rows_bf(PAIR, 768), rows_f32(TOK, KEYS), rows_f32(TILE), rows_bf(TILE), rows_f32(TILE),
            rows_f32(24, 256),
        ],
        ATTEND_SCRATCH
        + (pltpu.VMEM((KEYS, TOK), BF16), pltpu.VMEM((PAIR, SPAN), BF16), pltpu.VMEM((PAIR, WIDTH), F32)),
        specs={0: SMEM},
    )
    att0_keep, att0_send = run_kernel(
        attention_weights_plain_kernel,
        [place, normed0, mixed0, context0, grad_low0, order],
        [rows_bf(HALF_ATT, 256)] * 2,
        [pltpu.VMEM((ROWS_ATT, 256), BF16)],
        specs={0: SMEM},
    )
    att = PageSum(place, att0_keep, exchange(att0_send, 0))
    mlp1.tie(att0_send)
    mlp1.advance()
    mlp0.tie(mlp1.sent)
    mlp0.advance()
    first_other = swap_head(first_send)
    table0 = table_of(after(total0, mlp0.sent), base, row_back, col_map)
    table1 = table_of(after(total1a, mlp0.sent), base, row_back, col_map)
    table1_send = table_of(after(total1b, mlp0.sent), base, row_back, col_map)
    shared = jnp.concatenate([small_att0[:12], small_att1[:12]], axis=0)
    come = swap_head(jnp.concatenate([shared, small_att1[16:24], table1_send], axis=0))

    att1_keep, att1_come, first_other, come, x2_send = settle(
        (att, mlp0, mlp1), (att1_keep, att1_come, first_other, come, x2_send)
    )
    att.advance((att1_keep, att1_come))
    mlp0.advance()
    mlp1.advance()
    x2_come = swap_head(x2_send)
    grad_in = run_kernel(
        last_kernel,
        [place, whole, gain[0][0], first_keep, first_other, kept0],
        [shape_of((WIN, 2 * WIN, WIDTH), F32)],
        [pltpu.VMEM((TILE, WIDTH), F32)],
        specs={0: SMEM},
    )[0]
    sums = jnp.concatenate(
        [
            shared + come[:24],
            small_att1[12:16] + come[24:28],
            small_att0[12:20],
            small_mlp1[:4],
            table0,
            table1 + come[32:48],
        ],
        axis=0,
    )

    def add_over(value, pairs):
        return value, lax.ppermute(value, ("band", "col"), pairs)

    sums, sums_come = add_over(sums, STEP_PAIRS[0])
    x2_come, sums, sums_come = settle((att, mlp0, mlp1), (x2_come, sums, sums_come))
    att.advance()
    mlp0.advance()
    mlp1.advance()
    x2_move, x2_stay = run_kernel(
        last_entry_kernel,
        [x2_keep, x2_come, middle1, row_fc2[1]],
        [rows_bf(4 * QUAD)] * 2,
        [pltpu.VMEM((TILE, WIDTH), F32)],
    )
    x2_come = lax.ppermute(x2_move, "band", band_down)
    sums, sums_come = add_over(sums + sums_come, band_pairs(1, 1))
    x2_come, sums, sums_come = settle((att, mlp0, mlp1), (x2_come, sums, sums_come))
    att.advance()
    mlp0.advance()
    tall_shapes = [(2, 512, 1024), (2, 1024, 512)]
    tall = unpack(unpack_mlp_kernel, place, mlp1.halves, tall_shapes, 1)
    x2_edge = jnp.concatenate([x2_come[3 * QUAD :], x2_stay[3 * QUAD :]], axis=0)
    x2_far = lax.ppermute(x2_edge, ("col", "head"), edge_right)
    sums, sums_come = add_over(sums + sums_come, band_pairs(2, 2))
    x2_far, sums, sums_come = settle((att, mlp0), (x2_far, sums, sums_come))
    att.advance()
    mlp0.advance()
    x2_edge = swap_head(jnp.where(head == 1, x2_far, x2_edge))
    sums, sums_come = add_over(sums + sums_come, band_pairs(4, 4))
    x2_edge, sums, sums_come = settle((att, mlp0), (x2_edge, sums, sums_come))
    att.advance()
    mlp0.advance()
    sums = sums + sums_come
    act_out = run_kernel(
        leave_kernel,
        [x2_edge, x2_stay, x2_come],
        [shape_of((WIN, 2 * WIN, WIDTH), F32)],
        [pltpu.VMEM((TILE, WIDTH), F32)],
    )[0]
    settle((att, mlp0))
    att.advance()
    g_fc1, g_fc2 = unpack(unpack_mlp_kernel, place, mlp0.halves, tall_shapes, 0, tall)
    settle((att,))
    att.advance()
    g_qkv, g_proj = unpack(unpack_att_kernel, place, att.halves, [(2, 512, 768), (2, 256, 512)], None)

    def row_at(start, count):
        return sums[start : start + count].reshape(-1)

    g_gain = jnp.stack([row_at(8, 2), row_at(0, 2), row_at(20, 2), row_at(12, 2)]).reshape(2, 2, WIDTH)
    g_bias = jnp.stack([row_at(10, 2), row_at(2, 2), row_at(22, 2), row_at(14, 2)]).reshape(2, 2, WIDTH)
    g_bfc2 = jnp.stack([row_at(4, 2), row_at(16, 2)])
    g_bproj = jnp.stack([row_at(6, 2), row_at(18, 2)])
    g_qv = jnp.stack([sums[28:31], sums[24:27]])[:, ::2].reshape(2, 2, GROUP, HEAD_DIM)
    g_qv = g_qv.transpose(0, 2, 1, 3).reshape(2, 2 * SPAN)
    g_bfc1 = jnp.stack([row_at(32, 4), row_at(36, 4)])

    def table_rows(start):
        full = jnp.concatenate([sums[start : start + GROUP], sums[start + GROUP : start + 2 * GROUP]], axis=1)
        return full[:, : rel_table.shape[1]].T

    g_table = jnp.stack([table_rows(40), table_rows(56)])

    return (
        act_out, grad_in, g_gain, g_bias, g_qkv, g_qv, g_table, g_proj, g_bproj, g_fc1, g_bfc1, g_fc2, g_bfc2,
    )


def fits(mesh):
    return dict(mesh.shape) == {"band": 8, "col": 2, "head": 2}


def solution(mesh):
    placed = (
        P("band", ("col", "head"), None),
        P(),
        P(),
        P(None, None, "head"),
        P(None, "head"),
        P(None, None, "head"),
        P(None, "head", None),
        P(),
        P(None, None, "head"),
        P(None, "head"),
        P(None, "head", None),
        P(),
        P("band", ("col", "head"), None),
    )
    return jax.shard_map(
        fast_device if fits(mesh) else on_device,
        mesh=mesh,
        in_specs=placed,
        out_specs=(
            P("band", ("col", "head"), None),
            P("band", ("col", "head"), None),
            P(),
            P(),
            P(None, None, "head"),
            P(None, "head"),
            P(None, None, "head"),
            P(None, "head", None),
            P(),
            P(None, None, "head"),
            P(None, "head"),
            P(None, "head", None),
            P(),
        ),
        check_vma=False,
    )
```

```python
from functools import partial

import jax
import jax.numpy as jnp
import numpy as np
from jax import lax
from jax.experimental import pallas as pl
from jax.experimental.pallas import tpu as pltpu
from jax.sharding import PartitionSpec as P

HEAD_DIM = 32
WIN = 10
SHIFT = 5
BLOCKS = 2


EPSILON = 1e-05
HIGHEST = lax.Precision.HIGHEST


def shifted_2(value, axis, steps):
    count = lax.axis_size(axis)
    pairs = [(source, (source + steps) % count) for source in range(count)]
    return lax.ppermute(value, axis, pairs)


def layer_norm(array, gain_row, bias_row):
    centre = array - jnp.mean(array, axis=-1, keepdims=True)
    spread = jnp.mean(centre * centre, axis=-1, keepdims=True)
    return centre * lax.rsqrt(spread + EPSILON) * gain_row + bias_row


def offsets(window):
    places = jnp.arange(window, dtype=jnp.int32)
    spread = jnp.arange(2 * window - 1, dtype=jnp.int32)
    return (
        spread[None, None, :] == places[:, None, None] - places[None, :, None] + window - 1
    ).astype(jnp.float32)


def position_bias(table):
    head_count = table.shape[-1]
    table_grid = table.reshape(2 * WIN - 1, 2 * WIN - 1, head_count)
    onehot = offsets(WIN)
    full = jnp.einsum("ika,jlb,abh->hijkl", onehot, onehot, table_grid, precision=HIGHEST)
    return full.reshape(head_count, WIN * WIN, WIN * WIN)


def table_grad(grad_offset):
    head_count = grad_offset.shape[0]
    onehot = offsets(WIN)
    spread = grad_offset.reshape(head_count, WIN, WIN, WIN, WIN)
    full = jnp.einsum("ika,jlb,hijkl->abh", onehot, onehot, spread, precision=HIGHEST)
    return full.reshape((2 * WIN - 1) * (2 * WIN - 1), head_count)


def gather_tile(array):
    return lax.all_gather(array, "head", axis=1, tiled=True)


def sum_tile(array):
    return lax.psum_scatter(
        array.astype(jnp.bfloat16), "head", scatter_dimension=1, tiled=True
    ).astype(jnp.float32)


def gather_grad(array):
    return lax.all_gather(array, "head", axis=1, tiled=True)


def sum_grad(array):
    return lax.psum_scatter(
        array.astype(jnp.bfloat16), "head", scatter_dimension=1, tiled=True
    ).astype(jnp.float32)


def roll_ahead(array):
    upper = shifted_2(array[:SHIFT], "band", -1)
    array = jnp.concatenate([array[SHIFT:], upper], axis=0)
    leftmost = shifted_2(array[:, :SHIFT], ("col", "head"), -1)
    return jnp.concatenate([array[:, SHIFT:], leftmost], axis=1)


def roll_behind(array):
    lower = shifted_2(array[-SHIFT:], "band", 1)
    array = jnp.concatenate([lower, array[:-SHIFT]], axis=0)
    rightmost = shifted_2(array[:, -SHIFT:], ("col", "head"), 1)
    return jnp.concatenate([rightmost, array[:, :-SHIFT]], axis=1)


def pack_members(members):
    group = lax.axis_size("band") * lax.axis_size("col")
    flat = jnp.concatenate([member.reshape(-1) for member in members])
    padding = -flat.shape[0] % group
    return jnp.concatenate([flat, jnp.zeros((padding,), jnp.float32)])


def unpack_members(flat, members):
    result = []
    start = 0
    for member in members:
        count = member.size
        result.append(flat[start : start + count].reshape(member.shape))
        start = start + count
    return tuple(result)


def to_windows(tile_rows):
    height, breadth, depth = tile_rows.shape
    window_count = breadth // height
    split = tile_rows.reshape(height, window_count, height, depth).transpose(1, 0, 2, 3)
    return split.reshape(window_count * height * height, depth)


def from_windows(flat_rows, height):
    window_count = flat_rows.shape[0] // (height * height)
    depth = flat_rows.shape[1]
    split = flat_rows.reshape(window_count, height, height, depth).transpose(1, 0, 2, 3)
    return split.reshape(height, window_count * height, depth)


def region_ids(places, extent):
    return (places >= extent - WIN).astype(jnp.int32) + (places >= extent - SHIFT).astype(jnp.int32)


def shift_mask(breadth):
    rows_all = WIN * lax.axis_size("band")
    cols_all = breadth * lax.axis_size("col")
    rows_here = WIN * lax.axis_index("band") + jnp.arange(WIN, dtype=jnp.int32)
    cols_here = breadth * lax.axis_index("col") + jnp.arange(breadth, dtype=jnp.int32)
    region = 3 * region_ids(rows_here, rows_all)[:, None] + region_ids(cols_here, cols_all)[None, :]
    window_count = breadth // WIN
    labels = to_windows(region[:, :, None])[:, 0].reshape(window_count, WIN * WIN)
    return jnp.where(labels[:, :, None] != labels[:, None, :], -100.0, 0.0).astype(jnp.float32)


def scores(queries, key_rows, offset, region_mask):
    logits = jnp.einsum("wqhd,wkhd->whqk", queries, key_rows, preferred_element_type=jnp.float32)
    logits = logits * HEAD_DIM ** (-0.5) + offset[None]
    if region_mask is not None:
        logits = logits + region_mask[:, None]
    return logits


def forward_block(source, weights, shifted):
    norm_gain, norm_bias, w_qkv, b_qv, table, w_proj, b_proj, w_fc1, b_fc1, w_fc2, b_fc2 = weights
    height = source.shape[0]
    heads_here = table.shape[-1]
    normed = layer_norm(source, norm_gain[0], norm_bias[0]).astype(jnp.bfloat16)
    if shifted:
        normed = roll_ahead(normed)
    gathered = gather_tile(normed)
    window_count = gathered.shape[1] // height
    flat_rows = to_windows(gathered)
    projected = jnp.dot(flat_rows, w_qkv, preferred_element_type=jnp.float32)
    projected = projected.reshape(window_count, height * height, heads_here, 3, HEAD_DIM)
    qv_bias = b_qv.reshape(heads_here, 2, HEAD_DIM)
    queries = (projected[..., 0, :] + qv_bias[:, 0]).astype(jnp.bfloat16)
    key_rows = projected[..., 1, :].astype(jnp.bfloat16)
    values = (projected[..., 2, :] + qv_bias[:, 1]).astype(jnp.bfloat16)
    offset = position_bias(table)
    region_mask = shift_mask(gathered.shape[1]) if shifted else None
    logits = scores(queries, key_rows, offset, region_mask)
    log_total = jax.nn.logsumexp(logits, axis=-1)
    probs_low = jnp.exp(logits - log_total[..., None]).astype(jnp.bfloat16)
    context = jnp.einsum("whqk,wkhd->wqhd", probs_low, values, preferred_element_type=jnp.float32)
    context = context.astype(jnp.bfloat16).reshape(
        window_count * height * height, heads_here * HEAD_DIM
    )
    partial_out = from_windows(jnp.dot(context, w_proj, preferred_element_type=jnp.float32), height)
    branch = sum_tile(partial_out) + b_proj
    if shifted:
        branch = roll_behind(branch.astype(jnp.bfloat16)).astype(jnp.float32)
    middle = source + branch
    second = layer_norm(middle, norm_gain[1], norm_bias[1]).astype(jnp.bfloat16)
    second_tile = gather_tile(second)
    mlp_rows = second_tile.reshape(-1, second_tile.shape[-1])
    hidden = jnp.dot(mlp_rows, w_fc1, preferred_element_type=jnp.float32) + b_fc1
    active = jax.nn.gelu(hidden, approximate=False).astype(jnp.bfloat16)
    out_part = jnp.dot(active, w_fc2, preferred_element_type=jnp.float32).reshape(second_tile.shape)
    result = middle + sum_tile(out_part) + b_fc2
    saved_state = (
        source,
        middle,
        flat_rows,
        queries,
        key_rows,
        values,
        log_total,
        context,
        mlp_rows,
        hidden,
        offset,
        region_mask,
    )
    return (result, saved_state)


def backward_block(upstream, weights, saved_state, shifted):
    norm_gain, norm_bias, w_qkv, b_qv, table, w_proj, b_proj, w_fc1, b_fc1, w_fc2, b_fc2 = weights
    (
        source,
        middle,
        flat_rows,
        queries,
        key_rows,
        values,
        log_total,
        context,
        mlp_rows,
        hidden,
        offset,
        region_mask,
    ) = saved_state
    height = source.shape[0]
    window_count, window_len, heads_here, _ = queries.shape
    grad_low = upstream.astype(jnp.bfloat16)
    grad_tile = gather_grad(grad_low)
    grad_rows = grad_tile.reshape(-1, grad_tile.shape[-1])
    active = jax.nn.gelu(hidden, approximate=False).astype(jnp.bfloat16)
    g_fc2 = jnp.dot(active.T, grad_rows, preferred_element_type=jnp.float32)
    g_bfc2 = jnp.sum(grad_low.astype(jnp.float32), axis=(0, 1))
    g_active = jnp.dot(grad_rows, w_fc2.T, preferred_element_type=jnp.float32)
    g_hidden = jax.vjp(partial(jax.nn.gelu, approximate=False), hidden)[1](g_active)[0].astype(
        jnp.bfloat16
    )
    g_bfc1 = jnp.sum(g_hidden.astype(jnp.float32), axis=0)
    g_fc1 = jnp.dot(mlp_rows.T, g_hidden, preferred_element_type=jnp.float32)
    g_second = sum_grad(
        jnp.dot(g_hidden, w_fc1.T, preferred_element_type=jnp.float32).reshape(grad_tile.shape)
    )
    pull_second = jax.vjp(layer_norm, middle, norm_gain[1], norm_bias[1])[1]
    g_mid_norm, g_gain2, g_bias2 = pull_second(g_second)
    g_middle = upstream + g_mid_norm
    g_branch = g_middle.astype(jnp.bfloat16)
    if shifted:
        g_branch = roll_ahead(g_branch)
    g_bproj = jnp.sum(g_branch.astype(jnp.float32), axis=(0, 1))
    g_output = to_windows(gather_grad(g_branch))
    g_proj = jnp.dot(context.T, g_output, preferred_element_type=jnp.float32)
    g_context = jnp.dot(g_output, w_proj.T, preferred_element_type=jnp.float32).astype(jnp.bfloat16)
    g_context = g_context.reshape(window_count, window_len, heads_here, HEAD_DIM)
    logits = scores(queries, key_rows, offset, region_mask)
    probs = jnp.exp(logits - log_total[..., None])
    probs_low = probs.astype(jnp.bfloat16)
    g_values = jnp.einsum(
        "whqk,wqhd->wkhd", probs_low, g_context, preferred_element_type=jnp.float32
    ).astype(jnp.bfloat16)
    g_probs = jnp.einsum("wqhd,wkhd->whqk", g_context, values, preferred_element_type=jnp.float32)
    centre = jnp.sum(probs * g_probs, axis=-1, keepdims=True)
    g_logits = (probs * (g_probs - centre)).astype(jnp.bfloat16)
    g_table = table_grad(jnp.sum(g_logits.astype(jnp.float32), axis=0))
    inv_root = HEAD_DIM ** (-0.5)
    g_queries = (
        jnp.einsum("whqk,wkhd->wqhd", g_logits, key_rows, preferred_element_type=jnp.float32)
        * inv_root
    ).astype(jnp.bfloat16)
    g_keys = (
        jnp.einsum("whqk,wqhd->wkhd", g_logits, queries, preferred_element_type=jnp.float32)
        * inv_root
    ).astype(jnp.bfloat16)
    g_mixed = jnp.stack([g_queries, g_keys, g_values], axis=3).reshape(
        window_count * window_len, heads_here * 3 * HEAD_DIM
    )
    g_bqv = jnp.stack(
        [
            jnp.sum(g_queries.astype(jnp.float32), axis=(0, 1)),
            jnp.sum(g_values.astype(jnp.float32), axis=(0, 1)),
        ],
        axis=1,
    ).reshape(-1)
    g_qkv = jnp.dot(flat_rows.T, g_mixed, preferred_element_type=jnp.float32)
    g_first = sum_grad(
        from_windows(jnp.dot(g_mixed, w_qkv.T, preferred_element_type=jnp.float32), height)
    )
    if shifted:
        g_first = roll_behind(g_first.astype(jnp.bfloat16)).astype(jnp.float32)
    pull_first = jax.vjp(layer_norm, source, norm_gain[0], norm_bias[0])[1]
    g_source, g_gain1, g_bias1 = pull_first(g_first)
    g_input = g_middle + g_source
    sharded = (g_qkv, g_bqv, g_table, g_proj, g_fc1, g_bfc1, g_fc2)
    shared = (jnp.stack([g_gain1, g_gain2]), jnp.stack([g_bias1, g_bias2]), g_bproj, g_bfc2)
    return (g_input, sharded, shared)


def on_device(
    act_in,
    ln_gain,
    ln_bias,
    w_qkv,
    b_qv,
    rel_table,
    w_proj,
    b_proj,
    w_fc1,
    b_fc1,
    w_fc2,
    b_fc2,
    grad_out,
):
    params = (ln_gain, ln_bias, w_qkv, b_qv, rel_table, w_proj, b_proj, w_fc1, b_fc1, w_fc2, b_fc2)
    layers = [tuple((member[block_id] for member in params)) for block_id in range(BLOCKS)]
    residual = act_in.astype(jnp.float32)
    layer_inputs = []
    stored = []
    for block_id in range(BLOCKS):
        layer_inputs.append(residual)
        residual, saved_state = forward_block(residual, layers[block_id], block_id % 2 == 1)
        stored.append(saved_state)
    upstream = grad_out
    sharded_all = [None] * BLOCKS
    shared_all = [None] * BLOCKS
    for block_id in reversed(range(BLOCKS)):
        saved_state = forward_block(layer_inputs[block_id], layers[block_id], block_id % 2 == 1)[1]
        upstream, sharded, shared = backward_block(
            upstream, layers[block_id], saved_state, block_id % 2 == 1
        )
        sharded_all[block_id] = sharded
        shared_all[block_id] = shared
    sharded_stack = tuple(
        (jnp.stack([entry[member] for entry in sharded_all]) for member in range(7))
    )
    shared_stack = tuple(
        (jnp.stack([entry[member] for entry in shared_all]) for member in range(4))
    )
    packed_all = pack_members(sharded_stack)
    packed_part = lax.psum_scatter(
        packed_all.astype(jnp.bfloat16), ("band", "col"), scatter_dimension=0, tiled=True
    ).astype(jnp.float32)
    packed_all = lax.all_gather(
        packed_part.astype(jnp.bfloat16), ("band", "col"), axis=0, tiled=True
    ).astype(packed_part.dtype)
    sharded_stack = unpack_members(packed_all, sharded_stack)
    shared_stack = lax.psum(shared_stack, ("band", "col", "head"))
    return (
        residual,
        upstream,
        shared_stack[0],
        shared_stack[1],
        sharded_stack[0],
        sharded_stack[1],
        sharded_stack[2],
        sharded_stack[3],
        shared_stack[2],
        sharded_stack[4],
        sharded_stack[5],
        sharded_stack[6],
        shared_stack[3],
    )


F32 = jnp.float32
BF16 = jnp.bfloat16
WIDTH = 512
QUAD = 32
LIVE = SHIFT * SHIFT
UNIT = 2 * QUAD
TOK = 2 * UNIT
TILE = 4 * UNIT
PAIR = 2 * TILE
GROUP = 8
SPAN = GROUP * HEAD_DIM
KEYS = GROUP * TOK
OFFSETS = 2 * WIN - 1
ENTRIES = 384
SCALE = HEAD_DIM ** (-0.5)
FAR = -1e30
ROOT_HALF = 0.5 ** 0.5
ROOT_TWO_PI = (2.0 * np.pi) ** (-0.5)
VMEM = pl.BlockSpec(memory_space=pltpu.VMEM)
SMEM = pl.BlockSpec(memory_space=pltpu.SMEM)
ROWS_QKV = 3 * 512
ROWS_ATT = ROWS_QKV + 512
ROWS_MLP = 4096
HALF_ATT = ROWS_ATT // 2
HEAD, COL, NEAR = 0, 1, 5
QUARTER_ATT = HALF_ATT // 2
EIGHTH = HALF_ATT // 8


def shape_of(shape, kind):
    return jax.ShapeDtypeStruct(shape, kind)


def layer_spec(array, layer):
    rest = array.shape[1:]
    return pl.BlockSpec((1,) + rest, lambda _: (layer,) + (0,) * len(rest), pipeline_mode=pl.Buffered(1))


COSTS = {
    "attention_plain_kernel": 6.0,
    "mlp_plain_kernel": 4.5,
    "attention_shifted_kernel": 5.5,
    "mlp_shifted_kernel": 5.0,
    "attention_shifted_back_kernel": 6.0,
    "mlp_plain_back_kernel": 2.0,
    "attention_plain_back_kernel": 6.0,
    "mlp_weights_kernel": 2.0,
    "attention_weights_plain_kernel": 2.0,
    "attention_weights_shifted_kernel": 2.7,
    "table_kernel": 1.2,
    "bias_body": 1.2,
    "pack_kernel": 1.5,
    "unpack_mlp_kernel": 3.0,
    "unpack_layer_kernel": 5.0,
    "unpack_last_kernel": 2.5,
}


def run_kernel(kernel, operands, outs, scratch=(), limit=24, specs=None, aliases=None, out_specs=None):
    specs = specs or {}
    name = getattr(kernel, "func", kernel).__name__
    in_specs = [specs.get(place, VMEM) for place in range(len(operands))]
    return pl.pallas_call(
        kernel,
        grid=(1,),
        in_specs=in_specs,
        out_specs=out_specs or [VMEM] * len(outs),
        out_shape=list(outs),
        scratch_shapes=list(scratch),
        input_output_aliases=aliases or {},
        cost_estimate=pl.CostEstimate(
            flops=int(COSTS.get(name, 0.7) * 4.6e9), bytes_accessed=1 << 10, transcendentals=0
        ),
        compiler_params=pltpu.CompilerParams(vmem_limit_bytes=limit << 20),
        name=name,
    )(*operands)


def mm(left, right):
    return lax.dot_general(left, right, (((1,), (0,)), ((), ())), preferred_element_type=F32)


def mm_nt(left, right):
    return lax.dot_general(left, right, (((1,), (1,)), ((), ())), preferred_element_type=F32)


def mm_tn(left, right):
    return lax.dot_general(left, right, (((0,), (0,)), ((), ())), preferred_element_type=F32)


def halves_of(value):
    high = value.astype(BF16)
    return high, (value - high.astype(F32)).astype(BF16)


def norm_parts(value):
    centre = value - jnp.mean(value, axis=-1, keepdims=True)
    inverse = lax.rsqrt(jnp.mean(centre * centre, axis=-1, keepdims=True) + EPSILON)
    return centre * inverse, inverse


def norm_back(grad, gain, unit, inverse):
    scaled = grad * gain
    return (
        scaled
        - jnp.mean(scaled, axis=-1, keepdims=True)
        - unit * jnp.mean(scaled * unit, axis=-1, keepdims=True)
    ) * inverse


def column_sum(value):
    return jnp.sum(value, axis=0, keepdims=True)


def put_row(ref, row, value):
    for part in range(value.shape[1] // 256):
        ref[row + part : row + part + 1, :] = value[:, 256 * part : 256 * (part + 1)]


def token_place(row, col):
    return ((col // SHIFT) * 2 + row // SHIFT) * QUAD + (row % SHIFT) * SHIFT + col % SHIFT


def constants():
    row_map = np.zeros((TOK, 160), np.float32)
    col_map = np.zeros((TOK, TOK), np.float32)
    token_row = np.zeros((TOK,), np.int32)
    token_col = np.zeros((TOK,), np.int32)
    for row in range(WIN):
        for col in range(WIN):
            place = token_place(row, col)
            row_map[place, row * 16 + col] = 1.0
            col_map[row * WIN + col, place] = 1.0
            token_row[place] = row
            token_col[place] = col
    base = np.full((1, 256), -4000, np.int32)
    for lane in range(OFFSETS * WIN):
        base[0, lane] = (OFFSETS - 1 - lane // WIN) * OFFSETS - lane % WIN + WIN - 1
    order = np.zeros((768, 768), np.float32)
    for head in range(GROUP):
        for part in range(3):
            for place in range(HEAD_DIM):
                order[head * 96 + part * 32 + place, part * SPAN + head * HEAD_DIM + place] = 1.0
    heads = np.zeros((KEYS, SPAN), np.float32)
    for head in range(GROUP):
        heads[head * TOK : (head + 1) * TOK, head * HEAD_DIM : (head + 1) * HEAD_DIM] = 1.0
    order_qv = np.zeros((2 * SPAN, 2 * SPAN), np.float32)
    for head in range(GROUP):
        for part in range(2):
            for place in range(HEAD_DIM):
                order_qv[part * SPAN + head * HEAD_DIM + place, (2 * head + part) * HEAD_DIM + place] = 1.0
    return (
        jnp.asarray(row_map, BF16),
        jnp.asarray(row_map.T, BF16),
        jnp.asarray(col_map, BF16),
        jnp.asarray(base),
        jnp.asarray(order, BF16),
        jnp.asarray(heads, BF16),
        jnp.asarray(order_qv, BF16),
        token_row,
        token_col,
    )


def enter_rows(in_ref, buf, start):
    for row in range(WIN):
        line = in_ref[row].astype(F32)
        for unit in range(4):
            first = unit * UNIT + (row // SHIFT) * QUAD + (row % SHIFT) * SHIFT
            buf[start + first : start + first + SHIFT, :] = line[unit * SHIFT : (unit + 1) * SHIFT, :]


def enter_kernel(in_ref, out_ref, buf):
    buf[...] = jnp.zeros(buf.shape, F32)
    enter_rows(in_ref, buf, 0)
    out_ref[...] = buf[...].astype(BF16)


def enter_units(tile):
    return run_kernel(
        enter_kernel, [tile], [shape_of((TILE, WIDTH), BF16)], [pltpu.VMEM((TILE, WIDTH), F32)]
    )[0]


def leave_rows(value_ref, out_ref):
    for row in range(WIN):
        for unit in range(4):
            start = unit * UNIT + (row // SHIFT) * QUAD + (row % SHIFT) * SHIFT
            out_ref[row, unit * SHIFT : (unit + 1) * SHIFT, :] = value_ref[start : start + SHIFT, :]


def leave_kernel(first, stay, come, out_ref, buf):
    buf[0:UNIT, :] = first[TILE:, :].astype(F32)
    for unit in range(3):
        lines = slice(QUAD * unit, QUAD * (unit + 1))
        start = UNIT * (unit + 1)
        buf[start : start + QUAD, :] = come[lines, :].astype(F32)
        buf[start + QUAD : start + UNIT, :] = stay[lines, :].astype(F32)
    leave_rows(buf, out_ref)


def part_quads(value, upper, lower, units):
    for unit in range(units):
        lines = slice(QUAD * unit, QUAD * (unit + 1))
        upper[lines, :] = value[UNIT * unit : UNIT * unit + QUAD, :].astype(upper.dtype)
        lower[lines, :] = value[UNIT * unit + QUAD : UNIT * (unit + 1), :].astype(lower.dtype)


def join_quads(out, start, upper, lower, units):
    for unit in range(units):
        lines = slice(QUAD * unit, QUAD * (unit + 1))
        first = start + UNIT * unit
        out[first : first + QUAD, :] = upper[lines, :]
        out[first + QUAD : first + UNIT, :] = lower[lines, :]


def enter_entry_kernel(keep, come, tile, edge):
    value = (keep[...] + come[...].astype(F32)).astype(BF16)
    tile[...] = value
    edge[...] = value[3 * UNIT :, :]


def roll_ahead_kernel(place, tile, come, send, stay):
    part_quads(tile, send, stay, 3)
    taken = jnp.where(place[HEAD] == 1, come[...], tile[3 * UNIT :, :])
    send[3 * QUAD :, :] = taken[:QUAD, :]
    stay[3 * QUAD :, :] = taken[QUAD:, :]


def roll_back_kernel(place, stay_main, send_main, edge, come, send, stay):
    taken = jnp.where(place[HEAD] == 1, come[...], edge[...])
    stay[: 3 * QUAD, :] = stay_main[...]
    stay[3 * QUAD :, :] = taken[:QUAD, :]
    send[: 3 * QUAD, :] = send_main[...]
    send[3 * QUAD :, :] = taken[QUAD:, :]


def grad_enter_kernel(in_ref, send, stay, buf):
    buf[...] = jnp.zeros(buf.shape, F32)
    enter_rows(in_ref, buf, 0)
    part_quads(buf, send, stay, 4)


def grad_join_kernel(stay, come, out):
    join_quads(out, 0, stay, come, 4)


def last_entry_kernel(keep, come, middle, b_fc2, send, stay, buf):
    buf[...] = keep[...] + come[...].astype(F32) + middle[...] + b_fc2[...]
    part_quads(buf, stay, send, 4)


def entry_onehot(base_ref):
    entry = lax.broadcasted_iota(jnp.int32, (ENTRIES, 256), 0)
    return (entry == base_ref[...]).astype(F32).astype(BF16)


LINES = WIN * GROUP


def bias_body(table_ref, base_ref, row_map_ref, col_map_ref, out_ref, left, right, strip):
    table = table_ref[...]
    turned = jnp.concatenate([pltpu.roll(table, ENTRIES - col, 1) if col else table for col in range(WIN)], axis=0)
    high, low = halves_of(turned)
    onehot = entry_onehot(base_ref)
    spread = mm(high, onehot) + mm(low, onehot)
    left[0:LINES, :] = spread[:, :128]
    right[0:LINES, :] = spread[:, 128:]
    left[LINES:, :] = jnp.zeros((16 * GROUP - LINES, 128), F32)
    right[LINES:, :] = jnp.zeros((16 * GROUP - LINES, 128), F32)
    for head in range(GROUP):
        wide = jnp.concatenate(
            [left[pl.ds(head, 16, stride=GROUP), :], right[pl.ds(head, 16, stride=GROUP), :]], axis=1
        )
        for row in range(WIN):
            start = (WIN - 1 - row) * WIN
            strip[16 * row : 16 * (row + 1), TOK * head : TOK * (head + 1)] = wide[:, start : start + TOK]
    high, low = halves_of(strip[...])
    rows = mm(row_map_ref[...], high) + mm(row_map_ref[...], low)
    live = lax.broadcasted_iota(jnp.int32, (TOK, TOK), 1) % QUAD < LIVE
    for head in range(GROUP):
        high, low = halves_of(rows[:, TOK * head : TOK * (head + 1)])
        value = mm(high, col_map_ref[...]) + mm(low, col_map_ref[...])
        out_ref[:, TOK * head : TOK * (head + 1)] = jnp.where(live, value, FAR)


BIAS_SCRATCH = (
    pltpu.VMEM((16 * GROUP, 128), F32),
    pltpu.VMEM((16 * GROUP, 128), F32),
    pltpu.VMEM((160, KEYS), F32),
)


def table_body(sum_ref, base_ref, row_back_ref, col_map_ref, out_ref, row, left, right, strip):
    high, low = halves_of(sum_ref[...])
    turned = [
        mm_nt(high[:, TOK * head : TOK * (head + 1)], col_map_ref[...])
        + mm_nt(low[:, TOK * head : TOK * (head + 1)], col_map_ref[...])
        for head in range(GROUP)
    ]
    high, low = halves_of(jnp.concatenate(turned, axis=1))
    strip[...] = mm(row_back_ref[...], high) + mm(row_back_ref[...], low)
    for head in range(GROUP):
        total = jnp.zeros((16, 256), F32)
        for line in range(WIN):
            block = strip[16 * line : 16 * (line + 1), TOK * head : TOK * (head + 1)]
            wide = jnp.concatenate([block, jnp.zeros((16, 128), F32)], axis=1)
            start = (WIN - 1 - line) * WIN
            total = total + (pltpu.roll(wide, start, 1) if start else wide)
        left[pl.ds(head, 16, stride=GROUP), :] = total[:, :128]
        right[pl.ds(head, 16, stride=GROUP), :] = total[:, 128:]
    onehot = entry_onehot(base_ref)
    high, low = halves_of(jnp.concatenate([left[0:LINES, :], right[0:LINES, :]], axis=1))
    spread = mm_nt(high, onehot) + mm_nt(low, onehot)
    table = spread[0:GROUP, :]
    for col in range(1, WIN):
        table = table + pltpu.roll(spread[GROUP * col : GROUP * (col + 1), :], col, 1)
    out_ref[row : row + GROUP, :] = table[:, :256]
    out_ref[row + GROUP : row + 2 * GROUP, :] = jnp.concatenate(
        [table[:, 256:], jnp.zeros((GROUP, 128), F32)], axis=1
    )


def pack_kernel(place, w_qkv_ref, w_proj_ref, order_ref, first_ref, second_ref, part_ref):
    for layer, out_ref in enumerate((first_ref, second_ref)):
        mixed = mm(w_qkv_ref[layer], order_ref[...]).astype(BF16)
        for part in range(3):
            out_ref[512 * part : 512 * (part + 1), :] = mixed[:, 256 * part : 256 * (part + 1)]
        for part in range(2):
            out_ref[ROWS_QKV + 256 * part : ROWS_QKV + 256 * (part + 1), :] = w_proj_ref[
                layer, :, 256 * part : 256 * (part + 1)
            ]
    start = place[COL] * HALF_ATT + place[NEAR] * QUARTER_ATT
    part_ref[...] = second_ref[pl.ds(pl.multiple_of(start, QUARTER_ATT), QUARTER_ATT), :]


def pack_weights(place, w_qkv, w_proj, order):
    return run_kernel(
        pack_kernel,
        [place, w_qkv, w_proj, order],
        [pltpu.HBM((ROWS_ATT, 256), BF16)] * 2 + [shape_of((QUARTER_ATT, 256), BF16)],
        specs={0: SMEM},
    )


def join_pack(place_ref, mine, theirs, out):
    out[pl.ds(pl.multiple_of(place_ref[COL] * HALF_ATT, HALF_ATT), HALF_ATT), :] = mine[...]
    out[pl.ds(pl.multiple_of((1 - place_ref[COL]) * HALF_ATT, HALF_ATT), HALF_ATT), :] = theirs[...]


def bias_of(table, base, row_map, col_map):
    return run_kernel(
        bias_body,
        [table, base, row_map, col_map],
        [shape_of((TOK, KEYS), F32)],
        BIAS_SCRATCH,
    )[0]


def project(normed, pack_ref, qv_ref):
    parts = [mm(normed, pack_ref[512 * part : 512 * (part + 1), :]) for part in range(3)]
    return (
        (parts[0] + qv_ref[0:1, :]).astype(BF16),
        parts[1].astype(BF16),
        (parts[2] + qv_ref[1:2, :]).astype(BF16),
    )


def spread_heads(ref, value, heads_ref):
    for head in range(GROUP):
        lines = slice(TOK * head, TOK * (head + 1))
        ref[lines, :] = value * heads_ref[lines, :]


def attend(qkv_ref, base, bias_ref, region, heads_ref, probs_ref, probs_base, stack, wide):
    rows = pl.ds(base, TOK)
    spread_heads(stack, qkv_ref[rows, 256:512], heads_ref)
    logits = mm_nt(qkv_ref[rows, 0:256], stack[...])
    for head in range(GROUP):
        lanes = slice(TOK * head, TOK * (head + 1))
        score = logits[:, lanes] * SCALE + bias_ref[:, lanes]
        if region is not None:
            score = score + region
        grown = jnp.exp(score - jnp.max(score, axis=-1, keepdims=True))
        probs = (grown / jnp.sum(grown, axis=-1, keepdims=True)).astype(BF16)
        wide[:, lanes] = probs
        probs_ref[pl.ds(probs_base + TOK * head, TOK), :] = probs
    spread_heads(stack, qkv_ref[rows, 512:768], heads_ref)
    return mm(wide[...], stack[...]).astype(BF16)


def attend_back(qkv_ref, base, grad, heads_ref, probs_ref, probs_base, total_ref, stack, wide, tall, mixed_ref):
    rows = pl.ds(base, TOK)
    spread_heads(stack, qkv_ref[rows, 512:768], heads_ref)
    grad_probs = mm_nt(grad, stack[...])
    for head in range(GROUP):
        lanes = slice(TOK * head, TOK * (head + 1))
        probs = probs_ref[pl.ds(probs_base + TOK * head, TOK), :].astype(F32)
        part = grad_probs[:, lanes]
        centre = jnp.sum(probs * part, axis=-1, keepdims=True)
        inner = (probs * (part - centre)).astype(BF16)
        wide[:, lanes] = inner
        tall[lanes, :] = inner
        total_ref[:, lanes] = total_ref[:, lanes] + inner.astype(F32)
    spread_heads(stack, grad, heads_ref)
    mixed_ref[rows, 512:768] = mm_tn(probs_ref[pl.ds(probs_base, KEYS), :], stack[...]).astype(BF16)
    spread_heads(stack, qkv_ref[rows, 256:512], heads_ref)
    mixed_ref[rows, 0:256] = (mm(wide[...], stack[...]) * SCALE).astype(BF16)
    spread_heads(stack, qkv_ref[rows, 0:256], heads_ref)
    mixed_ref[rows, 256:512] = (mm_tn(tall[...], stack[...]) * SCALE).astype(BF16)


def project_out(context, pack_ref):
    return jnp.concatenate(
        [mm(context, pack_ref[ROWS_QKV + 256 * part : ROWS_QKV + 256 * (part + 1), :]) for part in range(2)],
        axis=1,
    )


def project_out_back(grad, pack_ref):
    return (
        mm_nt(grad[:, :256], pack_ref[ROWS_QKV : ROWS_QKV + 256, :])
        + mm_nt(grad[:, 256:], pack_ref[ROWS_QKV + 256 : ROWS_ATT, :])
    ).astype(BF16)


def project_back(mixed_ref, pack_ref):
    total = mm_nt(mixed_ref[:, 0:256], pack_ref[0:512, :])
    for part in range(1, 3):
        total = total + mm_nt(mixed_ref[:, 256 * part : 256 * (part + 1)], pack_ref[512 * part : 512 * (part + 1), :])
    return total


ATTEND_SCRATCH = (pltpu.VMEM((KEYS, SPAN), BF16), pltpu.VMEM((TOK, KEYS), BF16))


def attention_plain_kernel(
    place_ref, own, other, gain, bias, pack, qv, offset, heads,
    whole, normed_out, qkv, probs, context, part_out, stack, wide, buf,
):
    here = place_ref[HEAD]
    buf[...] = jnp.zeros(buf.shape, F32)
    enter_rows(own, buf, 0)
    enter_rows(other, buf, TILE)
    whole[pl.ds(pl.multiple_of(here * TILE, TILE), TILE), :] = buf[:TILE, :].astype(BF16)
    whole[pl.ds(pl.multiple_of((1 - here) * TILE, TILE), TILE), :] = buf[TILE:, :].astype(BF16)
    unit, _ = norm_parts(whole[...].astype(F32))
    normed_out[...] = (unit * gain[...] + bias[...]).astype(BF16)
    for part, value in enumerate(project(normed_out[...], pack, qv)):
        qkv[:, 256 * part : 256 * (part + 1)] = value

    def window(place, carry):
        base = pl.multiple_of(place * TOK, TOK)
        context[pl.ds(base, TOK), :] = attend(
            qkv, base, offset, None, heads, probs, pl.multiple_of(place * KEYS, KEYS), stack, wide
        )
        return carry

    lax.fori_loop(0, PAIR // TOK, window, 0)
    part_out[...] = project_out(context[...], pack).astype(BF16)


def attention_shifted_kernel(
    place_ref, stay, come, gain, bias, gain2, bias2, pack_a, pack_mine, pack_theirs, qv_a, qv_b, off_a, off_b,
    ids_q, ids_k, heads, b_proj,
    keep, normed_out, qkv_a, qkv_b, probs_a, probs_b, context_a, context_b, middle_out, second_out, stack, wide,
    pack_b,
):
    join_pack(place_ref, pack_mine, pack_theirs, pack_b)
    join_quads(keep, 0, stay, come, 4)
    unit, _ = norm_parts(keep[...].astype(F32))
    normed_out[...] = (unit * gain[...] + bias[...]).astype(BF16)
    total = keep[...].astype(F32) + b_proj[...]
    for pack, qv, off, qkv, probs, context in (
        (pack_a, qv_a, off_a, qkv_a, probs_a, context_a),
        (pack_b, qv_b, off_b, qkv_b, probs_b, context_b),
    ):
        for part, value in enumerate(project(normed_out[...], pack, qv)):
            qkv[:, 256 * part : 256 * (part + 1)] = value

        def window(place, carry):
            base = pl.multiple_of(place * TOK, TOK)
            region = jnp.where(ids_q[pl.ds(base, TOK), :] != ids_k[place], -100.0, 0.0)
            context[pl.ds(base, TOK), :] = attend(
                qkv, base, off, region, heads, probs, pl.multiple_of(place * KEYS, KEYS), stack, wide
            )
            return carry

        lax.fori_loop(0, TILE // TOK, window, 0)
        total = total + project_out(context[...], pack)
    middle_out[...] = total
    unit, _ = norm_parts(total)
    second_out[...] = (unit * gain2[...] + bias2[...]).astype(BF16)


def gelu_parts(hidden):
    chance = 0.5 * (1.0 + lax.erf(hidden * ROOT_HALF))
    slope = chance + hidden * (jnp.exp(-0.5 * hidden * hidden) * ROOT_TWO_PI)
    return (hidden * chance).astype(BF16), slope.astype(BF16)


CHUNK = 256


def mlp_plain_kernel(
    place_ref, whole, part_own, part_other, b_proj, gain, bias, w_fc1, b_fc1, w_fc2, b_fc2,
    middle, second, active, slope, keep, send, spun,
):
    here = place_ref[HEAD]
    middle[...] = (
        whole[...].astype(F32) + (part_own[...].astype(F32) + part_other[...].astype(F32)) + b_proj[...]
    )
    unit, _ = norm_parts(middle[...])
    second[...] = (unit * gain[...] + bias[...]).astype(BF16)
    for place in range(1024 // CHUNK):
        lanes = slice(CHUNK * place, CHUNK * (place + 1))
        hidden = mm(second[...], w_fc1[0, :, lanes]) + b_fc1[:, lanes]
        active[:, lanes], slope[:, lanes] = gelu_parts(hidden)
    out = mm(active[...], w_fc2[0])
    spun[0 : PAIR - UNIT, :] = out[UNIT:, :]
    spun[PAIR - UNIT :, :] = out[:UNIT, :]
    send[...] = spun[pl.ds((1 - here) * TILE, TILE), :].astype(BF16)
    spun[0 : PAIR - UNIT, :] = spun[0 : PAIR - UNIT, :] + middle[UNIT:, :]
    spun[PAIR - UNIT :, :] = spun[PAIR - UNIT :, :] + middle[:UNIT, :]
    keep[...] = spun[pl.ds(here * TILE, TILE), :] + b_fc2[...]


def mlp_shifted_kernel(
    place_ref, own, other, grad_own, grad_other, grad_far, w_fc1, b_fc1, w_fc2,
    second, grad, active, inner, keep, send, back_keep, back_send, small, slope, spun,
):
    here = place_ref[HEAD]
    mine = pl.ds(pl.multiple_of(here * TILE, TILE), TILE)
    theirs = pl.ds(pl.multiple_of((1 - here) * TILE, TILE), TILE)
    spun[mine, :] = grad_own[...]
    spun[theirs, :] = grad_other[...]
    grad[0 : 7 * UNIT, :] = spun[UNIT:, :]
    grad[7 * UNIT :, :] = grad_far[...]
    second[mine, :] = own[...]
    second[theirs, :] = other[...]
    for place in range(1024 // CHUNK):
        lanes = slice(CHUNK * place, CHUNK * (place + 1))
        hidden = mm(second[...], w_fc1[0, :, lanes]) + b_fc1[:, lanes]
        active[:, lanes], slope[:, lanes] = gelu_parts(hidden)
    for place in range(1024 // CHUNK):
        lanes = slice(CHUNK * place, CHUNK * (place + 1))
        back = mm_nt(grad[...], w_fc2[0, lanes, :]) * slope[:, lanes].astype(F32)
        inner[:, lanes] = back.astype(BF16)
    back_keep[...] = mm_nt(inner[mine, :], w_fc1[0])
    back_send[...] = mm_nt(inner[theirs, :], w_fc1[0]).astype(BF16)
    keep[...] = mm(active[mine, :], w_fc2[0])
    send[...] = mm(active[theirs, :], w_fc2[0]).astype(BF16)
    put_row(small, 0, column_sum(inner[...].astype(F32)))
    small[4:, :] = jnp.zeros((4, 256), F32)


def mlp_plain_back_kernel(
    place_ref, own, other, slope, w_fc1, w_fc2,
    grad, inner, back, spun,
):
    for which, value in enumerate((own, other)):
        here = place_ref[HEAD] if which == 0 else 1 - place_ref[HEAD]
        start = pl.multiple_of(here * TILE, TILE)
        for unit in range(4):
            lines = slice(QUAD * unit, QUAD * (unit + 1))
            spun[pl.ds(start + UNIT * unit, QUAD), :] = value[4 * QUAD + QUAD * unit : 4 * QUAD + QUAD * (unit + 1), :]
            spun[pl.ds(start + UNIT * unit + QUAD, QUAD), :] = value[lines, :]
    grad[0:UNIT, :] = spun[PAIR - UNIT :, :]
    grad[UNIT:, :] = spun[0 : PAIR - UNIT, :]
    for place in range(1024 // CHUNK):
        lanes = slice(CHUNK * place, CHUNK * (place + 1))
        value = mm_nt(grad[...], w_fc2[0, lanes, :]) * slope[:, lanes].astype(F32)
        inner[:, lanes] = value.astype(BF16)
    back[...] = mm_nt(inner[...], w_fc1[0]).astype(BF16)


def deal_halves(place_ref, whole, keep, send, half, base=0, start=0):
    mine = pl.multiple_of(place_ref[COL] * half, half)
    theirs = pl.multiple_of((1 - place_ref[COL]) * half, half)
    keep[start : start + half, :] = whole[pl.ds(base + mine, half), :]
    send[start : start + half, :] = whole[pl.ds(base + theirs, half), :]


def mlp_weights_kernel(place_ref, second, active, grad, inner, keep, send, out):
    for place in range(4):
        lanes = slice(256 * place, 256 * (place + 1))
        out[512 * place : 512 * (place + 1), :] = mm_tn(second[...], inner[:, lanes]).astype(BF16)
    for place in range(2):
        lanes = slice(256 * place, 256 * (place + 1))
        start = 2048 + 1024 * place
        out[start : start + 1024, :] = mm_tn(active[...], grad[:, lanes]).astype(BF16)
    deal_halves(place_ref, out, keep, send, ROWS_MLP // 2)


def mlp_weights(place, second, active, grad, inner):
    return run_kernel(
        mlp_weights_kernel,
        [place, second, active, grad, inner],
        [shape_of((ROWS_MLP // 2, 256), BF16)] * 2,
        [pltpu.VMEM((ROWS_MLP, 256), BF16)],
        specs={0: SMEM},
    )


def attention_shifted_back_kernel(
    place_ref, grad_all, back_own, back_other, middle, entry, gain, gain2, qkv_a, qkv_b, probs_a, probs_b,
    pack_a, pack_mine, pack_theirs, heads,
    grad_low, mixed_a, mixed_b, total_a, total_b, stay_main, send_main, edge, small,
    stack, wide, tall, grad_context, below, pack_b,
):
    join_pack(place_ref, pack_mine, pack_theirs, pack_b)
    here = place_ref[HEAD]
    upstream = grad_all[pl.ds(pl.multiple_of(here * TILE, TILE), TILE), :].astype(F32)
    back = back_own[...] + back_other[...].astype(F32)
    unit, inverse = norm_parts(middle[...])
    put_row(small, 0, column_sum(back * unit))
    put_row(small, 2, column_sum(back))
    put_row(small, 4, column_sum(upstream))
    grad_middle = upstream + norm_back(back, gain2[...], unit, inverse)
    grad_low[...] = grad_middle.astype(BF16)
    put_row(small, 6, column_sum(grad_low[...].astype(F32)))
    first = jnp.zeros((TILE, WIDTH), F32)
    for pack, qkv, probs, mixed, total in (
        (pack_a, qkv_a, probs_a, mixed_a, total_a),
        (pack_b, qkv_b, probs_b, mixed_b, total_b),
    ):
        grad_context[...] = project_out_back(grad_low[...], pack)
        total[...] = jnp.zeros((TOK, KEYS), F32)

        def window(place, carry):
            base = pl.multiple_of(place * TOK, TOK)
            attend_back(
                qkv, base, grad_context[pl.ds(base, TOK), :], heads, probs, pl.multiple_of(place * KEYS, KEYS),
                total, stack, wide, tall, mixed,
            )
            return carry

        lax.fori_loop(0, TILE // TOK, window, 0)
        first = first + project_back(mixed, pack)
    unit, inverse = norm_parts(entry[...].astype(F32))
    put_row(small, 8, column_sum(first * unit))
    put_row(small, 10, column_sum(first))
    put_row(small, 12, column_sum(mixed_a[...].astype(F32)))
    small[15:16, :] = jnp.zeros((1, 256), F32)
    put_row(small, 16, column_sum(mixed_b[...].astype(F32)))
    small[19:24, :] = jnp.zeros((5, 256), F32)
    below[...] = grad_middle + norm_back(first, gain[...], unit, inverse)
    part_quads(below, stay_main, send_main, 3)
    edge[...] = below[3 * UNIT :, :].astype(BF16)


def attention_plain_back_kernel(
    place_ref, grad, back_own, back_other, middle, whole, gain, gain2, qkv, probs, pack, heads, inner,
    grad_low, mixed, total, first_keep, first_send, kept, small, stack, wide, tall, grad_context, first,
):
    here = place_ref[HEAD]
    mine = pl.ds(pl.multiple_of(here * TILE, TILE), TILE)
    theirs = pl.ds(pl.multiple_of((1 - here) * TILE, TILE), TILE)
    back = back_own[...].astype(F32) + back_other[...].astype(F32)
    unit, inverse = norm_parts(middle[...])
    share = back_own[...].astype(F32)
    put_row(small, 0, column_sum(share * unit))
    put_row(small, 2, column_sum(share))
    put_row(small, 4, column_sum(grad[mine, :].astype(F32)))
    first[...] = grad[...].astype(F32) + norm_back(back, gain2[...], unit, inverse)
    kept[...] = first[mine, :]
    grad_low[...] = first[...].astype(BF16)
    put_row(small, 6, column_sum(grad_low[mine, :].astype(F32)))
    grad_context[...] = project_out_back(grad_low[...], pack)
    total[...] = jnp.zeros((TOK, KEYS), F32)

    def window(place, carry):
        base = pl.multiple_of(place * TOK, TOK)
        attend_back(
            qkv, base, grad_context[pl.ds(base, TOK), :], heads, probs, pl.multiple_of(place * KEYS, KEYS),
            total, stack, wide, tall, mixed,
        )
        return carry

    lax.fori_loop(0, PAIR // TOK, window, 0)
    first[...] = project_back(mixed, pack)
    first_keep[...] = first[mine, :]
    first_send[...] = first[theirs, :].astype(BF16)
    unit, _ = norm_parts(whole[...].astype(F32))
    put_row(small, 8, column_sum(first[...] * unit))
    put_row(small, 10, column_sum(first[...]))
    put_row(small, 12, column_sum(mixed[...].astype(F32)))
    small[15:16, :] = jnp.zeros((1, 256), F32)
    put_row(small, 16, column_sum(inner[...].astype(F32)))
    small[20:24, :] = jnp.zeros((4, 256), F32)


def attention_weights_body(normed, mixed, context, grad_low, order, out, start):
    turned = [mm_tn(normed[...], mixed[:, 256 * part : 256 * (part + 1)]).astype(BF16) for part in range(3)]
    canon = mm_nt(jnp.concatenate(turned, axis=1), order[...]).astype(BF16)
    for part in range(3):
        out[start + 512 * part : start + 512 * (part + 1), :] = canon[:, 256 * part : 256 * (part + 1)]
    for part in range(2):
        lines = slice(start + ROWS_QKV + 256 * part, start + ROWS_QKV + 256 * (part + 1))
        out[lines, :] = mm_tn(context[...], grad_low[:, 256 * part : 256 * (part + 1)]).astype(BF16)


def attention_weights_plain_kernel(place_ref, normed, mixed, context, grad_low, order, keep, send, out):
    attention_weights_body(normed, mixed, context, grad_low, order, out, 0)
    deal_halves(place_ref, out, keep, send, HALF_ATT)


def attention_weights_shifted_kernel(
    place_ref, normed, mixed_a, mixed_b, context_a, context_b, grad_low, order, mlp_keep, mlp_send, keep, send, out
):
    attention_weights_body(normed, mixed_a, context_a, grad_low, order, out, 0)
    attention_weights_body(normed, mixed_b, context_b, grad_low, order, out, ROWS_ATT)
    for which, mlp, ref in ((place_ref[COL], mlp_keep, keep), (1 - place_ref[COL], mlp_send, send)):
        for block in range(GROUP):
            first = 4 * EIGHTH * block
            ref[first : first + 2 * EIGHTH, :] = mlp[2 * EIGHTH * block : 2 * EIGHTH * (block + 1), :]
            for part in range(2):
                start = pl.multiple_of(which * HALF_ATT, HALF_ATT) + part * ROWS_ATT + EIGHTH * block
                first = EIGHTH * (4 * block + 2 + part)
                ref[first : first + EIGHTH, :] = out[pl.ds(start, EIGHTH), :]


def table_kernel(total, base, row_back, col_map, out, left, right, strip):
    table_body(total, base, row_back, col_map, out, 0, left, right, strip)


def table_of(total, base, row_back, col_map):
    return run_kernel(
        table_kernel, [total, base, row_back, col_map], [shape_of((2 * GROUP, 256), F32)], BIAS_SCRATCH
    )[0]


def last_kernel(place_ref, whole, gain, keep, other, kept, out, buf):
    here = place_ref[HEAD]
    unit, inverse = norm_parts(whole[pl.ds(pl.multiple_of(here * TILE, TILE), TILE), :].astype(F32))
    buf[...] = kept[...] + norm_back(keep[...] + other[:TILE, :].astype(F32), gain[...], unit, inverse)
    leave_rows(buf, out)


def band_pairs(first, second):
    return [(band * 2 + col, (band ^ (first if col == 0 else second)) * 2 + col) for band in range(8) for col in range(2)]


STEP_PAIRS = (
    [(band * 2 + col, band * 2 + 1 - col) for band in range(8) for col in range(2)],
    band_pairs(1, 2),
    band_pairs(2, 1),
    band_pairs(4, 4),
)


def exchange(value, step):
    return lax.ppermute(value, ("band", "col"), STEP_PAIRS[step])


def double_kernel(place_ref, mine, come, out, *, step):
    half = mine.shape[0]
    out[pl.ds(pl.multiple_of(place_ref[COL + step] * half, half), half), :] = mine[...]
    out[pl.ds(pl.multiple_of((1 - place_ref[COL + step]) * half, half), half), :] = come[...]


def double(place, mine, come, step):
    return run_kernel(
        partial(double_kernel, step=step),
        [place, mine, come],
        [shape_of((2 * mine.shape[0], 256), BF16)],
        specs={0: SMEM},
    )[0]


def after(value, *others):
    return lax.optimization_barrier((value,) + others)[0]


def add_low(left, right):
    return (left.astype(F32) + right.astype(F32)).astype(BF16)


class PageSum:
    def __init__(self, place, kept, send, across=False):
        self.place, self.kept, self.sent, self.across, self.stage = place, kept, send, across, 0
        self.come = exchange(send, 0)

    def tie(self, *others):
        self.kept = after(self.kept, *others)

    def advance(self):
        self.stage += 1
        stage = self.stage
        kept, come = self.kept, self.come
        rows = kept.shape[0]
        if stage < 4:
            half = rows // 2
            bit = self.place[COL + stage]

            def half_at(value, which):
                return lax.dynamic_slice_in_dim(value, which * half, half, 0)

            self.sent = add_low(half_at(kept, 1 - bit), half_at(come, 1 - bit))
            self.kept = add_low(half_at(kept, bit), half_at(come, bit))
            self.come = exchange(self.sent, stage)
            return
        if stage == 4 and self.across:
            start = rows // 4 * 3
            self.sent = add_low(kept[start:], come[start:])
            self.kept = add_low(kept[:start], come[:start])
            self.come = swap_head(self.sent)
            return
        if self.across:
            stage -= 1
            if stage == 4:
                start = rows - come.shape[0]
                self.kept = jnp.concatenate([kept[:start], add_low(kept[start:], come)], axis=0)
        elif stage == 4:
            self.kept = add_low(kept, come)
        if stage > 4:
            bit = self.place[COL + 8 - stage]
            whole = jnp.zeros((2 * rows, 256), BF16)
            whole = lax.dynamic_update_slice_in_dim(whole, kept, bit * rows, 0)
            self.kept = lax.dynamic_update_slice_in_dim(whole, come, (1 - bit) * rows, 0)
        self.sent = self.kept
        self.come = exchange(self.sent, 7 - stage)

    @property
    def halves(self):
        return self.kept, self.come


def settle(chains, extras=()):
    flat = [item for chain in chains for item in chain.halves] + list(extras)
    flat = lax.optimization_barrier(tuple(flat))
    for number, chain in enumerate(chains):
        chain.kept, chain.come = flat[2 * number : 2 * number + 2]
    return list(flat[2 * len(chains) :])


def both_halves(place_ref, mine, come):
    return (place_ref[COL], mine), (1 - place_ref[COL], come)


def unpack_att(whole, qkv, proj):
    for part in range(3):
        qkv[0, :, 256 * part : 256 * (part + 1)] = whole[512 * part : 512 * (part + 1), :].astype(F32)
    for part in range(2):
        start = ROWS_QKV + 256 * part
        proj[0, :, 256 * part : 256 * (part + 1)] = whole[start : start + 256, :].astype(F32)


def unpack_mlp(whole, fc1, fc2):
    for part in range(4):
        fc1[0, :, 256 * part : 256 * (part + 1)] = whole[512 * part : 512 * (part + 1), :].astype(F32)
    for part in range(2):
        start = 2048 + 1024 * part
        fc2[0, :, 256 * part : 256 * (part + 1)] = whole[start : start + 1024, :].astype(F32)


def unpack_layer_kernel(place_ref, mine, come, qkv, proj, fc1, fc2, att_whole, mlp_whole):
    for which, value in both_halves(place_ref, mine, come):
        for block in range(GROUP):
            first = 3 * EIGHTH * block
            start = pl.multiple_of(which * (ROWS_MLP // 2), 16) + 2 * EIGHTH * block
            mlp_whole[pl.ds(start, 2 * EIGHTH), :] = value[first : first + 2 * EIGHTH, :]
            start = pl.multiple_of(which * HALF_ATT, 16) + EIGHTH * block
            att_whole[pl.ds(start, EIGHTH), :] = value[first + 2 * EIGHTH : first + 3 * EIGHTH, :]
    unpack_att(att_whole, qkv, proj)
    unpack_mlp(mlp_whole, fc1, fc2)


def unpack_mlp_kernel(place_ref, mine, come, *refs):
    fc1, fc2, whole = refs[-3:]
    for which, value in both_halves(place_ref, mine, come):
        whole[pl.ds(pl.multiple_of(which * (ROWS_MLP // 2), 16), ROWS_MLP // 2), :] = value[...]
    unpack_mlp(whole, fc1, fc2)


SMALLS = 256
TABLE_ROWS = (40, 56)


def unpack_last_kernel(
    place_ref, mine, come, order_qv, qkv_in, proj_in,
    qkv, proj, gain, bias, b_qv, table, b_proj, b_fc1, b_fc2, whole, sums,
):
    for which, value in both_halves(place_ref, mine, come):
        whole[pl.ds(pl.multiple_of(which * HALF_ATT, 16), HALF_ATT), :] = value[:HALF_ATT, :]
        start = pl.multiple_of(which * (SMALLS // 2), 16)
        sums[pl.ds(start, SMALLS // 2), :] = value[HALF_ATT:, :].astype(F32)
    unpack_att(whole, qkv, proj)

    for layer, (norm1, norm2) in enumerate(((8, 0), (20, 12))):
        for which, row in enumerate((norm1, norm2)):
            for part in range(2):
                lanes = slice(256 * part, 256 * (part + 1))
                gain[layer, which : which + 1, lanes] = sums[row + part : row + part + 1, :]
                bias[layer, which : which + 1, lanes] = sums[row + 2 + part : row + 3 + part, :]
    for layer, base in enumerate((0, 12)):
        for part in range(2):
            lanes = slice(256 * part, 256 * (part + 1))
            b_fc2[layer : layer + 1, lanes] = sums[base + 4 + part : base + 5 + part, :]
            b_proj[layer : layer + 1, lanes] = sums[base + 6 + part : base + 7 + part, :]
    for layer, base in enumerate((32, 36)):
        for part in range(4):
            b_fc1[layer : layer + 1, 256 * part : 256 * (part + 1)] = sums[base + part : base + part + 1, :]
    for layer, base in enumerate((28, 24)):
        row = jnp.concatenate([sums[base : base + 1, :], sums[base + 2 : base + 3, :]], axis=1)
        b_qv[layer : layer + 1, :] = mm(row.astype(BF16), order_qv[...])
    for layer, base in enumerate(TABLE_ROWS):
        rows = jnp.concatenate(
            [sums[base : base + GROUP, :], sums[base + GROUP : base + 2 * GROUP, :128]], axis=1
        )
        table[layer] = rows[:, : table.shape[2]]


def swap_head(value):
    return lax.ppermute(value, "head", [(0, 1), (1, 0)])


def fast_device(
    act_in, ln_gain, ln_bias, w_qkv, b_qv, rel_table, w_proj, b_proj, w_fc1, b_fc1, w_fc2, b_fc2, grad_out
):
    row_map, row_back, col_map, base, order, heads, order_qv, token_row, token_col = constants()
    band = lax.axis_index("band")
    col = lax.axis_index("col")
    head = lax.axis_index("head")
    bands = lax.axis_size("band")
    cols = lax.axis_size("col")
    digit = [(band >> power) & 1 for power in range(3)]
    place = jnp.stack(
        [
            head,
            col,
            jnp.where(col == 0, digit[0], digit[1]),
            jnp.where(col == 0, digit[1], digit[0]),
            digit[2],
            digit[0],
        ]
    ).astype(jnp.int32)
    band_up = [(here, (here - 1) % bands) for here in range(bands)]
    band_down = [(here, (here + 1) % bands) for here in range(bands)]
    col_left = [(here, (here - 1) % cols) for here in range(cols)]
    edge_left = [(here * 2 + 1, (here - 1) % cols * 2 + 1) for here in range(cols)]
    edge_right = [(here * 2 + 1, (here + 1) % cols * 2 + 1) for here in range(cols)]
    gain = [[ln_gain[layer, which][None] for which in range(2)] for layer in range(2)]
    bias = [[ln_bias[layer, which][None] for which in range(2)] for layer in range(2)]
    row_proj = [b_proj[layer][None] for layer in range(2)]
    row_fc1 = [b_fc1[layer][None] for layer in range(2)]
    row_fc2 = [b_fc2[layer][None] for layer in range(2)]
    qv = b_qv.reshape(2, GROUP, 2, HEAD_DIM).transpose(0, 2, 1, 3).reshape(2, 2, SPAN)
    tables = jnp.pad(rel_table, ((0, 0), (0, ENTRIES - rel_table.shape[1]), (0, 0))).transpose(0, 2, 1)

    def rows_bf(count, width=WIDTH):
        return shape_of((count, width), BF16)

    def rows_f32(count, width=WIDTH):
        return shape_of((count, width), F32)

    def saved(count, width=WIDTH, kind=BF16):
        return pltpu.HBM((count, width), kind)

    def far(value):
        return pltpu.with_memory_space_constraint(value, pltpu.HBM)

    x_other = swap_head(act_in)
    pack0, pack1, pack1_part = pack_weights(place, far(w_qkv), far(w_proj), order)
    pack1_part = swap_head(pack1_part)
    small1 = jnp.concatenate([tables[1], jnp.pad(qv[1], ((0, 6), (0, ENTRIES - SPAN)))], axis=0)
    small1_other = swap_head(small1)
    off0 = bias_of(tables[0], base, row_map, col_map)
    whole, normed0, qkv0, probs0, context0, part0 = run_kernel(
        attention_plain_kernel,
        [place, act_in, x_other, gain[0][0], bias[0][0], far(pack0), qv[0], off0, heads],
        [
            rows_bf(PAIR), saved(PAIR), saved(PAIR, 768), saved(4 * KEYS, TOK), saved(PAIR, SPAN), rows_bf(PAIR),
        ],
        ATTEND_SCRATCH + (pltpu.VMEM((PAIR, WIDTH), F32),),
        specs={0: SMEM},
    )
    part0_other = swap_head(part0)

    off1 = bias_of(after(tables[1], part0), base, row_map, col_map)
    grad_send, grad_stay = run_kernel(
        grad_enter_kernel, [after(grad_out, part0)], [rows_bf(4 * QUAD)] * 2, [pltpu.VMEM((TILE, WIDTH), F32)]
    )
    grad_come = lax.ppermute(grad_send, "band", band_up)
    (grad_own,) = run_kernel(grad_join_kernel, [grad_stay, grad_come], [rows_bf(TILE)])
    pack1_part = after(pack1_part, part0)
    near = [(here, here ^ 1) for here in range(bands)]
    pack1_mine = double(place, pack1_part, lax.ppermute(pack1_part, "band", near), NEAR - COL)
    pack1_theirs = lax.ppermute(pack1_mine, "col", [(0, 1), (1, 0)])
    part0 = after(part0, pack1_mine, grad_own, off1)

    middle0, second0, active0, slope0, x1_keep, x1_send = run_kernel(
        mlp_plain_kernel,
        [
            place, whole, part0, part0_other, row_proj[0], gain[0][1], bias[0][1], far(w_fc1), row_fc1[0],
            far(w_fc2), row_fc2[0],
        ],
        [
            saved(PAIR, WIDTH, F32), saved(PAIR), saved(PAIR, 1024), saved(PAIR, 1024), rows_f32(TILE),
            rows_bf(TILE),
        ],
        [pltpu.VMEM((PAIR, WIDTH), F32)],
        specs={0: SMEM, 7: layer_spec(w_fc1, 0), 9: layer_spec(w_fc2, 0)},
    )
    x1_come = swap_head(x1_send)
    off1_other = bias_of(after(small1_other[:GROUP], x1_send), base, row_map, col_map)
    qv1_other = small1_other[GROUP : GROUP + 2, :SPAN]
    tile, edge = run_kernel(enter_entry_kernel, [x1_keep, x1_come], [rows_bf(TILE), rows_bf(UNIT)])
    edge = lax.ppermute(edge, ("col", "head"), edge_left)
    send, stay = run_kernel(roll_ahead_kernel, [place, tile, edge], [rows_bf(4 * QUAD)] * 2, specs={0: SMEM})
    come = lax.ppermute(send, "band", band_up)
    grad_other = swap_head(after(grad_own, tile))

    rows_id = region_ids(WIN * band + jnp.asarray(token_row), WIN * bands)
    cols_id = region_ids(
        2 * WIN * (2 * col + head) + WIN * jnp.arange(2, dtype=jnp.int32)[:, None] + jnp.asarray(token_col)[None],
        4 * WIN * cols,
    )
    ids = (3 * rows_id[None] + cols_id).astype(F32)
    x1, normed1, qkv1a, qkv1b, probs1a, probs1b, context1a, context1b, middle1, second1_own = run_kernel(
        attention_shifted_kernel,
        [
            place, stay, come, gain[1][0], bias[1][0], gain[1][1], bias[1][1], far(pack1),
            pack1_mine, pack1_theirs, qv[1], qv1_other, off1, off1_other, ids.reshape(TILE, 1), ids.reshape(2, 1, TOK), heads,
            row_proj[1],
        ],
        [
            saved(TILE), saved(TILE), saved(TILE, 768), saved(TILE, 768), saved(2 * KEYS, TOK),
            saved(2 * KEYS, TOK), saved(TILE, SPAN), saved(TILE, SPAN), saved(TILE, WIDTH, F32), rows_bf(TILE),
        ],
        ATTEND_SCRATCH + (pltpu.VMEM((ROWS_ATT, 256), BF16),),
        specs={0: SMEM},
    )
    second1_other = swap_head(second1_own)
    grad_far = jnp.where(head == 0, grad_own[:UNIT], grad_other[:UNIT])
    grad_far = lax.ppermute(after(grad_far, second1_own), "col", col_left)
    second1, grad_all, active1, inner1, x2_keep, x2_send, back1_keep, back1_send, small_mlp1 = run_kernel(
        mlp_shifted_kernel,
        [place, second1_own, second1_other, grad_own, grad_other, grad_far, far(w_fc1), row_fc1[1], far(w_fc2)],
        [
            rows_bf(PAIR), rows_bf(PAIR), rows_bf(PAIR, 1024), rows_bf(PAIR, 1024), saved(TILE, WIDTH, F32),
            rows_bf(TILE), rows_f32(TILE), rows_bf(TILE), rows_f32(8, 256),
        ],
        [pltpu.VMEM((PAIR, 1024), BF16), pltpu.VMEM((PAIR, WIDTH), BF16)],
        specs={0: SMEM, 6: layer_spec(w_fc1, 1), 8: layer_spec(w_fc2, 1)},
    )
    back1_other = swap_head(back1_send)
    mlp1_keep, mlp1_send = mlp_weights(place, second1, active1, grad_all, inner1)
    back1_keep = after(back1_keep, mlp1_send)
    grad_low1, mixed1a, mixed1b, total1a, total1b, stay_main, send_main, edge, small_att1 = run_kernel(
        attention_shifted_back_kernel,
        [
            place, grad_all, back1_keep, back1_other, far(middle1), far(x1), gain[1][0], gain[1][1], far(qkv1a),
            far(qkv1b), far(probs1a), far(probs1b), far(pack1), pack1_mine, pack1_theirs, heads,
        ],
        [
            rows_bf(TILE), rows_bf(TILE, 768), rows_bf(TILE, 768), saved(TOK, KEYS, F32), saved(TOK, KEYS, F32),
            rows_bf(3 * QUAD), rows_bf(3 * QUAD), rows_bf(UNIT), rows_f32(24, 256),
        ],
        ATTEND_SCRATCH
        + (
            pltpu.VMEM((KEYS, TOK), BF16),
            pltpu.VMEM((TILE, SPAN), BF16),
            pltpu.VMEM((TILE, WIDTH), F32),
            pltpu.VMEM((ROWS_ATT, 256), BF16),
        ),
        specs={0: SMEM},
    )

    edge_come = lax.ppermute(edge, ("col", "head"), edge_right)
    send, stay = run_kernel(
        roll_back_kernel, [place, stay_main, send_main, edge, edge_come], [rows_bf(4 * QUAD)] * 2, specs={0: SMEM}
    )
    come = lax.ppermute(send, "band", band_down)
    layer1_keep, layer1_send = run_kernel(
        attention_weights_shifted_kernel,
        [
            place, far(after(normed1, send)), mixed1a, mixed1b, far(context1a), far(context1b), grad_low1, order,
            mlp1_keep, mlp1_send,
        ],
        [rows_bf(2 * ROWS_ATT, 256)] * 2,
        [pltpu.VMEM((2 * ROWS_ATT, 256), BF16)],
        specs={0: SMEM},
    )
    own = jnp.concatenate([stay, after(come, layer1_send)], axis=0)
    own_other = swap_head(own)
    come = own
    layer1 = PageSum(place, layer1_keep, after(layer1_send, come), across=True)
    layer1.advance()
    slope0 = after(slope0, layer1.sent)
    grad0, inner0, back0 = run_kernel(
        mlp_plain_back_kernel,
        [
            place, own, own_other, far(slope0), far(w_fc1), far(w_fc2),
        ],
        [rows_bf(PAIR), rows_bf(PAIR, 1024), rows_bf(PAIR)],
        [pltpu.VMEM((PAIR, WIDTH), BF16)],
        specs={0: SMEM, 4: layer_spec(w_fc1, 0), 5: layer_spec(w_fc2, 0)},
    )
    back0_other = swap_head(back0)
    mlp0_keep, mlp0_send = mlp_weights(place, far(second0), far(active0), grad0, inner0)
    table1_send = table_of(far(after(total1b, back0)), base, row_back, col_map)
    table1 = table_of(far(after(total1a, back0)), base, row_back, col_map)
    mlp0 = PageSum(place, mlp0_keep, after(mlp0_send, back0_other))
    layer1.tie(back0_other, mlp0_send, table1, table1_send)
    layer1.advance()
    back0 = after(back0, layer1.sent)
    grad_low0, mixed0, total0, first_keep, first_send, kept0, small_att0 = run_kernel(
        attention_plain_back_kernel,
        [
            place, grad0, back0, back0_other, far(middle0), whole, gain[0][0], gain[0][1], far(qkv0), far(probs0),
            far(pack0), heads, inner0,
        ],
        [
            rows_bf(PAIR), rows_bf(PAIR, 768), rows_f32(TOK, KEYS), rows_f32(TILE), rows_bf(TILE), rows_f32(TILE),
            rows_f32(24, 256),
        ],
        ATTEND_SCRATCH
        + (pltpu.VMEM((KEYS, TOK), BF16), pltpu.VMEM((PAIR, SPAN), BF16), pltpu.VMEM((PAIR, WIDTH), F32)),
        specs={0: SMEM},
    )
    att0_keep, att0_send = run_kernel(
        attention_weights_plain_kernel,
        [place, far(normed0), mixed0, far(context0), grad_low0, order],
        [rows_bf(HALF_ATT, 256)] * 2,
        [pltpu.VMEM((ROWS_ATT, 256), BF16)],
        specs={0: SMEM},
    )
    shared = jnp.concatenate([small_att0[:12], small_att1[:12]], axis=0)
    come = swap_head(jnp.concatenate([shared, small_att1[16:24], table1_send], axis=0))
    att0 = PageSum(place, att0_keep, att0_send)

    layer1.tie(att0.sent)
    layer1.advance()
    mlp0.tie(layer1.sent)
    mlp0.advance()
    table0 = table_of(after(total0, mlp0.sent), base, row_back, col_map)
    x2_come = swap_head(after(x2_send, mlp0.sent))
    sums = jnp.concatenate(
        [
            shared + come[:24],
            small_att1[12:16] + come[24:28],
            small_att0[12:20],
            small_mlp1[:4],
            table0,
            table1 + come[32:48],
        ],
        axis=0,
    )
    sums = jnp.pad(sums.astype(BF16), ((0, SMALLS - sums.shape[0]), (0, 0)))
    sums_keep = lax.dynamic_slice_in_dim(sums, col * (SMALLS // 2), SMALLS // 2, 0)
    sums_send = lax.dynamic_slice_in_dim(sums, (1 - col) * (SMALLS // 2), SMALLS // 2, 0)
    sums_come = exchange(sums_send, 0)
    sums_keep, sums_come, x2_come = settle((att0, mlp0, layer1), (sums_keep, sums_come, x2_come))

    att0.kept = jnp.concatenate([att0.kept, sums_keep], axis=0)
    att0.come = jnp.concatenate([att0.come, sums_come], axis=0)
    att0.advance()
    mlp0.advance()
    layer1.advance()
    x2_move, x2_stay = run_kernel(
        last_entry_kernel,
        [far(x2_keep), x2_come, far(middle1), row_fc2[1]],
        [rows_bf(4 * QUAD)] * 2,
        [pltpu.VMEM((TILE, WIDTH), F32)],
    )
    x2_come = lax.ppermute(after(x2_move, layer1.sent), "band", band_down)
    (x2_come,) = settle((att0, mlp0, layer1), (x2_come,))

    att0.advance()
    mlp0.advance()
    layer1.advance()
    x2_edge = jnp.concatenate([x2_come[3 * QUAD :], x2_stay[3 * QUAD :]], axis=0)
    x2_far = lax.ppermute(x2_edge, ("col", "head"), edge_right)
    (x2_far,) = settle((att0, mlp0, layer1), (x2_far,))

    att0.advance()
    mlp0.advance()
    layer1.advance()
    x2_edge = jnp.where(head == 1, x2_far, x2_edge)
    other = swap_head(jnp.concatenate([first_send, x2_edge], axis=0))
    (other,) = settle((att0, mlp0, layer1), (other,))

    att0.advance()
    mlp0.advance()
    layer1.advance()
    grad_in = run_kernel(
        last_kernel,
        [place, whole, gain[0][0], first_keep, other, kept0],
        [shape_of((WIN, 2 * WIN, WIDTH), F32)],
        [pltpu.VMEM((TILE, WIDTH), F32)],
        specs={0: SMEM},
    )[0]
    act_out = run_kernel(
        leave_kernel,
        [other, x2_stay, x2_come],
        [shape_of((WIN, 2 * WIN, WIDTH), F32)],
        [pltpu.VMEM((TILE, WIDTH), F32)],
    )[0]
    settle((att0, mlp0, layer1), (grad_in, act_out))

    att0.advance()
    mlp0.advance()
    layer1.advance()
    settle((att0, mlp0, layer1))

    shapes = [(2, 512, 768), (2, 256, 512), (2, 512, 1024), (2, 1024, 512)]
    outs = [shape_of(shape, F32) for shape in shapes]
    anywhere = pl.BlockSpec(memory_space=pl.ANY)
    att0.advance()
    mlp0.advance()
    settle((att0, mlp0))

    att0.advance()
    g_qkv, g_proj, g_fc1, g_fc2 = run_kernel(
        unpack_layer_kernel,
        [place, *layer1.halves],
        outs,
        [pltpu.VMEM((ROWS_ATT, 256), BF16), pltpu.VMEM((ROWS_MLP, 256), BF16)],
        specs={0: SMEM},
        out_specs=[layer_spec(out, 1) for out in outs],
    )
    g_fc1, g_fc2 = run_kernel(
        unpack_mlp_kernel,
        [place, *mlp0.halves, g_fc1, g_fc2],
        outs[2:],
        [pltpu.VMEM((ROWS_MLP, 256), BF16)],
        specs={0: SMEM, 3: anywhere, 4: anywhere},
        out_specs=[layer_spec(out, 0) for out in outs[2:]],
        aliases={3: 0, 4: 1},
    )
    g_qkv, g_proj, g_gain, g_bias, g_qv, g_table, g_bproj, g_bfc1, g_bfc2 = run_kernel(
        unpack_last_kernel,
        [place, *att0.halves, order_qv, g_qkv, g_proj],
        outs[:2]
        + [
            shape_of(array.shape, F32)
            for array in (ln_gain, ln_bias, b_qv, rel_table.transpose(0, 2, 1), b_proj, b_fc1, b_fc2)
        ],
        [pltpu.VMEM((ROWS_ATT, 256), BF16), pltpu.VMEM((SMALLS, 256), F32)],
        specs={0: SMEM, 4: pl.BlockSpec(memory_space=pl.ANY), 5: pl.BlockSpec(memory_space=pl.ANY)},
        out_specs=[layer_spec(out, 0) for out in outs[:2]] + [VMEM] * 7,
        aliases={4: 0, 5: 1},
    )
    g_table = g_table.transpose(0, 2, 1)
    return (
        act_out, grad_in, g_gain, g_bias, g_qkv, g_qv, g_table, g_proj, g_bproj, g_fc1, g_bfc1, g_fc2, g_bfc2,
    )


def fits(mesh):
    return dict(mesh.shape) == {"band": 8, "col": 2, "head": 2}


def solution(mesh):
    placed = (
        P("band", ("col", "head"), None),
        P(),
        P(),
        P(None, None, "head"),
        P(None, "head"),
        P(None, None, "head"),
        P(None, "head", None),
        P(),
        P(None, None, "head"),
        P(None, "head"),
        P(None, "head", None),
        P(),
        P("band", ("col", "head"), None),
    )
    return jax.shard_map(
        fast_device if fits(mesh) else on_device,
        mesh=mesh,
        in_specs=placed,
        out_specs=(
            P("band", ("col", "head"), None),
            P("band", ("col", "head"), None),
            P(),
            P(),
            P(None, None, "head"),
            P(None, "head"),
            P(None, None, "head"),
            P(None, "head", None),
            P(),
            P(None, None, "head"),
            P(None, "head"),
            P(None, "head", None),
            P(),
        ),
        check_vma=False,
    )
```

```python
from functools import partial

import jax
import jax.numpy as jnp
import numpy as np
from jax import lax
from jax.experimental import pallas as pl
from jax.experimental.pallas import tpu as pltpu
from jax.sharding import PartitionSpec as P

HEAD_DIM = 32
WIN = 10
SHIFT = 5
BLOCKS = 2


EPSILON = 1e-05
HIGHEST = lax.Precision.HIGHEST


def shifted_2(value, axis, steps):
    count = lax.axis_size(axis)
    pairs = [(source, (source + steps) % count) for source in range(count)]
    return lax.ppermute(value, axis, pairs)


def layer_norm(array, gain_row, bias_row):
    centre = array - jnp.mean(array, axis=-1, keepdims=True)
    spread = jnp.mean(centre * centre, axis=-1, keepdims=True)
    return centre * lax.rsqrt(spread + EPSILON) * gain_row + bias_row


def offsets(window):
    places = jnp.arange(window, dtype=jnp.int32)
    spread = jnp.arange(2 * window - 1, dtype=jnp.int32)
    return (
        spread[None, None, :] == places[:, None, None] - places[None, :, None] + window - 1
    ).astype(jnp.float32)


def position_bias(table):
    head_count = table.shape[-1]
    table_grid = table.reshape(2 * WIN - 1, 2 * WIN - 1, head_count)
    onehot = offsets(WIN)
    full = jnp.einsum("ika,jlb,abh->hijkl", onehot, onehot, table_grid, precision=HIGHEST)
    return full.reshape(head_count, WIN * WIN, WIN * WIN)


def table_grad(grad_offset):
    head_count = grad_offset.shape[0]
    onehot = offsets(WIN)
    spread = grad_offset.reshape(head_count, WIN, WIN, WIN, WIN)
    full = jnp.einsum("ika,jlb,hijkl->abh", onehot, onehot, spread, precision=HIGHEST)
    return full.reshape((2 * WIN - 1) * (2 * WIN - 1), head_count)


def gather_tile(array):
    return lax.all_gather(array, "head", axis=1, tiled=True)


def sum_tile(array):
    return lax.psum_scatter(
        array.astype(jnp.bfloat16), "head", scatter_dimension=1, tiled=True
    ).astype(jnp.float32)


def gather_grad(array):
    return lax.all_gather(array, "head", axis=1, tiled=True)


def sum_grad(array):
    return lax.psum_scatter(
        array.astype(jnp.bfloat16), "head", scatter_dimension=1, tiled=True
    ).astype(jnp.float32)


def roll_ahead(array):
    upper = shifted_2(array[:SHIFT], "band", -1)
    array = jnp.concatenate([array[SHIFT:], upper], axis=0)
    leftmost = shifted_2(array[:, :SHIFT], ("col", "head"), -1)
    return jnp.concatenate([array[:, SHIFT:], leftmost], axis=1)


def roll_behind(array):
    lower = shifted_2(array[-SHIFT:], "band", 1)
    array = jnp.concatenate([lower, array[:-SHIFT]], axis=0)
    rightmost = shifted_2(array[:, -SHIFT:], ("col", "head"), 1)
    return jnp.concatenate([rightmost, array[:, :-SHIFT]], axis=1)


def pack_members(members):
    group = lax.axis_size("band") * lax.axis_size("col")
    flat = jnp.concatenate([member.reshape(-1) for member in members])
    padding = -flat.shape[0] % group
    return jnp.concatenate([flat, jnp.zeros((padding,), jnp.float32)])


def unpack_members(flat, members):
    result = []
    start = 0
    for member in members:
        count = member.size
        result.append(flat[start : start + count].reshape(member.shape))
        start = start + count
    return tuple(result)


def to_windows(tile_rows):
    height, breadth, depth = tile_rows.shape
    window_count = breadth // height
    split = tile_rows.reshape(height, window_count, height, depth).transpose(1, 0, 2, 3)
    return split.reshape(window_count * height * height, depth)


def from_windows(flat_rows, height):
    window_count = flat_rows.shape[0] // (height * height)
    depth = flat_rows.shape[1]
    split = flat_rows.reshape(window_count, height, height, depth).transpose(1, 0, 2, 3)
    return split.reshape(height, window_count * height, depth)


def region_ids(places, extent):
    return (places >= extent - WIN).astype(jnp.int32) + (places >= extent - SHIFT).astype(jnp.int32)


def shift_mask(breadth):
    rows_all = WIN * lax.axis_size("band")
    cols_all = breadth * lax.axis_size("col")
    rows_here = WIN * lax.axis_index("band") + jnp.arange(WIN, dtype=jnp.int32)
    cols_here = breadth * lax.axis_index("col") + jnp.arange(breadth, dtype=jnp.int32)
    region = 3 * region_ids(rows_here, rows_all)[:, None] + region_ids(cols_here, cols_all)[None, :]
    window_count = breadth // WIN
    labels = to_windows(region[:, :, None])[:, 0].reshape(window_count, WIN * WIN)
    return jnp.where(labels[:, :, None] != labels[:, None, :], -100.0, 0.0).astype(jnp.float32)


def scores(queries, key_rows, offset, region_mask):
    logits = jnp.einsum("wqhd,wkhd->whqk", queries, key_rows, preferred_element_type=jnp.float32)
    logits = logits * HEAD_DIM ** (-0.5) + offset[None]
    if region_mask is not None:
        logits = logits + region_mask[:, None]
    return logits


def forward_block(source, weights, shifted):
    norm_gain, norm_bias, w_qkv, b_qv, table, w_proj, b_proj, w_fc1, b_fc1, w_fc2, b_fc2 = weights
    height = source.shape[0]
    heads_here = table.shape[-1]
    normed = layer_norm(source, norm_gain[0], norm_bias[0]).astype(jnp.bfloat16)
    if shifted:
        normed = roll_ahead(normed)
    gathered = gather_tile(normed)
    window_count = gathered.shape[1] // height
    flat_rows = to_windows(gathered)
    projected = jnp.dot(flat_rows, w_qkv, preferred_element_type=jnp.float32)
    projected = projected.reshape(window_count, height * height, heads_here, 3, HEAD_DIM)
    qv_bias = b_qv.reshape(heads_here, 2, HEAD_DIM)
    queries = (projected[..., 0, :] + qv_bias[:, 0]).astype(jnp.bfloat16)
    key_rows = projected[..., 1, :].astype(jnp.bfloat16)
    values = (projected[..., 2, :] + qv_bias[:, 1]).astype(jnp.bfloat16)
    offset = position_bias(table)
    region_mask = shift_mask(gathered.shape[1]) if shifted else None
    logits = scores(queries, key_rows, offset, region_mask)
    log_total = jax.nn.logsumexp(logits, axis=-1)
    probs_low = jnp.exp(logits - log_total[..., None]).astype(jnp.bfloat16)
    context = jnp.einsum("whqk,wkhd->wqhd", probs_low, values, preferred_element_type=jnp.float32)
    context = context.astype(jnp.bfloat16).reshape(
        window_count * height * height, heads_here * HEAD_DIM
    )
    partial_out = from_windows(jnp.dot(context, w_proj, preferred_element_type=jnp.float32), height)
    branch = sum_tile(partial_out) + b_proj
    if shifted:
        branch = roll_behind(branch.astype(jnp.bfloat16)).astype(jnp.float32)
    middle = source + branch
    second = layer_norm(middle, norm_gain[1], norm_bias[1]).astype(jnp.bfloat16)
    second_tile = gather_tile(second)
    mlp_rows = second_tile.reshape(-1, second_tile.shape[-1])
    hidden = jnp.dot(mlp_rows, w_fc1, preferred_element_type=jnp.float32) + b_fc1
    active = jax.nn.gelu(hidden, approximate=False).astype(jnp.bfloat16)
    out_part = jnp.dot(active, w_fc2, preferred_element_type=jnp.float32).reshape(second_tile.shape)
    result = middle + sum_tile(out_part) + b_fc2
    saved_state = (
        source,
        middle,
        flat_rows,
        queries,
        key_rows,
        values,
        log_total,
        context,
        mlp_rows,
        hidden,
        offset,
        region_mask,
    )
    return (result, saved_state)


def backward_block(upstream, weights, saved_state, shifted):
    norm_gain, norm_bias, w_qkv, b_qv, table, w_proj, b_proj, w_fc1, b_fc1, w_fc2, b_fc2 = weights
    (
        source,
        middle,
        flat_rows,
        queries,
        key_rows,
        values,
        log_total,
        context,
        mlp_rows,
        hidden,
        offset,
        region_mask,
    ) = saved_state
    height = source.shape[0]
    window_count, window_len, heads_here, _ = queries.shape
    grad_low = upstream.astype(jnp.bfloat16)
    grad_tile = gather_grad(grad_low)
    grad_rows = grad_tile.reshape(-1, grad_tile.shape[-1])
    active = jax.nn.gelu(hidden, approximate=False).astype(jnp.bfloat16)
    g_fc2 = jnp.dot(active.T, grad_rows, preferred_element_type=jnp.float32)
    g_bfc2 = jnp.sum(grad_low.astype(jnp.float32), axis=(0, 1))
    g_active = jnp.dot(grad_rows, w_fc2.T, preferred_element_type=jnp.float32)
    g_hidden = jax.vjp(partial(jax.nn.gelu, approximate=False), hidden)[1](g_active)[0].astype(
        jnp.bfloat16
    )
    g_bfc1 = jnp.sum(g_hidden.astype(jnp.float32), axis=0)
    g_fc1 = jnp.dot(mlp_rows.T, g_hidden, preferred_element_type=jnp.float32)
    g_second = sum_grad(
        jnp.dot(g_hidden, w_fc1.T, preferred_element_type=jnp.float32).reshape(grad_tile.shape)
    )
    pull_second = jax.vjp(layer_norm, middle, norm_gain[1], norm_bias[1])[1]
    g_mid_norm, g_gain2, g_bias2 = pull_second(g_second)
    g_middle = upstream + g_mid_norm
    g_branch = g_middle.astype(jnp.bfloat16)
    if shifted:
        g_branch = roll_ahead(g_branch)
    g_bproj = jnp.sum(g_branch.astype(jnp.float32), axis=(0, 1))
    g_output = to_windows(gather_grad(g_branch))
    g_proj = jnp.dot(context.T, g_output, preferred_element_type=jnp.float32)
    g_context = jnp.dot(g_output, w_proj.T, preferred_element_type=jnp.float32).astype(jnp.bfloat16)
    g_context = g_context.reshape(window_count, window_len, heads_here, HEAD_DIM)
    logits = scores(queries, key_rows, offset, region_mask)
    probs = jnp.exp(logits - log_total[..., None])
    probs_low = probs.astype(jnp.bfloat16)
    g_values = jnp.einsum(
        "whqk,wqhd->wkhd", probs_low, g_context, preferred_element_type=jnp.float32
    ).astype(jnp.bfloat16)
    g_probs = jnp.einsum("wqhd,wkhd->whqk", g_context, values, preferred_element_type=jnp.float32)
    centre = jnp.sum(probs * g_probs, axis=-1, keepdims=True)
    g_logits = (probs * (g_probs - centre)).astype(jnp.bfloat16)
    g_table = table_grad(jnp.sum(g_logits.astype(jnp.float32), axis=0))
    inv_root = HEAD_DIM ** (-0.5)
    g_queries = (
        jnp.einsum("whqk,wkhd->wqhd", g_logits, key_rows, preferred_element_type=jnp.float32)
        * inv_root
    ).astype(jnp.bfloat16)
    g_keys = (
        jnp.einsum("whqk,wqhd->wkhd", g_logits, queries, preferred_element_type=jnp.float32)
        * inv_root
    ).astype(jnp.bfloat16)
    g_mixed = jnp.stack([g_queries, g_keys, g_values], axis=3).reshape(
        window_count * window_len, heads_here * 3 * HEAD_DIM
    )
    g_bqv = jnp.stack(
        [
            jnp.sum(g_queries.astype(jnp.float32), axis=(0, 1)),
            jnp.sum(g_values.astype(jnp.float32), axis=(0, 1)),
        ],
        axis=1,
    ).reshape(-1)
    g_qkv = jnp.dot(flat_rows.T, g_mixed, preferred_element_type=jnp.float32)
    g_first = sum_grad(
        from_windows(jnp.dot(g_mixed, w_qkv.T, preferred_element_type=jnp.float32), height)
    )
    if shifted:
        g_first = roll_behind(g_first.astype(jnp.bfloat16)).astype(jnp.float32)
    pull_first = jax.vjp(layer_norm, source, norm_gain[0], norm_bias[0])[1]
    g_source, g_gain1, g_bias1 = pull_first(g_first)
    g_input = g_middle + g_source
    sharded = (g_qkv, g_bqv, g_table, g_proj, g_fc1, g_bfc1, g_fc2)
    shared = (jnp.stack([g_gain1, g_gain2]), jnp.stack([g_bias1, g_bias2]), g_bproj, g_bfc2)
    return (g_input, sharded, shared)


def on_device(
    act_in,
    ln_gain,
    ln_bias,
    w_qkv,
    b_qv,
    rel_table,
    w_proj,
    b_proj,
    w_fc1,
    b_fc1,
    w_fc2,
    b_fc2,
    grad_out,
):
    params = (ln_gain, ln_bias, w_qkv, b_qv, rel_table, w_proj, b_proj, w_fc1, b_fc1, w_fc2, b_fc2)
    layers = [tuple((member[block_id] for member in params)) for block_id in range(BLOCKS)]
    residual = act_in.astype(jnp.float32)
    layer_inputs = []
    stored = []
    for block_id in range(BLOCKS):
        layer_inputs.append(residual)
        residual, saved_state = forward_block(residual, layers[block_id], block_id % 2 == 1)
        stored.append(saved_state)
    upstream = grad_out
    sharded_all = [None] * BLOCKS
    shared_all = [None] * BLOCKS
    for block_id in reversed(range(BLOCKS)):
        saved_state = forward_block(layer_inputs[block_id], layers[block_id], block_id % 2 == 1)[1]
        upstream, sharded, shared = backward_block(
            upstream, layers[block_id], saved_state, block_id % 2 == 1
        )
        sharded_all[block_id] = sharded
        shared_all[block_id] = shared
    sharded_stack = tuple(
        (jnp.stack([entry[member] for entry in sharded_all]) for member in range(7))
    )
    shared_stack = tuple(
        (jnp.stack([entry[member] for entry in shared_all]) for member in range(4))
    )
    packed_all = pack_members(sharded_stack)
    packed_part = lax.psum_scatter(
        packed_all.astype(jnp.bfloat16), ("band", "col"), scatter_dimension=0, tiled=True
    ).astype(jnp.float32)
    packed_all = lax.all_gather(
        packed_part.astype(jnp.bfloat16), ("band", "col"), axis=0, tiled=True
    ).astype(packed_part.dtype)
    sharded_stack = unpack_members(packed_all, sharded_stack)
    shared_stack = lax.psum(shared_stack, ("band", "col", "head"))
    return (
        residual,
        upstream,
        shared_stack[0],
        shared_stack[1],
        sharded_stack[0],
        sharded_stack[1],
        sharded_stack[2],
        sharded_stack[3],
        shared_stack[2],
        sharded_stack[4],
        sharded_stack[5],
        sharded_stack[6],
        shared_stack[3],
    )


F32 = jnp.float32
BF16 = jnp.bfloat16
WIDTH = 512
QUAD = 32
LIVE = SHIFT * SHIFT
UNIT = 2 * QUAD
TOK = 2 * UNIT
TILE = 4 * UNIT
PAIR = 2 * TILE
GROUP = 8
SPAN = GROUP * HEAD_DIM
KEYS = GROUP * TOK
OFFSETS = 2 * WIN - 1
ENTRIES = 384
SCALE = HEAD_DIM ** (-0.5)
FAR = -1e30
ROOT_HALF = 0.5 ** 0.5
ROOT_TWO_PI = (2.0 * np.pi) ** (-0.5)
VMEM = pl.BlockSpec(memory_space=pltpu.VMEM)
SMEM = pl.BlockSpec(memory_space=pltpu.SMEM)
ROWS_QKV = 3 * 512
ROWS_ATT = ROWS_QKV + 512
ROWS_MLP = 4096
HALF_ATT = ROWS_ATT // 2
HEAD, COL, NEAR = 0, 1, 5
QUARTER_ATT = HALF_ATT // 2
EIGHTH = HALF_ATT // 8


def shape_of(shape, kind):
    return jax.ShapeDtypeStruct(shape, kind)


def layer_spec(array, layer):
    rest = array.shape[1:]
    return pl.BlockSpec((1,) + rest, lambda _: (layer,) + (0,) * len(rest), pipeline_mode=pl.Buffered(1))


COSTS = {
    "attention_plain_kernel": 6.0,
    "mlp_plain_kernel": 4.5,
    "attention_shifted_kernel": 5.5,
    "mlp_shifted_kernel": 5.0,
    "attention_shifted_back_kernel": 6.0,
    "mlp_plain_back_kernel": 2.0,
    "attention_plain_back_kernel": 6.0,
    "mlp_weights_kernel": 2.0,
    "attention_weights_plain_kernel": 2.0,
    "attention_weights_shifted_kernel": 2.7,
    "table_kernel": 1.2,
    "bias_body": 1.2,
    "pack_kernel": 1.5,
    "unpack_mlp_kernel": 3.0,
    "unpack_layer_kernel": 5.0,
    "unpack_last_kernel": 2.5,
}


def run_kernel(kernel, operands, outs, scratch=(), limit=24, specs=None, aliases=None, out_specs=None):
    specs = specs or {}
    name = getattr(kernel, "func", kernel).__name__
    in_specs = [specs.get(place, VMEM) for place in range(len(operands))]
    return pl.pallas_call(
        kernel,
        grid=(1,),
        in_specs=in_specs,
        out_specs=out_specs or [VMEM] * len(outs),
        out_shape=list(outs),
        scratch_shapes=list(scratch),
        input_output_aliases=aliases or {},
        cost_estimate=pl.CostEstimate(
            flops=int(COSTS.get(name, 0.7) * 4.6e9), bytes_accessed=1 << 10, transcendentals=0
        ),
        compiler_params=pltpu.CompilerParams(vmem_limit_bytes=limit << 20),
        name=name,
    )(*operands)


def mm(left, right):
    return lax.dot_general(left, right, (((1,), (0,)), ((), ())), preferred_element_type=F32)


def mm_nt(left, right):
    return lax.dot_general(left, right, (((1,), (1,)), ((), ())), preferred_element_type=F32)


def mm_tn(left, right):
    return lax.dot_general(left, right, (((0,), (0,)), ((), ())), preferred_element_type=F32)


def halves_of(value):
    high = value.astype(BF16)
    return high, (value - high.astype(F32)).astype(BF16)


def norm_parts(value):
    centre = value - jnp.mean(value, axis=-1, keepdims=True)
    inverse = lax.rsqrt(jnp.mean(centre * centre, axis=-1, keepdims=True) + EPSILON)
    return centre * inverse, inverse


def norm_back(grad, gain, unit, inverse):
    scaled = grad * gain
    return (
        scaled
        - jnp.mean(scaled, axis=-1, keepdims=True)
        - unit * jnp.mean(scaled * unit, axis=-1, keepdims=True)
    ) * inverse


def column_sum(value):
    return jnp.sum(value, axis=0, keepdims=True)


def put_row(ref, row, value):
    for part in range(value.shape[1] // 256):
        ref[row + part : row + part + 1, :] = value[:, 256 * part : 256 * (part + 1)]


def token_place(row, col):
    return ((col // SHIFT) * 2 + row // SHIFT) * QUAD + (row % SHIFT) * SHIFT + col % SHIFT


def constants():
    row_map = np.zeros((TOK, 160), np.float32)
    col_map = np.zeros((TOK, TOK), np.float32)
    token_row = np.zeros((TOK,), np.int32)
    token_col = np.zeros((TOK,), np.int32)
    for row in range(WIN):
        for col in range(WIN):
            place = token_place(row, col)
            row_map[place, row * 16 + col] = 1.0
            col_map[row * WIN + col, place] = 1.0
            token_row[place] = row
            token_col[place] = col
    base = np.full((1, 256), -4000, np.int32)
    for lane in range(OFFSETS * WIN):
        base[0, lane] = (OFFSETS - 1 - lane // WIN) * OFFSETS - lane % WIN + WIN - 1
    order = np.zeros((768, 768), np.float32)
    for head in range(GROUP):
        for part in range(3):
            for place in range(HEAD_DIM):
                order[head * 96 + part * 32 + place, part * SPAN + head * HEAD_DIM + place] = 1.0
    heads = np.zeros((KEYS, SPAN), np.float32)
    for head in range(GROUP):
        heads[head * TOK : (head + 1) * TOK, head * HEAD_DIM : (head + 1) * HEAD_DIM] = 1.0
    order_qv = np.zeros((2 * SPAN, 2 * SPAN), np.float32)
    for head in range(GROUP):
        for part in range(2):
            for place in range(HEAD_DIM):
                order_qv[part * SPAN + head * HEAD_DIM + place, (2 * head + part) * HEAD_DIM + place] = 1.0
    return (
        jnp.asarray(row_map, BF16),
        jnp.asarray(row_map.T, BF16),
        jnp.asarray(col_map, BF16),
        jnp.asarray(base),
        jnp.asarray(order, BF16),
        jnp.asarray(heads, BF16),
        jnp.asarray(order_qv, BF16),
        token_row,
        token_col,
    )


def enter_rows(in_ref, buf, start):
    for row in range(WIN):
        line = in_ref[row].astype(F32)
        for unit in range(4):
            first = unit * UNIT + (row // SHIFT) * QUAD + (row % SHIFT) * SHIFT
            buf[start + first : start + first + SHIFT, :] = line[unit * SHIFT : (unit + 1) * SHIFT, :]


def enter_kernel(in_ref, out_ref, buf):
    buf[...] = jnp.zeros(buf.shape, F32)
    enter_rows(in_ref, buf, 0)
    out_ref[...] = buf[...].astype(BF16)


def enter_units(tile):
    return run_kernel(
        enter_kernel, [tile], [shape_of((TILE, WIDTH), BF16)], [pltpu.VMEM((TILE, WIDTH), F32)]
    )[0]


def leave_rows(value_ref, out_ref):
    for row in range(WIN):
        for unit in range(4):
            start = unit * UNIT + (row // SHIFT) * QUAD + (row % SHIFT) * SHIFT
            out_ref[row, unit * SHIFT : (unit + 1) * SHIFT, :] = value_ref[start : start + SHIFT, :]


def leave_kernel(first, stay, come, out_ref, buf):
    buf[0:UNIT, :] = first[TILE:, :].astype(F32)
    for unit in range(3):
        lines = slice(QUAD * unit, QUAD * (unit + 1))
        start = UNIT * (unit + 1)
        buf[start : start + QUAD, :] = come[lines, :].astype(F32)
        buf[start + QUAD : start + UNIT, :] = stay[lines, :].astype(F32)
    leave_rows(buf, out_ref)


def part_quads(value, upper, lower, units):
    for unit in range(units):
        lines = slice(QUAD * unit, QUAD * (unit + 1))
        upper[lines, :] = value[UNIT * unit : UNIT * unit + QUAD, :].astype(upper.dtype)
        lower[lines, :] = value[UNIT * unit + QUAD : UNIT * (unit + 1), :].astype(lower.dtype)


def join_quads(out, start, upper, lower, units):
    for unit in range(units):
        lines = slice(QUAD * unit, QUAD * (unit + 1))
        first = start + UNIT * unit
        out[first : first + QUAD, :] = upper[lines, :]
        out[first + QUAD : first + UNIT, :] = lower[lines, :]


def enter_entry_kernel(keep, come, tile, edge):
    value = (keep[...] + come[...].astype(F32)).astype(BF16)
    tile[...] = value
    edge[...] = value[3 * UNIT :, :]


def roll_ahead_kernel(place, tile, come, send, stay):
    part_quads(tile, send, stay, 3)
    taken = jnp.where(place[HEAD] == 1, come[...], tile[3 * UNIT :, :])
    send[3 * QUAD :, :] = taken[:QUAD, :]
    stay[3 * QUAD :, :] = taken[QUAD:, :]


def roll_back_kernel(place, stay_main, send_main, edge, come, send, stay):
    taken = jnp.where(place[HEAD] == 1, come[...], edge[...])
    stay[: 3 * QUAD, :] = stay_main[...]
    stay[3 * QUAD :, :] = taken[:QUAD, :]
    send[: 3 * QUAD, :] = send_main[...]
    send[3 * QUAD :, :] = taken[QUAD:, :]


def grad_enter_kernel(in_ref, send, stay, buf):
    buf[...] = jnp.zeros(buf.shape, F32)
    enter_rows(in_ref, buf, 0)
    part_quads(buf, send, stay, 4)


def grad_join_kernel(stay, come, out):
    join_quads(out, 0, stay, come, 4)


def last_entry_kernel(keep, come, middle, b_fc2, send, stay, buf):
    buf[...] = keep[...] + come[...].astype(F32) + middle[...] + b_fc2[...]
    part_quads(buf, stay, send, 4)


def entry_onehot(base_ref):
    entry = lax.broadcasted_iota(jnp.int32, (ENTRIES, 256), 0)
    return (entry == base_ref[...]).astype(F32).astype(BF16)


LINES = WIN * GROUP


def bias_body(table_ref, base_ref, row_map_ref, col_map_ref, out_ref, left, right, strip):
    table = table_ref[...]
    turned = jnp.concatenate([pltpu.roll(table, ENTRIES - col, 1) if col else table for col in range(WIN)], axis=0)
    high, low = halves_of(turned)
    onehot = entry_onehot(base_ref)
    spread = mm(high, onehot) + mm(low, onehot)
    left[0:LINES, :] = spread[:, :128]
    right[0:LINES, :] = spread[:, 128:]
    left[LINES:, :] = jnp.zeros((16 * GROUP - LINES, 128), F32)
    right[LINES:, :] = jnp.zeros((16 * GROUP - LINES, 128), F32)
    for head in range(GROUP):
        wide = jnp.concatenate(
            [left[pl.ds(head, 16, stride=GROUP), :], right[pl.ds(head, 16, stride=GROUP), :]], axis=1
        )
        for row in range(WIN):
            start = (WIN - 1 - row) * WIN
            strip[16 * row : 16 * (row + 1), TOK * head : TOK * (head + 1)] = wide[:, start : start + TOK]
    high, low = halves_of(strip[...])
    rows = mm(row_map_ref[...], high) + mm(row_map_ref[...], low)
    live = lax.broadcasted_iota(jnp.int32, (TOK, TOK), 1) % QUAD < LIVE
    for head in range(GROUP):
        high, low = halves_of(rows[:, TOK * head : TOK * (head + 1)])
        value = mm(high, col_map_ref[...]) + mm(low, col_map_ref[...])
        out_ref[:, TOK * head : TOK * (head + 1)] = jnp.where(live, value, FAR)


BIAS_SCRATCH = (
    pltpu.VMEM((16 * GROUP, 128), F32),
    pltpu.VMEM((16 * GROUP, 128), F32),
    pltpu.VMEM((160, KEYS), F32),
)


def table_body(sum_ref, base_ref, row_back_ref, col_map_ref, out_ref, row, left, right, strip):
    high, low = halves_of(sum_ref[...])
    turned = [
        mm_nt(high[:, TOK * head : TOK * (head + 1)], col_map_ref[...])
        + mm_nt(low[:, TOK * head : TOK * (head + 1)], col_map_ref[...])
        for head in range(GROUP)
    ]
    high, low = halves_of(jnp.concatenate(turned, axis=1))
    strip[...] = mm(row_back_ref[...], high) + mm(row_back_ref[...], low)
    for head in range(GROUP):
        total = jnp.zeros((16, 256), F32)
        for line in range(WIN):
            block = strip[16 * line : 16 * (line + 1), TOK * head : TOK * (head + 1)]
            wide = jnp.concatenate([block, jnp.zeros((16, 128), F32)], axis=1)
            start = (WIN - 1 - line) * WIN
            total = total + (pltpu.roll(wide, start, 1) if start else wide)
        left[pl.ds(head, 16, stride=GROUP), :] = total[:, :128]
        right[pl.ds(head, 16, stride=GROUP), :] = total[:, 128:]
    onehot = entry_onehot(base_ref)
    high, low = halves_of(jnp.concatenate([left[0:LINES, :], right[0:LINES, :]], axis=1))
    spread = mm_nt(high, onehot) + mm_nt(low, onehot)
    table = spread[0:GROUP, :]
    for col in range(1, WIN):
        table = table + pltpu.roll(spread[GROUP * col : GROUP * (col + 1), :], col, 1)
    out_ref[row : row + GROUP, :] = table[:, :256]
    out_ref[row + GROUP : row + 2 * GROUP, :] = jnp.concatenate(
        [table[:, 256:], jnp.zeros((GROUP, 128), F32)], axis=1
    )


def pack_kernel(place, w_qkv_ref, w_proj_ref, order_ref, first_ref, second_ref, part_ref):
    for layer, out_ref in enumerate((first_ref, second_ref)):
        mixed = mm(w_qkv_ref[layer], order_ref[...]).astype(BF16)
        for part in range(3):
            out_ref[512 * part : 512 * (part + 1), :] = mixed[:, 256 * part : 256 * (part + 1)]
        for part in range(2):
            out_ref[ROWS_QKV + 256 * part : ROWS_QKV + 256 * (part + 1), :] = w_proj_ref[
                layer, :, 256 * part : 256 * (part + 1)
            ]
    start = place[COL] * HALF_ATT + place[NEAR] * QUARTER_ATT
    part_ref[...] = second_ref[pl.ds(pl.multiple_of(start, QUARTER_ATT), QUARTER_ATT), :]


def pack_weights(place, w_qkv, w_proj, order):
    return run_kernel(
        pack_kernel,
        [place, w_qkv, w_proj, order],
        [pltpu.HBM((ROWS_ATT, 256), BF16)] * 2 + [shape_of((QUARTER_ATT, 256), BF16)],
        specs={0: SMEM},
    )


def join_pack(place_ref, mine, theirs, out):
    out[pl.ds(pl.multiple_of(place_ref[COL] * HALF_ATT, HALF_ATT), HALF_ATT), :] = mine[...]
    out[pl.ds(pl.multiple_of((1 - place_ref[COL]) * HALF_ATT, HALF_ATT), HALF_ATT), :] = theirs[...]


def bias_of(table, base, row_map, col_map):
    return run_kernel(
        bias_body,
        [table, base, row_map, col_map],
        [shape_of((TOK, KEYS), F32)],
        BIAS_SCRATCH,
    )[0]


def project(normed, pack_ref, qv_ref):
    parts = [mm(normed, pack_ref[512 * part : 512 * (part + 1), :]) for part in range(3)]
    return (
        (parts[0] + qv_ref[0:1, :]).astype(BF16),
        parts[1].astype(BF16),
        (parts[2] + qv_ref[1:2, :]).astype(BF16),
    )


def spread_heads(ref, value, heads_ref):
    for head in range(GROUP):
        lines = slice(TOK * head, TOK * (head + 1))
        ref[lines, :] = value * heads_ref[lines, :]


def attend(qkv_ref, base, bias_ref, region, heads_ref, probs_ref, probs_base, stack, wide):
    rows = pl.ds(base, TOK)
    spread_heads(stack, qkv_ref[rows, 256:512], heads_ref)
    logits = mm_nt(qkv_ref[rows, 0:256], stack[...])
    for head in range(GROUP):
        lanes = slice(TOK * head, TOK * (head + 1))
        score = logits[:, lanes] * SCALE + bias_ref[:, lanes]
        if region is not None:
            score = score + region
        grown = jnp.exp(score - jnp.max(score, axis=-1, keepdims=True))
        probs = (grown / jnp.sum(grown, axis=-1, keepdims=True)).astype(BF16)
        wide[:, lanes] = probs
        probs_ref[pl.ds(probs_base + TOK * head, TOK), :] = probs
    spread_heads(stack, qkv_ref[rows, 512:768], heads_ref)
    return mm(wide[...], stack[...]).astype(BF16)


def attend_back(qkv_ref, base, grad, heads_ref, probs_ref, probs_base, total_ref, stack, wide, tall, mixed_ref):
    rows = pl.ds(base, TOK)
    spread_heads(stack, qkv_ref[rows, 512:768], heads_ref)
    grad_probs = mm_nt(grad, stack[...])
    for head in range(GROUP):
        lanes = slice(TOK * head, TOK * (head + 1))
        probs = probs_ref[pl.ds(probs_base + TOK * head, TOK), :].astype(F32)
        part = grad_probs[:, lanes]
        centre = jnp.sum(probs * part, axis=-1, keepdims=True)
        inner = (probs * (part - centre)).astype(BF16)
        wide[:, lanes] = inner
        tall[lanes, :] = inner
        total_ref[:, lanes] = total_ref[:, lanes] + inner.astype(F32)
    spread_heads(stack, grad, heads_ref)
    mixed_ref[rows, 512:768] = mm_tn(probs_ref[pl.ds(probs_base, KEYS), :], stack[...]).astype(BF16)
    spread_heads(stack, qkv_ref[rows, 256:512], heads_ref)
    mixed_ref[rows, 0:256] = (mm(wide[...], stack[...]) * SCALE).astype(BF16)
    spread_heads(stack, qkv_ref[rows, 0:256], heads_ref)
    mixed_ref[rows, 256:512] = (mm_tn(tall[...], stack[...]) * SCALE).astype(BF16)


def project_out(context, pack_ref):
    return jnp.concatenate(
        [mm(context, pack_ref[ROWS_QKV + 256 * part : ROWS_QKV + 256 * (part + 1), :]) for part in range(2)],
        axis=1,
    )


def project_out_back(grad, pack_ref):
    return (
        mm_nt(grad[:, :256], pack_ref[ROWS_QKV : ROWS_QKV + 256, :])
        + mm_nt(grad[:, 256:], pack_ref[ROWS_QKV + 256 : ROWS_ATT, :])
    ).astype(BF16)


def project_back(mixed_ref, pack_ref):
    total = mm_nt(mixed_ref[:, 0:256], pack_ref[0:512, :])
    for part in range(1, 3):
        total = total + mm_nt(mixed_ref[:, 256 * part : 256 * (part + 1)], pack_ref[512 * part : 512 * (part + 1), :])
    return total


ATTEND_SCRATCH = (pltpu.VMEM((KEYS, SPAN), BF16), pltpu.VMEM((TOK, KEYS), BF16))


def attention_plain_kernel(
    place_ref, own, other, gain, bias, pack, qv, offset, heads,
    whole, normed_out, qkv, probs, context, part_out, stack, wide, buf,
):
    here = place_ref[HEAD]
    buf[...] = jnp.zeros(buf.shape, F32)
    enter_rows(own, buf, 0)
    enter_rows(other, buf, TILE)
    whole[pl.ds(pl.multiple_of(here * TILE, TILE), TILE), :] = buf[:TILE, :].astype(BF16)
    whole[pl.ds(pl.multiple_of((1 - here) * TILE, TILE), TILE), :] = buf[TILE:, :].astype(BF16)
    unit, _ = norm_parts(whole[...].astype(F32))
    normed_out[...] = (unit * gain[...] + bias[...]).astype(BF16)
    for part, value in enumerate(project(normed_out[...], pack, qv)):
        qkv[:, 256 * part : 256 * (part + 1)] = value

    def window(place, carry):
        base = pl.multiple_of(place * TOK, TOK)
        context[pl.ds(base, TOK), :] = attend(
            qkv, base, offset, None, heads, probs, pl.multiple_of(place * KEYS, KEYS), stack, wide
        )
        return carry

    lax.fori_loop(0, PAIR // TOK, window, 0)
    part_out[...] = project_out(context[...], pack).astype(BF16)


def attention_shifted_kernel(
    place_ref, stay, come, gain, bias, gain2, bias2, pack_a, pack_mine, pack_theirs, qv_a, qv_b, off_a, off_b,
    ids_q, ids_k, heads, b_proj,
    keep, normed_out, qkv_a, qkv_b, probs_a, probs_b, context_a, context_b, middle_out, second_out, stack, wide,
    pack_b,
):
    join_pack(place_ref, pack_mine, pack_theirs, pack_b)
    join_quads(keep, 0, stay, come, 4)
    unit, _ = norm_parts(keep[...].astype(F32))
    normed_out[...] = (unit * gain[...] + bias[...]).astype(BF16)
    total = keep[...].astype(F32) + b_proj[...]
    for pack, qv, off, qkv, probs, context in (
        (pack_a, qv_a, off_a, qkv_a, probs_a, context_a),
        (pack_b, qv_b, off_b, qkv_b, probs_b, context_b),
    ):
        for part, value in enumerate(project(normed_out[...], pack, qv)):
            qkv[:, 256 * part : 256 * (part + 1)] = value

        def window(place, carry):
            base = pl.multiple_of(place * TOK, TOK)
            region = jnp.where(ids_q[pl.ds(base, TOK), :] != ids_k[place], -100.0, 0.0)
            context[pl.ds(base, TOK), :] = attend(
                qkv, base, off, region, heads, probs, pl.multiple_of(place * KEYS, KEYS), stack, wide
            )
            return carry

        lax.fori_loop(0, TILE // TOK, window, 0)
        total = total + project_out(context[...], pack)
    middle_out[...] = total
    unit, _ = norm_parts(total)
    second_out[...] = (unit * gain2[...] + bias2[...]).astype(BF16)


def gelu_parts(hidden):
    chance = 0.5 * (1.0 + lax.erf(hidden * ROOT_HALF))
    slope = chance + hidden * (jnp.exp(-0.5 * hidden * hidden) * ROOT_TWO_PI)
    return (hidden * chance).astype(BF16), slope.astype(BF16)


CHUNK = 256


def mlp_plain_kernel(
    place_ref, whole, part_own, part_other, b_proj, gain, bias, w_fc1, b_fc1, w_fc2, b_fc2,
    middle, second, active, slope, keep, send, spun,
):
    here = place_ref[HEAD]
    middle[...] = (
        whole[...].astype(F32) + (part_own[...].astype(F32) + part_other[...].astype(F32)) + b_proj[...]
    )
    unit, _ = norm_parts(middle[...])
    second[...] = (unit * gain[...] + bias[...]).astype(BF16)
    for place in range(1024 // CHUNK):
        lanes = slice(CHUNK * place, CHUNK * (place + 1))
        hidden = mm(second[...], w_fc1[0, :, lanes]) + b_fc1[:, lanes]
        active[:, lanes], slope[:, lanes] = gelu_parts(hidden)
    out = mm(active[...], w_fc2[0])
    spun[0 : PAIR - UNIT, :] = out[UNIT:, :]
    spun[PAIR - UNIT :, :] = out[:UNIT, :]
    send[...] = spun[pl.ds((1 - here) * TILE, TILE), :].astype(BF16)
    spun[0 : PAIR - UNIT, :] = spun[0 : PAIR - UNIT, :] + middle[UNIT:, :]
    spun[PAIR - UNIT :, :] = spun[PAIR - UNIT :, :] + middle[:UNIT, :]
    keep[...] = spun[pl.ds(here * TILE, TILE), :] + b_fc2[...]


def mlp_shifted_kernel(
    place_ref, own, other, grad_own, grad_other, grad_far, w_fc1, b_fc1, w_fc2,
    second, grad, active, inner, keep, send, back_keep, back_send, small, slope, spun,
):
    here = place_ref[HEAD]
    mine = pl.ds(pl.multiple_of(here * TILE, TILE), TILE)
    theirs = pl.ds(pl.multiple_of((1 - here) * TILE, TILE), TILE)
    spun[mine, :] = grad_own[...]
    spun[theirs, :] = grad_other[...]
    grad[0 : 7 * UNIT, :] = spun[UNIT:, :]
    grad[7 * UNIT :, :] = grad_far[...]
    second[mine, :] = own[...]
    second[theirs, :] = other[...]
    for place in range(1024 // CHUNK):
        lanes = slice(CHUNK * place, CHUNK * (place + 1))
        hidden = mm(second[...], w_fc1[0, :, lanes]) + b_fc1[:, lanes]
        active[:, lanes], slope[:, lanes] = gelu_parts(hidden)
    for place in range(1024 // CHUNK):
        lanes = slice(CHUNK * place, CHUNK * (place + 1))
        back = mm_nt(grad[...], w_fc2[0, lanes, :]) * slope[:, lanes].astype(F32)
        inner[:, lanes] = back.astype(BF16)
    back_keep[...] = mm_nt(inner[mine, :], w_fc1[0])
    back_send[...] = mm_nt(inner[theirs, :], w_fc1[0]).astype(BF16)
    keep[...] = mm(active[mine, :], w_fc2[0])
    send[...] = mm(active[theirs, :], w_fc2[0]).astype(BF16)
    put_row(small, 0, column_sum(inner[...].astype(F32)))
    small[4:, :] = jnp.zeros((4, 256), F32)


def mlp_plain_back_kernel(
    place_ref, own, other, slope, w_fc1, w_fc2,
    grad, inner, back, spun,
):
    for which, value in enumerate((own, other)):
        here = place_ref[HEAD] if which == 0 else 1 - place_ref[HEAD]
        start = pl.multiple_of(here * TILE, TILE)
        for unit in range(4):
            lines = slice(QUAD * unit, QUAD * (unit + 1))
            spun[pl.ds(start + UNIT * unit, QUAD), :] = value[4 * QUAD + QUAD * unit : 4 * QUAD + QUAD * (unit + 1), :]
            spun[pl.ds(start + UNIT * unit + QUAD, QUAD), :] = value[lines, :]
    grad[0:UNIT, :] = spun[PAIR - UNIT :, :]
    grad[UNIT:, :] = spun[0 : PAIR - UNIT, :]
    for place in range(1024 // CHUNK):
        lanes = slice(CHUNK * place, CHUNK * (place + 1))
        value = mm_nt(grad[...], w_fc2[0, lanes, :]) * slope[:, lanes].astype(F32)
        inner[:, lanes] = value.astype(BF16)
    back[...] = mm_nt(inner[...], w_fc1[0]).astype(BF16)


def deal_halves(place_ref, whole, keep, send, half, base=0, start=0):
    mine = pl.multiple_of(place_ref[COL] * half, half)
    theirs = pl.multiple_of((1 - place_ref[COL]) * half, half)
    keep[start : start + half, :] = whole[pl.ds(base + mine, half), :]
    send[start : start + half, :] = whole[pl.ds(base + theirs, half), :]


def mlp_weights_kernel(place_ref, second, active, grad, inner, keep, send, out):
    for place in range(4):
        lanes = slice(256 * place, 256 * (place + 1))
        out[512 * place : 512 * (place + 1), :] = mm_tn(second[...], inner[:, lanes]).astype(BF16)
    for place in range(2):
        lanes = slice(256 * place, 256 * (place + 1))
        start = 2048 + 1024 * place
        out[start : start + 1024, :] = mm_tn(active[...], grad[:, lanes]).astype(BF16)
    deal_halves(place_ref, out, keep, send, ROWS_MLP // 2)


def mlp_weights(place, second, active, grad, inner):
    return run_kernel(
        mlp_weights_kernel,
        [place, second, active, grad, inner],
        [shape_of((ROWS_MLP // 2, 256), BF16)] * 2,
        [pltpu.VMEM((ROWS_MLP, 256), BF16)],
        specs={0: SMEM},
    )


def attention_shifted_back_kernel(
    place_ref, grad_all, back_own, back_other, middle, entry, gain, gain2, qkv_a, qkv_b, probs_a, probs_b,
    pack_a, pack_mine, pack_theirs, heads,
    grad_low, mixed_a, mixed_b, total_a, total_b, stay_main, send_main, edge, small,
    stack, wide, tall, grad_context, below, pack_b,
):
    join_pack(place_ref, pack_mine, pack_theirs, pack_b)
    here = place_ref[HEAD]
    upstream = grad_all[pl.ds(pl.multiple_of(here * TILE, TILE), TILE), :].astype(F32)
    back = back_own[...] + back_other[...].astype(F32)
    unit, inverse = norm_parts(middle[...])
    put_row(small, 0, column_sum(back * unit))
    put_row(small, 2, column_sum(back))
    put_row(small, 4, column_sum(upstream))
    grad_middle = upstream + norm_back(back, gain2[...], unit, inverse)
    grad_low[...] = grad_middle.astype(BF16)
    put_row(small, 6, column_sum(grad_low[...].astype(F32)))
    first = jnp.zeros((TILE, WIDTH), F32)
    for pack, qkv, probs, mixed, total in (
        (pack_a, qkv_a, probs_a, mixed_a, total_a),
        (pack_b, qkv_b, probs_b, mixed_b, total_b),
    ):
        grad_context[...] = project_out_back(grad_low[...], pack)
        total[...] = jnp.zeros((TOK, KEYS), F32)

        def window(place, carry):
            base = pl.multiple_of(place * TOK, TOK)
            attend_back(
                qkv, base, grad_context[pl.ds(base, TOK), :], heads, probs, pl.multiple_of(place * KEYS, KEYS),
                total, stack, wide, tall, mixed,
            )
            return carry

        lax.fori_loop(0, TILE // TOK, window, 0)
        first = first + project_back(mixed, pack)
    unit, inverse = norm_parts(entry[...].astype(F32))
    put_row(small, 8, column_sum(first * unit))
    put_row(small, 10, column_sum(first))
    put_row(small, 12, column_sum(mixed_a[...].astype(F32)))
    small[15:16, :] = jnp.zeros((1, 256), F32)
    put_row(small, 16, column_sum(mixed_b[...].astype(F32)))
    small[19:24, :] = jnp.zeros((5, 256), F32)
    below[...] = grad_middle + norm_back(first, gain[...], unit, inverse)
    part_quads(below, stay_main, send_main, 3)
    edge[...] = below[3 * UNIT :, :].astype(BF16)


def attention_plain_back_kernel(
    place_ref, grad, back_own, back_other, middle, whole, gain, gain2, qkv, probs, pack, heads, inner,
    grad_low, mixed, total, first_keep, first_send, kept, small, stack, wide, tall, grad_context, first,
):
    here = place_ref[HEAD]
    mine = pl.ds(pl.multiple_of(here * TILE, TILE), TILE)
    theirs = pl.ds(pl.multiple_of((1 - here) * TILE, TILE), TILE)
    back = back_own[...].astype(F32) + back_other[...].astype(F32)
    unit, inverse = norm_parts(middle[...])
    share = back_own[...].astype(F32)
    put_row(small, 0, column_sum(share * unit))
    put_row(small, 2, column_sum(share))
    put_row(small, 4, column_sum(grad[mine, :].astype(F32)))
    first[...] = grad[...].astype(F32) + norm_back(back, gain2[...], unit, inverse)
    kept[...] = first[mine, :]
    grad_low[...] = first[...].astype(BF16)
    put_row(small, 6, column_sum(grad_low[mine, :].astype(F32)))
    grad_context[...] = project_out_back(grad_low[...], pack)
    total[...] = jnp.zeros((TOK, KEYS), F32)

    def window(place, carry):
        base = pl.multiple_of(place * TOK, TOK)
        attend_back(
            qkv, base, grad_context[pl.ds(base, TOK), :], heads, probs, pl.multiple_of(place * KEYS, KEYS),
            total, stack, wide, tall, mixed,
        )
        return carry

    lax.fori_loop(0, PAIR // TOK, window, 0)
    first[...] = project_back(mixed, pack)
    first_keep[...] = first[mine, :]
    first_send[...] = first[theirs, :].astype(BF16)
    unit, _ = norm_parts(whole[...].astype(F32))
    put_row(small, 8, column_sum(first[...] * unit))
    put_row(small, 10, column_sum(first[...]))
    put_row(small, 12, column_sum(mixed[...].astype(F32)))
    small[15:16, :] = jnp.zeros((1, 256), F32)
    put_row(small, 16, column_sum(inner[...].astype(F32)))
    small[20:24, :] = jnp.zeros((4, 256), F32)


def attention_weights_body(normed, mixed, context, grad_low, order, out, start):
    turned = [mm_tn(normed[...], mixed[:, 256 * part : 256 * (part + 1)]).astype(BF16) for part in range(3)]
    canon = mm_nt(jnp.concatenate(turned, axis=1), order[...]).astype(BF16)
    for part in range(3):
        out[start + 512 * part : start + 512 * (part + 1), :] = canon[:, 256 * part : 256 * (part + 1)]
    for part in range(2):
        lines = slice(start + ROWS_QKV + 256 * part, start + ROWS_QKV + 256 * (part + 1))
        out[lines, :] = mm_tn(context[...], grad_low[:, 256 * part : 256 * (part + 1)]).astype(BF16)


def attention_weights_plain_kernel(place_ref, normed, mixed, context, grad_low, order, keep, send, out):
    attention_weights_body(normed, mixed, context, grad_low, order, out, 0)
    deal_halves(place_ref, out, keep, send, HALF_ATT)


def attention_weights_shifted_kernel(
    place_ref, normed, mixed_a, mixed_b, context_a, context_b, grad_low, order, mlp_keep, mlp_send, keep, send, out
):
    attention_weights_body(normed, mixed_a, context_a, grad_low, order, out, 0)
    attention_weights_body(normed, mixed_b, context_b, grad_low, order, out, ROWS_ATT)
    for which, mlp, ref in ((place_ref[COL], mlp_keep, keep), (1 - place_ref[COL], mlp_send, send)):
        for block in range(GROUP):
            first = 4 * EIGHTH * block
            ref[first : first + 2 * EIGHTH, :] = mlp[2 * EIGHTH * block : 2 * EIGHTH * (block + 1), :]
            for part in range(2):
                start = pl.multiple_of(which * HALF_ATT, HALF_ATT) + part * ROWS_ATT + EIGHTH * block
                first = EIGHTH * (4 * block + 2 + part)
                ref[first : first + EIGHTH, :] = out[pl.ds(start, EIGHTH), :]


def table_kernel(total, base, row_back, col_map, out, left, right, strip):
    table_body(total, base, row_back, col_map, out, 0, left, right, strip)


def table_of(total, base, row_back, col_map):
    return run_kernel(
        table_kernel, [total, base, row_back, col_map], [shape_of((2 * GROUP, 256), F32)], BIAS_SCRATCH
    )[0]


def last_kernel(place_ref, whole, gain, keep, other, kept, out, buf):
    here = place_ref[HEAD]
    unit, inverse = norm_parts(whole[pl.ds(pl.multiple_of(here * TILE, TILE), TILE), :].astype(F32))
    buf[...] = kept[...] + norm_back(keep[...] + other[:TILE, :].astype(F32), gain[...], unit, inverse)
    leave_rows(buf, out)


def band_pairs(first, second):
    return [(band * 2 + col, (band ^ (first if col == 0 else second)) * 2 + col) for band in range(8) for col in range(2)]


STEP_PAIRS = (
    [(band * 2 + col, band * 2 + 1 - col) for band in range(8) for col in range(2)],
    band_pairs(1, 2),
    band_pairs(2, 1),
    band_pairs(4, 4),
)


def exchange(value, step):
    return lax.ppermute(value, ("band", "col"), STEP_PAIRS[step])


def double_kernel(place_ref, mine, come, out, *, step):
    half = mine.shape[0]
    out[pl.ds(pl.multiple_of(place_ref[COL + step] * half, half), half), :] = mine[...]
    out[pl.ds(pl.multiple_of((1 - place_ref[COL + step]) * half, half), half), :] = come[...]


def double(place, mine, come, step):
    return run_kernel(
        partial(double_kernel, step=step),
        [place, mine, come],
        [shape_of((2 * mine.shape[0], 256), BF16)],
        specs={0: SMEM},
    )[0]


def after(value, *others):
    return lax.optimization_barrier((value,) + others)[0]


def add_low(left, right):
    return (left.astype(F32) + right.astype(F32)).astype(BF16)


class PageSum:
    def __init__(self, place, kept, send, across=False):
        self.place, self.kept, self.sent, self.across, self.stage = place, kept, send, across, 0
        self.come = exchange(send, 0)

    def tie(self, *others):
        self.kept = after(self.kept, *others)

    def advance(self):
        self.stage += 1
        stage = self.stage
        kept, come = self.kept, self.come
        rows = kept.shape[0]
        if stage < 4:
            half = rows // 2
            bit = self.place[COL + stage]

            def half_at(value, which):
                return lax.dynamic_slice_in_dim(value, which * half, half, 0)

            self.sent = add_low(half_at(kept, 1 - bit), half_at(come, 1 - bit))
            self.kept = add_low(half_at(kept, bit), half_at(come, bit))
            self.come = exchange(self.sent, stage)
            return
        if stage == 4 and self.across:
            start = rows // 4 * 3
            self.sent = add_low(kept[start:], come[start:])
            self.kept = add_low(kept[:start], come[:start])
            self.come = swap_head(self.sent)
            return
        if self.across:
            stage -= 1
            if stage == 4:
                start = rows - come.shape[0]
                self.kept = jnp.concatenate([kept[:start], add_low(kept[start:], come)], axis=0)
        elif stage == 4:
            self.kept = add_low(kept, come)
        if stage > 4:
            bit = self.place[COL + 8 - stage]
            whole = jnp.zeros((2 * rows, 256), BF16)
            whole = lax.dynamic_update_slice_in_dim(whole, kept, bit * rows, 0)
            self.kept = lax.dynamic_update_slice_in_dim(whole, come, (1 - bit) * rows, 0)
        self.sent = self.kept
        self.come = exchange(self.sent, 7 - stage)

    @property
    def halves(self):
        return self.kept, self.come


def both_halves(place_ref, mine, come):
    return (place_ref[COL], mine), (1 - place_ref[COL], come)


def unpack_att(whole, qkv, proj):
    for part in range(3):
        qkv[0, :, 256 * part : 256 * (part + 1)] = whole[512 * part : 512 * (part + 1), :].astype(F32)
    for part in range(2):
        start = ROWS_QKV + 256 * part
        proj[0, :, 256 * part : 256 * (part + 1)] = whole[start : start + 256, :].astype(F32)


def unpack_mlp(whole, fc1, fc2):
    for part in range(4):
        fc1[0, :, 256 * part : 256 * (part + 1)] = whole[512 * part : 512 * (part + 1), :].astype(F32)
    for part in range(2):
        start = 2048 + 1024 * part
        fc2[0, :, 256 * part : 256 * (part + 1)] = whole[start : start + 1024, :].astype(F32)


def unpack_layer_kernel(place_ref, mine, come, qkv, proj, fc1, fc2, att_whole, mlp_whole):
    for which, value in both_halves(place_ref, mine, come):
        for block in range(GROUP):
            first = 3 * EIGHTH * block
            start = pl.multiple_of(which * (ROWS_MLP // 2), 16) + 2 * EIGHTH * block
            mlp_whole[pl.ds(start, 2 * EIGHTH), :] = value[first : first + 2 * EIGHTH, :]
            start = pl.multiple_of(which * HALF_ATT, 16) + EIGHTH * block
            att_whole[pl.ds(start, EIGHTH), :] = value[first + 2 * EIGHTH : first + 3 * EIGHTH, :]
    unpack_att(att_whole, qkv, proj)
    unpack_mlp(mlp_whole, fc1, fc2)


def unpack_mlp_kernel(place_ref, mine, come, *refs):
    fc1, fc2, whole = refs[-3:]
    for which, value in both_halves(place_ref, mine, come):
        whole[pl.ds(pl.multiple_of(which * (ROWS_MLP // 2), 16), ROWS_MLP // 2), :] = value[...]
    unpack_mlp(whole, fc1, fc2)


SMALLS = 256
TABLE_ROWS = (40, 56)


def unpack_last_kernel(
    place_ref, mine, come, order_qv, qkv_in, proj_in,
    qkv, proj, gain, bias, b_qv, table, b_proj, b_fc1, b_fc2, whole, sums,
):
    for which, value in both_halves(place_ref, mine, come):
        whole[pl.ds(pl.multiple_of(which * HALF_ATT, 16), HALF_ATT), :] = value[:HALF_ATT, :]
        start = pl.multiple_of(which * (SMALLS // 2), 16)
        sums[pl.ds(start, SMALLS // 2), :] = value[HALF_ATT:, :].astype(F32)
    unpack_att(whole, qkv, proj)

    for layer, (norm1, norm2) in enumerate(((8, 0), (20, 12))):
        for which, row in enumerate((norm1, norm2)):
            for part in range(2):
                lanes = slice(256 * part, 256 * (part + 1))
                gain[layer, which : which + 1, lanes] = sums[row + part : row + part + 1, :]
                bias[layer, which : which + 1, lanes] = sums[row + 2 + part : row + 3 + part, :]
    for layer, base in enumerate((0, 12)):
        for part in range(2):
            lanes = slice(256 * part, 256 * (part + 1))
            b_fc2[layer : layer + 1, lanes] = sums[base + 4 + part : base + 5 + part, :]
            b_proj[layer : layer + 1, lanes] = sums[base + 6 + part : base + 7 + part, :]
    for layer, base in enumerate((32, 36)):
        for part in range(4):
            b_fc1[layer : layer + 1, 256 * part : 256 * (part + 1)] = sums[base + part : base + part + 1, :]
    for layer, base in enumerate((28, 24)):
        row = jnp.concatenate([sums[base : base + 1, :], sums[base + 2 : base + 3, :]], axis=1)
        b_qv[layer : layer + 1, :] = mm(row.astype(BF16), order_qv[...])
    for layer, base in enumerate(TABLE_ROWS):
        rows = jnp.concatenate(
            [sums[base : base + GROUP, :], sums[base + GROUP : base + 2 * GROUP, :128]], axis=1
        )
        table[layer] = rows[:, : table.shape[2]]


def swap_head(value):
    return lax.ppermute(value, "head", [(0, 1), (1, 0)])


def fast_device(
    act_in, ln_gain, ln_bias, w_qkv, b_qv, rel_table, w_proj, b_proj, w_fc1, b_fc1, w_fc2, b_fc2, grad_out
):
    row_map, row_back, col_map, base, order, heads, order_qv, token_row, token_col = constants()
    band = lax.axis_index("band")
    col = lax.axis_index("col")
    head = lax.axis_index("head")
    bands = lax.axis_size("band")
    cols = lax.axis_size("col")
    digit = [(band >> power) & 1 for power in range(3)]
    place = jnp.stack(
        [
            head,
            col,
            jnp.where(col == 0, digit[0], digit[1]),
            jnp.where(col == 0, digit[1], digit[0]),
            digit[2],
            digit[0],
        ]
    ).astype(jnp.int32)
    band_up = [(here, (here - 1) % bands) for here in range(bands)]
    band_down = [(here, (here + 1) % bands) for here in range(bands)]
    col_left = [(here, (here - 1) % cols) for here in range(cols)]
    edge_left = [(here * 2 + 1, (here - 1) % cols * 2 + 1) for here in range(cols)]
    edge_right = [(here * 2 + 1, (here + 1) % cols * 2 + 1) for here in range(cols)]
    gain = [[ln_gain[layer, which][None] for which in range(2)] for layer in range(2)]
    bias = [[ln_bias[layer, which][None] for which in range(2)] for layer in range(2)]
    row_proj = [b_proj[layer][None] for layer in range(2)]
    row_fc1 = [b_fc1[layer][None] for layer in range(2)]
    row_fc2 = [b_fc2[layer][None] for layer in range(2)]
    qv = b_qv.reshape(2, GROUP, 2, HEAD_DIM).transpose(0, 2, 1, 3).reshape(2, 2, SPAN)
    tables = jnp.pad(rel_table, ((0, 0), (0, ENTRIES - rel_table.shape[1]), (0, 0))).transpose(0, 2, 1)

    def rows_bf(count, width=WIDTH):
        return shape_of((count, width), BF16)

    def rows_f32(count, width=WIDTH):
        return shape_of((count, width), F32)

    def saved(count, width=WIDTH, kind=BF16):
        return pltpu.HBM((count, width), kind)

    def far(value):
        return pltpu.with_memory_space_constraint(value, pltpu.HBM)

    x_other = swap_head(act_in)
    pack0, pack1, pack1_part = pack_weights(place, far(w_qkv), far(w_proj), order)
    pack1_part = swap_head(pack1_part)
    small1 = jnp.concatenate([tables[1], jnp.pad(qv[1], ((0, 6), (0, ENTRIES - SPAN)))], axis=0)
    small1_other = swap_head(small1)
    off0 = bias_of(tables[0], base, row_map, col_map)
    whole, normed0, qkv0, probs0, context0, part0 = run_kernel(
        attention_plain_kernel,
        [place, act_in, x_other, gain[0][0], bias[0][0], far(pack0), qv[0], off0, heads],
        [
            rows_bf(PAIR), saved(PAIR), saved(PAIR, 768), saved(4 * KEYS, TOK), saved(PAIR, SPAN), rows_bf(PAIR),
        ],
        ATTEND_SCRATCH + (pltpu.VMEM((PAIR, WIDTH), F32),),
        specs={0: SMEM},
    )
    part0_other = swap_head(part0)

    off1 = bias_of(after(tables[1], part0), base, row_map, col_map)
    grad_send, grad_stay = run_kernel(
        grad_enter_kernel, [after(grad_out, part0)], [rows_bf(4 * QUAD)] * 2, [pltpu.VMEM((TILE, WIDTH), F32)]
    )
    grad_come = lax.ppermute(grad_send, "band", band_up)
    (grad_own,) = run_kernel(grad_join_kernel, [grad_stay, grad_come], [rows_bf(TILE)])
    pack1_part = after(pack1_part, part0)
    near = [(here, here ^ 1) for here in range(bands)]
    pack1_mine = double(place, pack1_part, lax.ppermute(pack1_part, "band", near), NEAR - COL)
    pack1_theirs = lax.ppermute(pack1_mine, "col", [(0, 1), (1, 0)])
    part0 = after(part0, pack1_mine, grad_own, off1)

    middle0, second0, active0, slope0, x1_keep, x1_send = run_kernel(
        mlp_plain_kernel,
        [
            place, whole, part0, part0_other, row_proj[0], gain[0][1], bias[0][1], far(w_fc1), row_fc1[0],
            far(w_fc2), row_fc2[0],
        ],
        [
            saved(PAIR, WIDTH, F32), saved(PAIR), saved(PAIR, 1024), saved(PAIR, 1024), rows_f32(TILE),
            rows_bf(TILE),
        ],
        [pltpu.VMEM((PAIR, WIDTH), F32)],
        specs={0: SMEM, 7: layer_spec(w_fc1, 0), 9: layer_spec(w_fc2, 0)},
    )
    x1_come = swap_head(x1_send)
    off1_other = bias_of(after(small1_other[:GROUP], x1_send), base, row_map, col_map)
    qv1_other = small1_other[GROUP : GROUP + 2, :SPAN]
    tile, edge = run_kernel(enter_entry_kernel, [x1_keep, x1_come], [rows_bf(TILE), rows_bf(UNIT)])
    edge = lax.ppermute(edge, ("col", "head"), edge_left)
    send, stay = run_kernel(roll_ahead_kernel, [place, tile, edge], [rows_bf(4 * QUAD)] * 2, specs={0: SMEM})
    come = lax.ppermute(send, "band", band_up)
    grad_other = swap_head(after(grad_own, tile))

    rows_id = region_ids(WIN * band + jnp.asarray(token_row), WIN * bands)
    cols_id = region_ids(
        2 * WIN * (2 * col + head) + WIN * jnp.arange(2, dtype=jnp.int32)[:, None] + jnp.asarray(token_col)[None],
        4 * WIN * cols,
    )
    ids = (3 * rows_id[None] + cols_id).astype(F32)
    x1, normed1, qkv1a, qkv1b, probs1a, probs1b, context1a, context1b, middle1, second1_own = run_kernel(
        attention_shifted_kernel,
        [
            place, stay, come, gain[1][0], bias[1][0], gain[1][1], bias[1][1], far(pack1),
            pack1_mine, pack1_theirs, qv[1], qv1_other, off1, off1_other, ids.reshape(TILE, 1), ids.reshape(2, 1, TOK), heads,
            row_proj[1],
        ],
        [
            saved(TILE), saved(TILE), saved(TILE, 768), saved(TILE, 768), saved(2 * KEYS, TOK),
            saved(2 * KEYS, TOK), saved(TILE, SPAN), saved(TILE, SPAN), saved(TILE, WIDTH, F32), rows_bf(TILE),
        ],
        ATTEND_SCRATCH + (pltpu.VMEM((ROWS_ATT, 256), BF16),),
        specs={0: SMEM},
    )
    second1_other = swap_head(second1_own)
    grad_far = jnp.where(head == 0, grad_own[:UNIT], grad_other[:UNIT])
    grad_far = lax.ppermute(after(grad_far, second1_own), "col", col_left)
    second1, grad_all, active1, inner1, x2_keep, x2_send, back1_keep, back1_send, small_mlp1 = run_kernel(
        mlp_shifted_kernel,
        [place, second1_own, second1_other, grad_own, grad_other, grad_far, far(w_fc1), row_fc1[1], far(w_fc2)],
        [
            rows_bf(PAIR), rows_bf(PAIR), rows_bf(PAIR, 1024), rows_bf(PAIR, 1024), saved(TILE, WIDTH, F32),
            rows_bf(TILE), rows_f32(TILE), rows_bf(TILE), rows_f32(8, 256),
        ],
        [pltpu.VMEM((PAIR, 1024), BF16), pltpu.VMEM((PAIR, WIDTH), BF16)],
        specs={0: SMEM, 6: layer_spec(w_fc1, 1), 8: layer_spec(w_fc2, 1)},
    )
    back1_other = swap_head(back1_send)
    mlp1_keep, mlp1_send = mlp_weights(place, second1, active1, grad_all, inner1)
    back1_keep = after(back1_keep, mlp1_send)
    grad_low1, mixed1a, mixed1b, total1a, total1b, stay_main, send_main, edge, small_att1 = run_kernel(
        attention_shifted_back_kernel,
        [
            place, grad_all, back1_keep, back1_other, far(middle1), far(x1), gain[1][0], gain[1][1], far(qkv1a),
            far(qkv1b), far(probs1a), far(probs1b), far(pack1), pack1_mine, pack1_theirs, heads,
        ],
        [
            rows_bf(TILE), rows_bf(TILE, 768), rows_bf(TILE, 768), saved(TOK, KEYS, F32), saved(TOK, KEYS, F32),
            rows_bf(3 * QUAD), rows_bf(3 * QUAD), rows_bf(UNIT), rows_f32(24, 256),
        ],
        ATTEND_SCRATCH
        + (
            pltpu.VMEM((KEYS, TOK), BF16),
            pltpu.VMEM((TILE, SPAN), BF16),
            pltpu.VMEM((TILE, WIDTH), F32),
            pltpu.VMEM((ROWS_ATT, 256), BF16),
        ),
        specs={0: SMEM},
    )

    edge_come = lax.ppermute(edge, ("col", "head"), edge_right)
    send, stay = run_kernel(
        roll_back_kernel, [place, stay_main, send_main, edge, edge_come], [rows_bf(4 * QUAD)] * 2, specs={0: SMEM}
    )
    come = lax.ppermute(send, "band", band_down)
    layer1_keep, layer1_send = run_kernel(
        attention_weights_shifted_kernel,
        [
            place, far(after(normed1, send)), mixed1a, mixed1b, far(context1a), far(context1b), grad_low1, order,
            mlp1_keep, mlp1_send,
        ],
        [rows_bf(2 * ROWS_ATT, 256)] * 2,
        [pltpu.VMEM((2 * ROWS_ATT, 256), BF16)],
        specs={0: SMEM},
    )
    own = jnp.concatenate([stay, after(come, layer1_send)], axis=0)
    own_other = swap_head(own)
    come = own
    layer1 = PageSum(place, layer1_keep, after(layer1_send, come), across=True)
    layer1.advance()
    slope0 = after(slope0, layer1.sent)
    grad0, inner0, back0 = run_kernel(
        mlp_plain_back_kernel,
        [
            place, own, own_other, far(slope0), far(w_fc1), far(w_fc2),
        ],
        [rows_bf(PAIR), rows_bf(PAIR, 1024), rows_bf(PAIR)],
        [pltpu.VMEM((PAIR, WIDTH), BF16)],
        specs={0: SMEM, 4: layer_spec(w_fc1, 0), 5: layer_spec(w_fc2, 0)},
    )
    back0_other = swap_head(back0)
    mlp0_keep, mlp0_send = mlp_weights(place, far(second0), far(active0), grad0, inner0)
    table1_send = table_of(far(after(total1b, back0)), base, row_back, col_map)
    table1 = table_of(far(after(total1a, back0)), base, row_back, col_map)
    mlp0 = PageSum(place, mlp0_keep, after(mlp0_send, back0_other))
    layer1.tie(mlp0_send)
    layer1.advance()
    layer1.tie(back0_other, table1, table1_send)
    layer1.advance()
    back0 = after(back0, layer1.sent, mlp0.sent)
    grad_low0, mixed0, total0, first_keep, first_send, kept0, small_att0 = run_kernel(
        attention_plain_back_kernel,
        [
            place, grad0, back0, back0_other, far(middle0), whole, gain[0][0], gain[0][1], far(qkv0), far(probs0),
            far(pack0), heads, inner0,
        ],
        [
            rows_bf(PAIR), rows_bf(PAIR, 768), saved(TOK, KEYS, F32), saved(TILE, WIDTH, F32), rows_bf(TILE),
            saved(TILE, WIDTH, F32),
            rows_f32(24, 256),
        ],
        ATTEND_SCRATCH
        + (pltpu.VMEM((KEYS, TOK), BF16), pltpu.VMEM((PAIR, SPAN), BF16), pltpu.VMEM((PAIR, WIDTH), F32)),
        specs={0: SMEM},
    )
    att0 = PageSum(
        place,
        *run_kernel(
            attention_weights_plain_kernel,
            [place, far(normed0), mixed0, far(context0), grad_low0, order],
            [rows_bf(HALF_ATT, 256)] * 2,
            [pltpu.VMEM((ROWS_ATT, 256), BF16)],
            specs={0: SMEM},
        ),
    )
    shared = after(jnp.concatenate([small_att0[:12], small_att1[:12]], axis=0), att0.sent)
    come = swap_head(jnp.concatenate([shared, small_att1[16:24], table1_send], axis=0))
    table0 = table_of(far(after(total0, shared)), base, row_back, col_map)
    turn = att0.sent

    def take(chain):
        chain.tie(turn)
        chain.advance()
        return chain.sent

    turn = take(mlp0)
    sums = jnp.concatenate(
        [
            shared + come[:24],
            small_att1[12:16] + come[24:28],
            small_att0[12:20],
            small_mlp1[:4],
            table0,
            table1 + come[32:48],
        ],
        axis=0,
    )
    sums = jnp.pad(after(sums, turn).astype(BF16), ((0, SMALLS - sums.shape[0]), (0, 0)))
    sums_keep = lax.dynamic_slice_in_dim(sums, col * (SMALLS // 2), SMALLS // 2, 0)
    sums_send = lax.dynamic_slice_in_dim(sums, (1 - col) * (SMALLS // 2), SMALLS // 2, 0)
    sums_come = exchange(sums_send, 0)
    att0.kept = jnp.concatenate([att0.kept, after(sums_keep, sums_send)], axis=0)
    att0.come = jnp.concatenate([att0.come, sums_come], axis=0)
    turn = take(att0)
    turn = take(layer1)
    turn = take(mlp0)
    x2_come = swap_head(after(x2_send, turn))
    turn = take(layer1)
    turn = take(att0)
    turn = take(mlp0)
    x2_move, x2_stay = run_kernel(
        last_entry_kernel,
        [far(x2_keep), after(x2_come, turn), far(middle1), row_fc2[1]],
        [rows_bf(4 * QUAD)] * 2,
        [pltpu.VMEM((TILE, WIDTH), F32)],
    )
    x2_come = lax.ppermute(x2_move, "band", band_down)
    layer1.tie(x2_move)
    turn = take(layer1)
    turn = take(att0)
    turn = take(mlp0)
    x2_edge = jnp.concatenate([after(x2_come, turn)[3 * QUAD :], x2_stay[3 * QUAD :]], axis=0)
    x2_far = lax.ppermute(x2_edge, ("col", "head"), edge_right)
    turn = take(layer1)
    turn = take(att0)
    turn = take(mlp0)
    x2_edge = jnp.where(head == 1, x2_far, x2_edge)
    other = swap_head(jnp.concatenate([first_send, after(x2_edge, turn)], axis=0))
    turn = take(layer1)
    turn = take(att0)
    turn = take(mlp0)
    grad_in = run_kernel(
        last_kernel,
        [place, whole, gain[0][0], far(first_keep), after(other, turn), far(kept0)],
        [shape_of((WIN, 2 * WIN, WIDTH), F32)],
        [pltpu.VMEM((TILE, WIDTH), F32)],
        specs={0: SMEM},
    )[0]
    act_out = run_kernel(
        leave_kernel,
        [after(other, turn), x2_stay, x2_come],
        [shape_of((WIN, 2 * WIN, WIDTH), F32)],
        [pltpu.VMEM((TILE, WIDTH), F32)],
    )[0]
    att0.tie(grad_in, act_out)
    turn = take(att0)
    turn = take(mlp0)
    shapes = [(2, 512, 768), (2, 256, 512), (2, 512, 1024), (2, 1024, 512)]
    outs = [shape_of(shape, F32) for shape in shapes]
    anywhere = pl.BlockSpec(memory_space=pl.ANY)
    layer1.tie(turn)
    g_qkv, g_proj, g_fc1, g_fc2 = run_kernel(
        unpack_layer_kernel,
        [place, *layer1.halves],
        outs,
        [pltpu.VMEM((ROWS_ATT, 256), BF16), pltpu.VMEM((ROWS_MLP, 256), BF16)],
        specs={0: SMEM},
        out_specs=[layer_spec(out, 1) for out in outs],
    )
    turn = take(att0)
    g_fc1, g_fc2 = run_kernel(
        unpack_mlp_kernel,
        [place, *mlp0.halves, g_fc1, g_fc2],
        outs[2:],
        [pltpu.VMEM((ROWS_MLP, 256), BF16)],
        specs={0: SMEM, 3: anywhere, 4: anywhere},
        out_specs=[layer_spec(out, 0) for out in outs[2:]],
        aliases={3: 0, 4: 1},
    )
    g_qkv, g_proj, g_gain, g_bias, g_qv, g_table, g_bproj, g_bfc1, g_bfc2 = run_kernel(
        unpack_last_kernel,
        [place, *att0.halves, order_qv, g_qkv, g_proj],
        outs[:2]
        + [
            shape_of(array.shape, F32)
            for array in (ln_gain, ln_bias, b_qv, rel_table.transpose(0, 2, 1), b_proj, b_fc1, b_fc2)
        ],
        [pltpu.VMEM((ROWS_ATT, 256), BF16), pltpu.VMEM((SMALLS, 256), F32)],
        specs={0: SMEM, 4: pl.BlockSpec(memory_space=pl.ANY), 5: pl.BlockSpec(memory_space=pl.ANY)},
        out_specs=[layer_spec(out, 0) for out in outs[:2]] + [VMEM] * 7,
        aliases={4: 0, 5: 1},
    )
    g_table = g_table.transpose(0, 2, 1)
    return (
        act_out, grad_in, g_gain, g_bias, g_qkv, g_qv, g_table, g_proj, g_bproj, g_fc1, g_bfc1, g_fc2, g_bfc2,
    )


def fits(mesh):
    return dict(mesh.shape) == {"band": 8, "col": 2, "head": 2}


def solution(mesh):
    placed = (
        P("band", ("col", "head"), None),
        P(),
        P(),
        P(None, None, "head"),
        P(None, "head"),
        P(None, None, "head"),
        P(None, "head", None),
        P(),
        P(None, None, "head"),
        P(None, "head"),
        P(None, "head", None),
        P(),
        P("band", ("col", "head"), None),
    )
    return jax.shard_map(
        fast_device if fits(mesh) else on_device,
        mesh=mesh,
        in_specs=placed,
        out_specs=(
            P("band", ("col", "head"), None),
            P("band", ("col", "head"), None),
            P(),
            P(),
            P(None, None, "head"),
            P(None, "head"),
            P(None, None, "head"),
            P(None, "head", None),
            P(),
            P(None, None, "head"),
            P(None, "head"),
            P(None, "head", None),
            P(),
        ),
        check_vma=False,
    )
```

```python
from functools import partial

import jax
import jax.numpy as jnp
import numpy as np
from jax import lax
from jax.experimental import pallas as pl
from jax.experimental.pallas import tpu as pltpu
from jax.sharding import PartitionSpec as P

HEAD_DIM = 32
WIN = 10
SHIFT = 5
BLOCKS = 2


EPSILON = 1e-05
HIGHEST = lax.Precision.HIGHEST


def shifted_2(value, axis, steps):
    count = lax.axis_size(axis)
    pairs = [(source, (source + steps) % count) for source in range(count)]
    return lax.ppermute(value, axis, pairs)


def layer_norm(array, gain_row, bias_row):
    centre = array - jnp.mean(array, axis=-1, keepdims=True)
    spread = jnp.mean(centre * centre, axis=-1, keepdims=True)
    return centre * lax.rsqrt(spread + EPSILON) * gain_row + bias_row


def offsets(window):
    places = jnp.arange(window, dtype=jnp.int32)
    spread = jnp.arange(2 * window - 1, dtype=jnp.int32)
    return (
        spread[None, None, :] == places[:, None, None] - places[None, :, None] + window - 1
    ).astype(jnp.float32)


def position_bias(table):
    head_count = table.shape[-1]
    table_grid = table.reshape(2 * WIN - 1, 2 * WIN - 1, head_count)
    onehot = offsets(WIN)
    full = jnp.einsum("ika,jlb,abh->hijkl", onehot, onehot, table_grid, precision=HIGHEST)
    return full.reshape(head_count, WIN * WIN, WIN * WIN)


def table_grad(grad_offset):
    head_count = grad_offset.shape[0]
    onehot = offsets(WIN)
    spread = grad_offset.reshape(head_count, WIN, WIN, WIN, WIN)
    full = jnp.einsum("ika,jlb,hijkl->abh", onehot, onehot, spread, precision=HIGHEST)
    return full.reshape((2 * WIN - 1) * (2 * WIN - 1), head_count)


def gather_tile(array):
    return lax.all_gather(array, "head", axis=1, tiled=True)


def sum_tile(array):
    return lax.psum_scatter(
        array.astype(jnp.bfloat16), "head", scatter_dimension=1, tiled=True
    ).astype(jnp.float32)


def gather_grad(array):
    return lax.all_gather(array, "head", axis=1, tiled=True)


def sum_grad(array):
    return lax.psum_scatter(
        array.astype(jnp.bfloat16), "head", scatter_dimension=1, tiled=True
    ).astype(jnp.float32)


def roll_ahead(array):
    upper = shifted_2(array[:SHIFT], "band", -1)
    array = jnp.concatenate([array[SHIFT:], upper], axis=0)
    leftmost = shifted_2(array[:, :SHIFT], ("col", "head"), -1)
    return jnp.concatenate([array[:, SHIFT:], leftmost], axis=1)


def roll_behind(array):
    lower = shifted_2(array[-SHIFT:], "band", 1)
    array = jnp.concatenate([lower, array[:-SHIFT]], axis=0)
    rightmost = shifted_2(array[:, -SHIFT:], ("col", "head"), 1)
    return jnp.concatenate([rightmost, array[:, :-SHIFT]], axis=1)


def pack_members(members):
    group = lax.axis_size("band") * lax.axis_size("col")
    flat = jnp.concatenate([member.reshape(-1) for member in members])
    padding = -flat.shape[0] % group
    return jnp.concatenate([flat, jnp.zeros((padding,), jnp.float32)])


def unpack_members(flat, members):
    result = []
    start = 0
    for member in members:
        count = member.size
        result.append(flat[start : start + count].reshape(member.shape))
        start = start + count
    return tuple(result)


def to_windows(tile_rows):
    height, breadth, depth = tile_rows.shape
    window_count = breadth // height
    split = tile_rows.reshape(height, window_count, height, depth).transpose(1, 0, 2, 3)
    return split.reshape(window_count * height * height, depth)


def from_windows(flat_rows, height):
    window_count = flat_rows.shape[0] // (height * height)
    depth = flat_rows.shape[1]
    split = flat_rows.reshape(window_count, height, height, depth).transpose(1, 0, 2, 3)
    return split.reshape(height, window_count * height, depth)


def region_ids(places, extent):
    return (places >= extent - WIN).astype(jnp.int32) + (places >= extent - SHIFT).astype(jnp.int32)


def shift_mask(breadth):
    rows_all = WIN * lax.axis_size("band")
    cols_all = breadth * lax.axis_size("col")
    rows_here = WIN * lax.axis_index("band") + jnp.arange(WIN, dtype=jnp.int32)
    cols_here = breadth * lax.axis_index("col") + jnp.arange(breadth, dtype=jnp.int32)
    region = 3 * region_ids(rows_here, rows_all)[:, None] + region_ids(cols_here, cols_all)[None, :]
    window_count = breadth // WIN
    labels = to_windows(region[:, :, None])[:, 0].reshape(window_count, WIN * WIN)
    return jnp.where(labels[:, :, None] != labels[:, None, :], -100.0, 0.0).astype(jnp.float32)


def scores(queries, key_rows, offset, region_mask):
    logits = jnp.einsum("wqhd,wkhd->whqk", queries, key_rows, preferred_element_type=jnp.float32)
    logits = logits * HEAD_DIM ** (-0.5) + offset[None]
    if region_mask is not None:
        logits = logits + region_mask[:, None]
    return logits


def forward_block(source, weights, shifted):
    norm_gain, norm_bias, w_qkv, b_qv, table, w_proj, b_proj, w_fc1, b_fc1, w_fc2, b_fc2 = weights
    height = source.shape[0]
    heads_here = table.shape[-1]
    normed = layer_norm(source, norm_gain[0], norm_bias[0]).astype(jnp.bfloat16)
    if shifted:
        normed = roll_ahead(normed)
    gathered = gather_tile(normed)
    window_count = gathered.shape[1] // height
    flat_rows = to_windows(gathered)
    projected = jnp.dot(flat_rows, w_qkv, preferred_element_type=jnp.float32)
    projected = projected.reshape(window_count, height * height, heads_here, 3, HEAD_DIM)
    qv_bias = b_qv.reshape(heads_here, 2, HEAD_DIM)
    queries = (projected[..., 0, :] + qv_bias[:, 0]).astype(jnp.bfloat16)
    key_rows = projected[..., 1, :].astype(jnp.bfloat16)
    values = (projected[..., 2, :] + qv_bias[:, 1]).astype(jnp.bfloat16)
    offset = position_bias(table)
    region_mask = shift_mask(gathered.shape[1]) if shifted else None
    logits = scores(queries, key_rows, offset, region_mask)
    log_total = jax.nn.logsumexp(logits, axis=-1)
    probs_low = jnp.exp(logits - log_total[..., None]).astype(jnp.bfloat16)
    context = jnp.einsum("whqk,wkhd->wqhd", probs_low, values, preferred_element_type=jnp.float32)
    context = context.astype(jnp.bfloat16).reshape(
        window_count * height * height, heads_here * HEAD_DIM
    )
    partial_out = from_windows(jnp.dot(context, w_proj, preferred_element_type=jnp.float32), height)
    branch = sum_tile(partial_out) + b_proj
    if shifted:
        branch = roll_behind(branch.astype(jnp.bfloat16)).astype(jnp.float32)
    middle = source + branch
    second = layer_norm(middle, norm_gain[1], norm_bias[1]).astype(jnp.bfloat16)
    second_tile = gather_tile(second)
    mlp_rows = second_tile.reshape(-1, second_tile.shape[-1])
    hidden = jnp.dot(mlp_rows, w_fc1, preferred_element_type=jnp.float32) + b_fc1
    active = jax.nn.gelu(hidden, approximate=False).astype(jnp.bfloat16)
    out_part = jnp.dot(active, w_fc2, preferred_element_type=jnp.float32).reshape(second_tile.shape)
    result = middle + sum_tile(out_part) + b_fc2
    saved_state = (
        source,
        middle,
        flat_rows,
        queries,
        key_rows,
        values,
        log_total,
        context,
        mlp_rows,
        hidden,
        offset,
        region_mask,
    )
    return (result, saved_state)


def backward_block(upstream, weights, saved_state, shifted):
    norm_gain, norm_bias, w_qkv, b_qv, table, w_proj, b_proj, w_fc1, b_fc1, w_fc2, b_fc2 = weights
    (
        source,
        middle,
        flat_rows,
        queries,
        key_rows,
        values,
        log_total,
        context,
        mlp_rows,
        hidden,
        offset,
        region_mask,
    ) = saved_state
    height = source.shape[0]
    window_count, window_len, heads_here, _ = queries.shape
    grad_low = upstream.astype(jnp.bfloat16)
    grad_tile = gather_grad(grad_low)
    grad_rows = grad_tile.reshape(-1, grad_tile.shape[-1])
    active = jax.nn.gelu(hidden, approximate=False).astype(jnp.bfloat16)
    g_fc2 = jnp.dot(active.T, grad_rows, preferred_element_type=jnp.float32)
    g_bfc2 = jnp.sum(grad_low.astype(jnp.float32), axis=(0, 1))
    g_active = jnp.dot(grad_rows, w_fc2.T, preferred_element_type=jnp.float32)
    g_hidden = jax.vjp(partial(jax.nn.gelu, approximate=False), hidden)[1](g_active)[0].astype(
        jnp.bfloat16
    )
    g_bfc1 = jnp.sum(g_hidden.astype(jnp.float32), axis=0)
    g_fc1 = jnp.dot(mlp_rows.T, g_hidden, preferred_element_type=jnp.float32)
    g_second = sum_grad(
        jnp.dot(g_hidden, w_fc1.T, preferred_element_type=jnp.float32).reshape(grad_tile.shape)
    )
    pull_second = jax.vjp(layer_norm, middle, norm_gain[1], norm_bias[1])[1]
    g_mid_norm, g_gain2, g_bias2 = pull_second(g_second)
    g_middle = upstream + g_mid_norm
    g_branch = g_middle.astype(jnp.bfloat16)
    if shifted:
        g_branch = roll_ahead(g_branch)
    g_bproj = jnp.sum(g_branch.astype(jnp.float32), axis=(0, 1))
    g_output = to_windows(gather_grad(g_branch))
    g_proj = jnp.dot(context.T, g_output, preferred_element_type=jnp.float32)
    g_context = jnp.dot(g_output, w_proj.T, preferred_element_type=jnp.float32).astype(jnp.bfloat16)
    g_context = g_context.reshape(window_count, window_len, heads_here, HEAD_DIM)
    logits = scores(queries, key_rows, offset, region_mask)
    probs = jnp.exp(logits - log_total[..., None])
    probs_low = probs.astype(jnp.bfloat16)
    g_values = jnp.einsum(
        "whqk,wqhd->wkhd", probs_low, g_context, preferred_element_type=jnp.float32
    ).astype(jnp.bfloat16)
    g_probs = jnp.einsum("wqhd,wkhd->whqk", g_context, values, preferred_element_type=jnp.float32)
    centre = jnp.sum(probs * g_probs, axis=-1, keepdims=True)
    g_logits = (probs * (g_probs - centre)).astype(jnp.bfloat16)
    g_table = table_grad(jnp.sum(g_logits.astype(jnp.float32), axis=0))
    inv_root = HEAD_DIM ** (-0.5)
    g_queries = (
        jnp.einsum("whqk,wkhd->wqhd", g_logits, key_rows, preferred_element_type=jnp.float32)
        * inv_root
    ).astype(jnp.bfloat16)
    g_keys = (
        jnp.einsum("whqk,wqhd->wkhd", g_logits, queries, preferred_element_type=jnp.float32)
        * inv_root
    ).astype(jnp.bfloat16)
    g_mixed = jnp.stack([g_queries, g_keys, g_values], axis=3).reshape(
        window_count * window_len, heads_here * 3 * HEAD_DIM
    )
    g_bqv = jnp.stack(
        [
            jnp.sum(g_queries.astype(jnp.float32), axis=(0, 1)),
            jnp.sum(g_values.astype(jnp.float32), axis=(0, 1)),
        ],
        axis=1,
    ).reshape(-1)
    g_qkv = jnp.dot(flat_rows.T, g_mixed, preferred_element_type=jnp.float32)
    g_first = sum_grad(
        from_windows(jnp.dot(g_mixed, w_qkv.T, preferred_element_type=jnp.float32), height)
    )
    if shifted:
        g_first = roll_behind(g_first.astype(jnp.bfloat16)).astype(jnp.float32)
    pull_first = jax.vjp(layer_norm, source, norm_gain[0], norm_bias[0])[1]
    g_source, g_gain1, g_bias1 = pull_first(g_first)
    g_input = g_middle + g_source
    sharded = (g_qkv, g_bqv, g_table, g_proj, g_fc1, g_bfc1, g_fc2)
    shared = (jnp.stack([g_gain1, g_gain2]), jnp.stack([g_bias1, g_bias2]), g_bproj, g_bfc2)
    return (g_input, sharded, shared)


def on_device(
    act_in,
    ln_gain,
    ln_bias,
    w_qkv,
    b_qv,
    rel_table,
    w_proj,
    b_proj,
    w_fc1,
    b_fc1,
    w_fc2,
    b_fc2,
    grad_out,
):
    params = (ln_gain, ln_bias, w_qkv, b_qv, rel_table, w_proj, b_proj, w_fc1, b_fc1, w_fc2, b_fc2)
    layers = [tuple((member[block_id] for member in params)) for block_id in range(BLOCKS)]
    residual = act_in.astype(jnp.float32)
    layer_inputs = []
    stored = []
    for block_id in range(BLOCKS):
        layer_inputs.append(residual)
        residual, saved_state = forward_block(residual, layers[block_id], block_id % 2 == 1)
        stored.append(saved_state)
    upstream = grad_out
    sharded_all = [None] * BLOCKS
    shared_all = [None] * BLOCKS
    for block_id in reversed(range(BLOCKS)):
        saved_state = forward_block(layer_inputs[block_id], layers[block_id], block_id % 2 == 1)[1]
        upstream, sharded, shared = backward_block(
            upstream, layers[block_id], saved_state, block_id % 2 == 1
        )
        sharded_all[block_id] = sharded
        shared_all[block_id] = shared
    sharded_stack = tuple(
        (jnp.stack([entry[member] for entry in sharded_all]) for member in range(7))
    )
    shared_stack = tuple(
        (jnp.stack([entry[member] for entry in shared_all]) for member in range(4))
    )
    packed_all = pack_members(sharded_stack)
    packed_part = lax.psum_scatter(
        packed_all.astype(jnp.bfloat16), ("band", "col"), scatter_dimension=0, tiled=True
    ).astype(jnp.float32)
    packed_all = lax.all_gather(
        packed_part.astype(jnp.bfloat16), ("band", "col"), axis=0, tiled=True
    ).astype(packed_part.dtype)
    sharded_stack = unpack_members(packed_all, sharded_stack)
    shared_stack = lax.psum(shared_stack, ("band", "col", "head"))
    return (
        residual,
        upstream,
        shared_stack[0],
        shared_stack[1],
        sharded_stack[0],
        sharded_stack[1],
        sharded_stack[2],
        sharded_stack[3],
        shared_stack[2],
        sharded_stack[4],
        sharded_stack[5],
        sharded_stack[6],
        shared_stack[3],
    )


F32 = jnp.float32
BF16 = jnp.bfloat16
WIDTH = 512
QUAD = 32
LIVE = SHIFT * SHIFT
UNIT = 2 * QUAD
TOK = 2 * UNIT
TILE = 4 * UNIT
PAIR = 2 * TILE
GROUP = 8
SPAN = GROUP * HEAD_DIM
KEYS = GROUP * TOK
OFFSETS = 2 * WIN - 1
ENTRIES = 384
SCALE = HEAD_DIM ** (-0.5)
FAR = -1e30
ROOT_HALF = 0.5 ** 0.5
ROOT_TWO_PI = (2.0 * np.pi) ** (-0.5)
VMEM = pl.BlockSpec(memory_space=pltpu.VMEM)
SMEM = pl.BlockSpec(memory_space=pltpu.SMEM)
ROWS_QKV = 3 * 512
ROWS_ATT = ROWS_QKV + 512
ROWS_MLP = 4096
HALF_ATT = ROWS_ATT // 2
HEAD, COL, NEAR = 0, 1, 5
QUARTER_ATT = HALF_ATT // 2
EIGHTH = HALF_ATT // 8


def shape_of(shape, kind):
    return jax.ShapeDtypeStruct(shape, kind)


def layer_spec(array, layer):
    rest = array.shape[1:]
    return pl.BlockSpec((1,) + rest, lambda _: (layer,) + (0,) * len(rest), pipeline_mode=pl.Buffered(1))


COSTS = {
    "attention_plain_kernel": 6.0,
    "mlp_plain_kernel": 4.5,
    "attention_shifted_kernel": 5.5,
    "mlp_shifted_kernel": 5.0,
    "attention_shifted_back_kernel": 6.0,
    "mlp_plain_back_kernel": 2.0,
    "attention_plain_back_kernel": 6.0,
    "mlp_weights_kernel": 2.0,
    "attention_weights_plain_kernel": 2.0,
    "attention_weights_shifted_kernel": 2.7,
    "table_kernel": 1.2,
    "bias_body": 1.2,
    "pack_kernel": 1.5,
    "unpack_mlp_kernel": 3.0,
    "unpack_layer_kernel": 5.0,
    "unpack_last_kernel": 2.5,
}


def run_kernel(kernel, operands, outs, scratch=(), limit=24, specs=None, aliases=None, out_specs=None):
    specs = specs or {}
    name = getattr(kernel, "func", kernel).__name__
    in_specs = [specs.get(place, VMEM) for place in range(len(operands))]
    return pl.pallas_call(
        kernel,
        grid=(1,),
        in_specs=in_specs,
        out_specs=out_specs or [VMEM] * len(outs),
        out_shape=list(outs),
        scratch_shapes=list(scratch),
        input_output_aliases=aliases or {},
        cost_estimate=pl.CostEstimate(
            flops=int(COSTS.get(name, 0.7) * 4.6e9), bytes_accessed=1 << 10, transcendentals=0
        ),
        compiler_params=pltpu.CompilerParams(vmem_limit_bytes=limit << 20),
        name=name,
    )(*operands)


def mm(left, right):
    return lax.dot_general(left, right, (((1,), (0,)), ((), ())), preferred_element_type=F32)


def mm_nt(left, right):
    return lax.dot_general(left, right, (((1,), (1,)), ((), ())), preferred_element_type=F32)


def mm_tn(left, right):
    return lax.dot_general(left, right, (((0,), (0,)), ((), ())), preferred_element_type=F32)


def halves_of(value):
    high = value.astype(BF16)
    return high, (value - high.astype(F32)).astype(BF16)


def norm_parts(value):
    centre = value - jnp.mean(value, axis=-1, keepdims=True)
    inverse = lax.rsqrt(jnp.mean(centre * centre, axis=-1, keepdims=True) + EPSILON)
    return centre * inverse, inverse


def norm_back(grad, gain, unit, inverse):
    scaled = grad * gain
    return (
        scaled
        - jnp.mean(scaled, axis=-1, keepdims=True)
        - unit * jnp.mean(scaled * unit, axis=-1, keepdims=True)
    ) * inverse


def column_sum(value):
    return jnp.sum(value, axis=0, keepdims=True)


def put_row(ref, row, value):
    for part in range(value.shape[1] // 256):
        ref[row + part : row + part + 1, :] = value[:, 256 * part : 256 * (part + 1)]


def token_place(row, col):
    return ((col // SHIFT) * 2 + row // SHIFT) * QUAD + (row % SHIFT) * SHIFT + col % SHIFT


def constants():
    row_map = np.zeros((TOK, 160), np.float32)
    col_map = np.zeros((TOK, TOK), np.float32)
    token_row = np.zeros((TOK,), np.int32)
    token_col = np.zeros((TOK,), np.int32)
    for row in range(WIN):
        for col in range(WIN):
            place = token_place(row, col)
            row_map[place, row * 16 + col] = 1.0
            col_map[row * WIN + col, place] = 1.0
            token_row[place] = row
            token_col[place] = col
    base = np.full((1, 256), -4000, np.int32)
    for lane in range(OFFSETS * WIN):
        base[0, lane] = (OFFSETS - 1 - lane // WIN) * OFFSETS - lane % WIN + WIN - 1
    order = np.zeros((768, 768), np.float32)
    for head in range(GROUP):
        for part in range(3):
            for place in range(HEAD_DIM):
                order[head * 96 + part * 32 + place, part * SPAN + head * HEAD_DIM + place] = 1.0
    heads = np.zeros((KEYS, SPAN), np.float32)
    for head in range(GROUP):
        heads[head * TOK : (head + 1) * TOK, head * HEAD_DIM : (head + 1) * HEAD_DIM] = 1.0
    order_qv = np.zeros((2 * SPAN, 2 * SPAN), np.float32)
    for head in range(GROUP):
        for part in range(2):
            for place in range(HEAD_DIM):
                order_qv[part * SPAN + head * HEAD_DIM + place, (2 * head + part) * HEAD_DIM + place] = 1.0
    return (
        jnp.asarray(row_map, BF16),
        jnp.asarray(row_map.T, BF16),
        jnp.asarray(col_map, BF16),
        jnp.asarray(base),
        jnp.asarray(order, BF16),
        jnp.asarray(heads, BF16),
        jnp.asarray(order_qv, BF16),
        token_row,
        token_col,
    )


def enter_rows(in_ref, buf, start):
    for row in range(WIN):
        line = in_ref[row].astype(F32)
        for unit in range(4):
            first = unit * UNIT + (row // SHIFT) * QUAD + (row % SHIFT) * SHIFT
            buf[start + first : start + first + SHIFT, :] = line[unit * SHIFT : (unit + 1) * SHIFT, :]


def enter_kernel(in_ref, out_ref, buf):
    buf[...] = jnp.zeros(buf.shape, F32)
    enter_rows(in_ref, buf, 0)
    out_ref[...] = buf[...].astype(BF16)


def enter_units(tile):
    return run_kernel(
        enter_kernel, [tile], [shape_of((TILE, WIDTH), BF16)], [pltpu.VMEM((TILE, WIDTH), F32)]
    )[0]


def leave_rows(value_ref, out_ref):
    for row in range(WIN):
        for unit in range(4):
            start = unit * UNIT + (row // SHIFT) * QUAD + (row % SHIFT) * SHIFT
            out_ref[row, unit * SHIFT : (unit + 1) * SHIFT, :] = value_ref[start : start + SHIFT, :]


def leave_kernel(first, stay, come, out_ref, buf):
    buf[0:UNIT, :] = first[TILE:, :].astype(F32)
    for unit in range(3):
        lines = slice(QUAD * unit, QUAD * (unit + 1))
        start = UNIT * (unit + 1)
        buf[start : start + QUAD, :] = come[lines, :].astype(F32)
        buf[start + QUAD : start + UNIT, :] = stay[lines, :].astype(F32)
    leave_rows(buf, out_ref)


def part_quads(value, upper, lower, units):
    for unit in range(units):
        lines = slice(QUAD * unit, QUAD * (unit + 1))
        upper[lines, :] = value[UNIT * unit : UNIT * unit + QUAD, :].astype(upper.dtype)
        lower[lines, :] = value[UNIT * unit + QUAD : UNIT * (unit + 1), :].astype(lower.dtype)


def join_quads(out, start, upper, lower, units):
    for unit in range(units):
        lines = slice(QUAD * unit, QUAD * (unit + 1))
        first = start + UNIT * unit
        out[first : first + QUAD, :] = upper[lines, :]
        out[first + QUAD : first + UNIT, :] = lower[lines, :]


def enter_entry_kernel(keep, come, tile, edge):
    value = (keep[...] + come[...].astype(F32)).astype(BF16)
    tile[...] = value
    edge[...] = value[3 * UNIT :, :]


def roll_ahead_kernel(place, tile, come, send, stay):
    part_quads(tile, send, stay, 3)
    taken = jnp.where(place[HEAD] == 1, come[...], tile[3 * UNIT :, :])
    send[3 * QUAD :, :] = taken[:QUAD, :]
    stay[3 * QUAD :, :] = taken[QUAD:, :]


def roll_back_kernel(place, stay_main, send_main, edge, come, send, stay):
    taken = jnp.where(place[HEAD] == 1, come[...], edge[...])
    stay[: 3 * QUAD, :] = stay_main[...]
    stay[3 * QUAD :, :] = taken[:QUAD, :]
    send[: 3 * QUAD, :] = send_main[...]
    send[3 * QUAD :, :] = taken[QUAD:, :]


def grad_enter_kernel(in_ref, send, stay, buf):
    buf[...] = jnp.zeros(buf.shape, F32)
    enter_rows(in_ref, buf, 0)
    part_quads(buf, send, stay, 4)


def grad_join_kernel(stay, come, out):
    join_quads(out, 0, stay, come, 4)


def last_entry_kernel(keep, come, middle, b_fc2, send, stay, buf):
    buf[...] = keep[...] + come[...].astype(F32) + middle[...] + b_fc2[...]
    part_quads(buf, stay, send, 4)


def entry_onehot(base_ref):
    entry = lax.broadcasted_iota(jnp.int32, (ENTRIES, 256), 0)
    return (entry == base_ref[...]).astype(F32).astype(BF16)


LINES = WIN * GROUP


def bias_body(table_ref, base_ref, row_map_ref, col_map_ref, out_ref, left, right, strip):
    table = table_ref[...]
    turned = jnp.concatenate([pltpu.roll(table, ENTRIES - col, 1) if col else table for col in range(WIN)], axis=0)
    high, low = halves_of(turned)
    onehot = entry_onehot(base_ref)
    spread = mm(high, onehot) + mm(low, onehot)
    left[0:LINES, :] = spread[:, :128]
    right[0:LINES, :] = spread[:, 128:]
    left[LINES:, :] = jnp.zeros((16 * GROUP - LINES, 128), F32)
    right[LINES:, :] = jnp.zeros((16 * GROUP - LINES, 128), F32)
    for head in range(GROUP):
        wide = jnp.concatenate(
            [left[pl.ds(head, 16, stride=GROUP), :], right[pl.ds(head, 16, stride=GROUP), :]], axis=1
        )
        for row in range(WIN):
            start = (WIN - 1 - row) * WIN
            strip[16 * row : 16 * (row + 1), TOK * head : TOK * (head + 1)] = wide[:, start : start + TOK]
    high, low = halves_of(strip[...])
    rows = mm(row_map_ref[...], high) + mm(row_map_ref[...], low)
    live = lax.broadcasted_iota(jnp.int32, (TOK, TOK), 1) % QUAD < LIVE
    for head in range(GROUP):
        high, low = halves_of(rows[:, TOK * head : TOK * (head + 1)])
        value = mm(high, col_map_ref[...]) + mm(low, col_map_ref[...])
        out_ref[:, TOK * head : TOK * (head + 1)] = jnp.where(live, value, FAR)


BIAS_SCRATCH = (
    pltpu.VMEM((16 * GROUP, 128), F32),
    pltpu.VMEM((16 * GROUP, 128), F32),
    pltpu.VMEM((160, KEYS), F32),
)


def table_body(sum_ref, base_ref, row_back_ref, col_map_ref, out_ref, row, left, right, strip):
    high, low = halves_of(sum_ref[...])
    turned = [
        mm_nt(high[:, TOK * head : TOK * (head + 1)], col_map_ref[...])
        + mm_nt(low[:, TOK * head : TOK * (head + 1)], col_map_ref[...])
        for head in range(GROUP)
    ]
    high, low = halves_of(jnp.concatenate(turned, axis=1))
    strip[...] = mm(row_back_ref[...], high) + mm(row_back_ref[...], low)
    for head in range(GROUP):
        total = jnp.zeros((16, 256), F32)
        for line in range(WIN):
            block = strip[16 * line : 16 * (line + 1), TOK * head : TOK * (head + 1)]
            wide = jnp.concatenate([block, jnp.zeros((16, 128), F32)], axis=1)
            start = (WIN - 1 - line) * WIN
            total = total + (pltpu.roll(wide, start, 1) if start else wide)
        left[pl.ds(head, 16, stride=GROUP), :] = total[:, :128]
        right[pl.ds(head, 16, stride=GROUP), :] = total[:, 128:]
    onehot = entry_onehot(base_ref)
    high, low = halves_of(jnp.concatenate([left[0:LINES, :], right[0:LINES, :]], axis=1))
    spread = mm_nt(high, onehot) + mm_nt(low, onehot)
    table = spread[0:GROUP, :]
    for col in range(1, WIN):
        table = table + pltpu.roll(spread[GROUP * col : GROUP * (col + 1), :], col, 1)
    out_ref[row : row + GROUP, :] = table[:, :256]
    out_ref[row + GROUP : row + 2 * GROUP, :] = jnp.concatenate(
        [table[:, 256:], jnp.zeros((GROUP, 128), F32)], axis=1
    )


def pack_kernel(place, w_qkv_ref, w_proj_ref, order_ref, first_ref, second_ref, part_ref):
    for layer, out_ref in enumerate((first_ref, second_ref)):
        mixed = mm(w_qkv_ref[layer], order_ref[...]).astype(BF16)
        for part in range(3):
            out_ref[512 * part : 512 * (part + 1), :] = mixed[:, 256 * part : 256 * (part + 1)]
        for part in range(2):
            out_ref[ROWS_QKV + 256 * part : ROWS_QKV + 256 * (part + 1), :] = w_proj_ref[
                layer, :, 256 * part : 256 * (part + 1)
            ]
    start = place[COL] * HALF_ATT + place[NEAR] * QUARTER_ATT
    part_ref[...] = second_ref[pl.ds(pl.multiple_of(start, QUARTER_ATT), QUARTER_ATT), :]


def pack_weights(place, w_qkv, w_proj, order):
    return run_kernel(
        pack_kernel,
        [place, w_qkv, w_proj, order],
        [pltpu.HBM((ROWS_ATT, 256), BF16)] * 2 + [shape_of((QUARTER_ATT, 256), BF16)],
        specs={0: SMEM},
    )


def join_pack(place_ref, mine, theirs, out):
    out[pl.ds(pl.multiple_of(place_ref[COL] * HALF_ATT, HALF_ATT), HALF_ATT), :] = mine[...]
    out[pl.ds(pl.multiple_of((1 - place_ref[COL]) * HALF_ATT, HALF_ATT), HALF_ATT), :] = theirs[...]


def bias_of(table, base, row_map, col_map):
    return run_kernel(
        bias_body,
        [table, base, row_map, col_map],
        [shape_of((TOK, KEYS), F32)],
        BIAS_SCRATCH,
    )[0]


def project(normed, pack_ref, qv_ref):
    parts = [mm(normed, pack_ref[512 * part : 512 * (part + 1), :]) for part in range(3)]
    return (
        (parts[0] + qv_ref[0:1, :]).astype(BF16),
        parts[1].astype(BF16),
        (parts[2] + qv_ref[1:2, :]).astype(BF16),
    )


def spread_heads(ref, value, heads_ref):
    for head in range(GROUP):
        lines = slice(TOK * head, TOK * (head + 1))
        ref[lines, :] = value * heads_ref[lines, :]


def attend(qkv_ref, base, bias_ref, region, heads_ref, probs_ref, probs_base, stack, wide):
    rows = pl.ds(base, TOK)
    spread_heads(stack, qkv_ref[rows, 256:512], heads_ref)
    logits = mm_nt(qkv_ref[rows, 0:256], stack[...])
    for head in range(GROUP):
        lanes = slice(TOK * head, TOK * (head + 1))
        score = logits[:, lanes] * SCALE + bias_ref[:, lanes]
        if region is not None:
            score = score + region
        grown = jnp.exp(score - jnp.max(score, axis=-1, keepdims=True))
        probs = (grown / jnp.sum(grown, axis=-1, keepdims=True)).astype(BF16)
        wide[:, lanes] = probs
        probs_ref[pl.ds(probs_base + TOK * head, TOK), :] = probs
    spread_heads(stack, qkv_ref[rows, 512:768], heads_ref)
    return mm(wide[...], stack[...]).astype(BF16)


def attend_back(qkv_ref, base, grad, heads_ref, probs_ref, probs_base, total_ref, stack, wide, tall, mixed_ref):
    rows = pl.ds(base, TOK)
    spread_heads(stack, qkv_ref[rows, 512:768], heads_ref)
    grad_probs = mm_nt(grad, stack[...])
    for head in range(GROUP):
        lanes = slice(TOK * head, TOK * (head + 1))
        probs = probs_ref[pl.ds(probs_base + TOK * head, TOK), :].astype(F32)
        part = grad_probs[:, lanes]
        centre = jnp.sum(probs * part, axis=-1, keepdims=True)
        inner = (probs * (part - centre)).astype(BF16)
        wide[:, lanes] = inner
        tall[lanes, :] = inner
        total_ref[:, lanes] = total_ref[:, lanes] + inner.astype(F32)
    spread_heads(stack, grad, heads_ref)
    mixed_ref[rows, 512:768] = mm_tn(probs_ref[pl.ds(probs_base, KEYS), :], stack[...]).astype(BF16)
    spread_heads(stack, qkv_ref[rows, 256:512], heads_ref)
    mixed_ref[rows, 0:256] = (mm(wide[...], stack[...]) * SCALE).astype(BF16)
    spread_heads(stack, qkv_ref[rows, 0:256], heads_ref)
    mixed_ref[rows, 256:512] = (mm_tn(tall[...], stack[...]) * SCALE).astype(BF16)


def project_out(context, pack_ref):
    return jnp.concatenate(
        [mm(context, pack_ref[ROWS_QKV + 256 * part : ROWS_QKV + 256 * (part + 1), :]) for part in range(2)],
        axis=1,
    )


def project_out_back(grad, pack_ref):
    return (
        mm_nt(grad[:, :256], pack_ref[ROWS_QKV : ROWS_QKV + 256, :])
        + mm_nt(grad[:, 256:], pack_ref[ROWS_QKV + 256 : ROWS_ATT, :])
    ).astype(BF16)


def project_back(mixed_ref, pack_ref):
    total = mm_nt(mixed_ref[:, 0:256], pack_ref[0:512, :])
    for part in range(1, 3):
        total = total + mm_nt(mixed_ref[:, 256 * part : 256 * (part + 1)], pack_ref[512 * part : 512 * (part + 1), :])
    return total


ATTEND_SCRATCH = (pltpu.VMEM((KEYS, SPAN), BF16), pltpu.VMEM((TOK, KEYS), BF16))


def attention_plain_kernel(
    place_ref, own, other, gain, bias, pack, qv, offset, heads,
    whole, normed_out, qkv, probs, context, part_out, stack, wide, buf,
):
    here = place_ref[HEAD]
    buf[...] = jnp.zeros(buf.shape, F32)
    enter_rows(own, buf, 0)
    enter_rows(other, buf, TILE)
    whole[pl.ds(pl.multiple_of(here * TILE, TILE), TILE), :] = buf[:TILE, :].astype(BF16)
    whole[pl.ds(pl.multiple_of((1 - here) * TILE, TILE), TILE), :] = buf[TILE:, :].astype(BF16)
    unit, _ = norm_parts(whole[...].astype(F32))
    normed_out[...] = (unit * gain[...] + bias[...]).astype(BF16)
    for part, value in enumerate(project(normed_out[...], pack, qv)):
        qkv[:, 256 * part : 256 * (part + 1)] = value

    def window(place, carry):
        base = pl.multiple_of(place * TOK, TOK)
        context[pl.ds(base, TOK), :] = attend(
            qkv, base, offset, None, heads, probs, pl.multiple_of(place * KEYS, KEYS), stack, wide
        )
        return carry

    lax.fori_loop(0, PAIR // TOK, window, 0)
    part_out[...] = project_out(context[...], pack).astype(BF16)


def attention_shifted_kernel(
    place_ref, stay, come, gain, bias, gain2, bias2, pack_a, pack_mine, pack_theirs, qv_a, qv_b, off_a, off_b,
    ids_q, ids_k, heads, b_proj,
    keep, normed_out, qkv_a, qkv_b, probs_a, probs_b, context_a, context_b, middle_out, second_out, stack, wide,
    pack_b,
):
    join_pack(place_ref, pack_mine, pack_theirs, pack_b)
    join_quads(keep, 0, stay, come, 4)
    unit, _ = norm_parts(keep[...].astype(F32))
    normed_out[...] = (unit * gain[...] + bias[...]).astype(BF16)
    total = keep[...].astype(F32) + b_proj[...]
    for pack, qv, off, qkv, probs, context in (
        (pack_a, qv_a, off_a, qkv_a, probs_a, context_a),
        (pack_b, qv_b, off_b, qkv_b, probs_b, context_b),
    ):
        for part, value in enumerate(project(normed_out[...], pack, qv)):
            qkv[:, 256 * part : 256 * (part + 1)] = value

        def window(place, carry):
            base = pl.multiple_of(place * TOK, TOK)
            region = jnp.where(ids_q[pl.ds(base, TOK), :] != ids_k[place], -100.0, 0.0)
            context[pl.ds(base, TOK), :] = attend(
                qkv, base, off, region, heads, probs, pl.multiple_of(place * KEYS, KEYS), stack, wide
            )
            return carry

        lax.fori_loop(0, TILE // TOK, window, 0)
        total = total + project_out(context[...], pack)
    middle_out[...] = total
    unit, _ = norm_parts(total)
    second_out[...] = (unit * gain2[...] + bias2[...]).astype(BF16)


def gelu_parts(hidden):
    chance = 0.5 * (1.0 + lax.erf(hidden * ROOT_HALF))
    slope = chance + hidden * (jnp.exp(-0.5 * hidden * hidden) * ROOT_TWO_PI)
    return (hidden * chance).astype(BF16), slope.astype(BF16)


CHUNK = 256


def mlp_plain_kernel(
    place_ref, whole, part_own, part_other, b_proj, gain, bias, w_fc1, b_fc1, w_fc2, b_fc2,
    middle, second, active, slope, keep, send, spun,
):
    here = place_ref[HEAD]
    middle[...] = (
        whole[...].astype(F32) + (part_own[...].astype(F32) + part_other[...].astype(F32)) + b_proj[...]
    )
    unit, _ = norm_parts(middle[...])
    second[...] = (unit * gain[...] + bias[...]).astype(BF16)
    for place in range(1024 // CHUNK):
        lanes = slice(CHUNK * place, CHUNK * (place + 1))
        hidden = mm(second[...], w_fc1[0, :, lanes]) + b_fc1[:, lanes]
        active[:, lanes], slope[:, lanes] = gelu_parts(hidden)
    out = mm(active[...], w_fc2[0])
    spun[0 : PAIR - UNIT, :] = out[UNIT:, :]
    spun[PAIR - UNIT :, :] = out[:UNIT, :]
    send[...] = spun[pl.ds((1 - here) * TILE, TILE), :].astype(BF16)
    spun[0 : PAIR - UNIT, :] = spun[0 : PAIR - UNIT, :] + middle[UNIT:, :]
    spun[PAIR - UNIT :, :] = spun[PAIR - UNIT :, :] + middle[:UNIT, :]
    keep[...] = spun[pl.ds(here * TILE, TILE), :] + b_fc2[...]


def mlp_shifted_kernel(
    place_ref, own, other, grad_own, grad_other, grad_far, w_fc1, b_fc1, w_fc2,
    second, grad, active, inner, keep, send, back_keep, back_send, small, slope, spun,
):
    here = place_ref[HEAD]
    mine = pl.ds(pl.multiple_of(here * TILE, TILE), TILE)
    theirs = pl.ds(pl.multiple_of((1 - here) * TILE, TILE), TILE)
    spun[mine, :] = grad_own[...]
    spun[theirs, :] = grad_other[...]
    grad[0 : 7 * UNIT, :] = spun[UNIT:, :]
    grad[7 * UNIT :, :] = grad_far[...]
    second[mine, :] = own[...]
    second[theirs, :] = other[...]
    for place in range(1024 // CHUNK):
        lanes = slice(CHUNK * place, CHUNK * (place + 1))
        hidden = mm(second[...], w_fc1[0, :, lanes]) + b_fc1[:, lanes]
        active[:, lanes], slope[:, lanes] = gelu_parts(hidden)
    for place in range(1024 // CHUNK):
        lanes = slice(CHUNK * place, CHUNK * (place + 1))
        back = mm_nt(grad[...], w_fc2[0, lanes, :]) * slope[:, lanes].astype(F32)
        inner[:, lanes] = back.astype(BF16)
    back_keep[...] = mm_nt(inner[mine, :], w_fc1[0])
    back_send[...] = mm_nt(inner[theirs, :], w_fc1[0]).astype(BF16)
    keep[...] = mm(active[mine, :], w_fc2[0])
    send[...] = mm(active[theirs, :], w_fc2[0]).astype(BF16)
    put_row(small, 0, column_sum(inner[...].astype(F32)))
    small[4:, :] = jnp.zeros((4, 256), F32)


def mlp_plain_back_kernel(
    place_ref, own, other, slope, w_fc1, w_fc2,
    grad, inner, back, spun,
):
    for which, value in enumerate((own, other)):
        here = place_ref[HEAD] if which == 0 else 1 - place_ref[HEAD]
        start = pl.multiple_of(here * TILE, TILE)
        for unit in range(4):
            lines = slice(QUAD * unit, QUAD * (unit + 1))
            spun[pl.ds(start + UNIT * unit, QUAD), :] = value[4 * QUAD + QUAD * unit : 4 * QUAD + QUAD * (unit + 1), :]
            spun[pl.ds(start + UNIT * unit + QUAD, QUAD), :] = value[lines, :]
    grad[0:UNIT, :] = spun[PAIR - UNIT :, :]
    grad[UNIT:, :] = spun[0 : PAIR - UNIT, :]
    for place in range(1024 // CHUNK):
        lanes = slice(CHUNK * place, CHUNK * (place + 1))
        value = mm_nt(grad[...], w_fc2[0, lanes, :]) * slope[:, lanes].astype(F32)
        inner[:, lanes] = value.astype(BF16)
    back[...] = mm_nt(inner[...], w_fc1[0]).astype(BF16)


def deal_halves(place_ref, whole, keep, send, half, base=0, start=0):
    mine = pl.multiple_of(place_ref[COL] * half, half)
    theirs = pl.multiple_of((1 - place_ref[COL]) * half, half)
    keep[start : start + half, :] = whole[pl.ds(base + mine, half), :]
    send[start : start + half, :] = whole[pl.ds(base + theirs, half), :]


def mlp_weights_kernel(place_ref, second, active, grad, inner, keep, send, out):
    for place in range(4):
        lanes = slice(256 * place, 256 * (place + 1))
        out[512 * place : 512 * (place + 1), :] = mm_tn(second[...], inner[:, lanes]).astype(BF16)
    for place in range(2):
        lanes = slice(256 * place, 256 * (place + 1))
        start = 2048 + 1024 * place
        out[start : start + 1024, :] = mm_tn(active[...], grad[:, lanes]).astype(BF16)
    deal_halves(place_ref, out, keep, send, ROWS_MLP // 2)


def mlp_weights(place, second, active, grad, inner):
    return run_kernel(
        mlp_weights_kernel,
        [place, second, active, grad, inner],
        [shape_of((ROWS_MLP // 2, 256), BF16)] * 2,
        [pltpu.VMEM((ROWS_MLP, 256), BF16)],
        specs={0: SMEM},
    )


def attention_shifted_back_kernel(
    place_ref, grad_all, back_own, back_other, middle, entry, gain, gain2, qkv_a, qkv_b, probs_a, probs_b,
    pack_a, pack_mine, pack_theirs, heads,
    grad_low, mixed_a, mixed_b, total_a, total_b, stay_main, send_main, edge, small,
    stack, wide, tall, grad_context, below, pack_b,
):
    join_pack(place_ref, pack_mine, pack_theirs, pack_b)
    here = place_ref[HEAD]
    upstream = grad_all[pl.ds(pl.multiple_of(here * TILE, TILE), TILE), :].astype(F32)
    back = back_own[...] + back_other[...].astype(F32)
    unit, inverse = norm_parts(middle[...])
    put_row(small, 0, column_sum(back * unit))
    put_row(small, 2, column_sum(back))
    put_row(small, 4, column_sum(upstream))
    grad_middle = upstream + norm_back(back, gain2[...], unit, inverse)
    grad_low[...] = grad_middle.astype(BF16)
    put_row(small, 6, column_sum(grad_low[...].astype(F32)))
    first = jnp.zeros((TILE, WIDTH), F32)
    for pack, qkv, probs, mixed, total in (
        (pack_a, qkv_a, probs_a, mixed_a, total_a),
        (pack_b, qkv_b, probs_b, mixed_b, total_b),
    ):
        grad_context[...] = project_out_back(grad_low[...], pack)
        total[...] = jnp.zeros((TOK, KEYS), F32)

        def window(place, carry):
            base = pl.multiple_of(place * TOK, TOK)
            attend_back(
                qkv, base, grad_context[pl.ds(base, TOK), :], heads, probs, pl.multiple_of(place * KEYS, KEYS),
                total, stack, wide, tall, mixed,
            )
            return carry

        lax.fori_loop(0, TILE // TOK, window, 0)
        first = first + project_back(mixed, pack)
    unit, inverse = norm_parts(entry[...].astype(F32))
    put_row(small, 8, column_sum(first * unit))
    put_row(small, 10, column_sum(first))
    put_row(small, 12, column_sum(mixed_a[...].astype(F32)))
    small[15:16, :] = jnp.zeros((1, 256), F32)
    put_row(small, 16, column_sum(mixed_b[...].astype(F32)))
    small[19:24, :] = jnp.zeros((5, 256), F32)
    below[...] = grad_middle + norm_back(first, gain[...], unit, inverse)
    part_quads(below, stay_main, send_main, 3)
    edge[...] = below[3 * UNIT :, :].astype(BF16)


def attention_plain_back_kernel(
    place_ref, grad, back_own, back_other, middle, whole, gain, gain2, qkv, probs, pack, heads, inner,
    grad_low, mixed, total, first_keep, first_send, kept, small, stack, wide, tall, grad_context, first,
):
    here = place_ref[HEAD]
    mine = pl.ds(pl.multiple_of(here * TILE, TILE), TILE)
    theirs = pl.ds(pl.multiple_of((1 - here) * TILE, TILE), TILE)
    back = back_own[...].astype(F32) + back_other[...].astype(F32)
    unit, inverse = norm_parts(middle[...])
    share = back_own[...].astype(F32)
    put_row(small, 0, column_sum(share * unit))
    put_row(small, 2, column_sum(share))
    put_row(small, 4, column_sum(grad[mine, :].astype(F32)))
    first[...] = grad[...].astype(F32) + norm_back(back, gain2[...], unit, inverse)
    kept[...] = first[mine, :]
    grad_low[...] = first[...].astype(BF16)
    put_row(small, 6, column_sum(grad_low[mine, :].astype(F32)))
    grad_context[...] = project_out_back(grad_low[...], pack)
    total[...] = jnp.zeros((TOK, KEYS), F32)

    def window(place, carry):
        base = pl.multiple_of(place * TOK, TOK)
        attend_back(
            qkv, base, grad_context[pl.ds(base, TOK), :], heads, probs, pl.multiple_of(place * KEYS, KEYS),
            total, stack, wide, tall, mixed,
        )
        return carry

    lax.fori_loop(0, PAIR // TOK, window, 0)
    first[...] = project_back(mixed, pack)
    first_keep[...] = first[mine, :]
    first_send[...] = first[theirs, :].astype(BF16)
    unit, _ = norm_parts(whole[...].astype(F32))
    put_row(small, 8, column_sum(first[...] * unit))
    put_row(small, 10, column_sum(first[...]))
    put_row(small, 12, column_sum(mixed[...].astype(F32)))
    small[15:16, :] = jnp.zeros((1, 256), F32)
    put_row(small, 16, column_sum(inner[...].astype(F32)))
    small[20:24, :] = jnp.zeros((4, 256), F32)


def attention_weights_body(normed, mixed, context, grad_low, order, out, start):
    turned = [mm_tn(normed[...], mixed[:, 256 * part : 256 * (part + 1)]).astype(BF16) for part in range(3)]
    canon = mm_nt(jnp.concatenate(turned, axis=1), order[...]).astype(BF16)
    for part in range(3):
        out[start + 512 * part : start + 512 * (part + 1), :] = canon[:, 256 * part : 256 * (part + 1)]
    for part in range(2):
        lines = slice(start + ROWS_QKV + 256 * part, start + ROWS_QKV + 256 * (part + 1))
        out[lines, :] = mm_tn(context[...], grad_low[:, 256 * part : 256 * (part + 1)]).astype(BF16)


def attention_weights_plain_kernel(place_ref, normed, mixed, context, grad_low, order, keep, send, out):
    attention_weights_body(normed, mixed, context, grad_low, order, out, 0)
    deal_halves(place_ref, out, keep, send, HALF_ATT)


def attention_weights_shifted_kernel(
    place_ref, normed, mixed_a, mixed_b, context_a, context_b, grad_low, order, mlp_keep, mlp_send, keep, send, out
):
    attention_weights_body(normed, mixed_a, context_a, grad_low, order, out, 0)
    attention_weights_body(normed, mixed_b, context_b, grad_low, order, out, ROWS_ATT)
    for which, mlp, ref in ((place_ref[COL], mlp_keep, keep), (1 - place_ref[COL], mlp_send, send)):
        for block in range(GROUP):
            first = 4 * EIGHTH * block
            ref[first : first + 2 * EIGHTH, :] = mlp[2 * EIGHTH * block : 2 * EIGHTH * (block + 1), :]
            for part in range(2):
                start = pl.multiple_of(which * HALF_ATT, HALF_ATT) + part * ROWS_ATT + EIGHTH * block
                first = EIGHTH * (4 * block + 2 + part)
                ref[first : first + EIGHTH, :] = out[pl.ds(start, EIGHTH), :]


def table_kernel(total, base, row_back, col_map, out, left, right, strip):
    table_body(total, base, row_back, col_map, out, 0, left, right, strip)


def table_of(total, base, row_back, col_map):
    return run_kernel(
        table_kernel, [total, base, row_back, col_map], [shape_of((2 * GROUP, 256), F32)], BIAS_SCRATCH
    )[0]


def last_kernel(place_ref, whole, gain, keep, other, kept, out, buf):
    here = place_ref[HEAD]
    unit, inverse = norm_parts(whole[pl.ds(pl.multiple_of(here * TILE, TILE), TILE), :].astype(F32))
    buf[...] = kept[...] + norm_back(keep[...] + other[:TILE, :].astype(F32), gain[...], unit, inverse)
    leave_rows(buf, out)


def band_pairs(first, second):
    return [(band * 2 + col, (band ^ (first if col == 0 else second)) * 2 + col) for band in range(8) for col in range(2)]


STEP_PAIRS = (
    [(band * 2 + col, band * 2 + 1 - col) for band in range(8) for col in range(2)],
    band_pairs(1, 2),
    band_pairs(2, 1),
    band_pairs(4, 4),
)


def exchange(value, step):
    return lax.ppermute(value, ("band", "col"), STEP_PAIRS[step])


def double_kernel(place_ref, mine, come, out, *, step):
    half = mine.shape[0]
    out[pl.ds(pl.multiple_of(place_ref[COL + step] * half, half), half), :] = mine[...]
    out[pl.ds(pl.multiple_of((1 - place_ref[COL + step]) * half, half), half), :] = come[...]


def double(place, mine, come, step):
    return run_kernel(
        partial(double_kernel, step=step),
        [place, mine, come],
        [shape_of((2 * mine.shape[0], 256), BF16)],
        specs={0: SMEM},
    )[0]


def after(value, *others):
    return lax.optimization_barrier((value,) + others)[0]


def add_low(left, right):
    return (left.astype(F32) + right.astype(F32)).astype(BF16)


class PageSum:
    def __init__(self, place, kept, send, across=False):
        self.place, self.kept, self.sent, self.across, self.stage = place, kept, send, across, 0
        self.come = exchange(send, 0)

    def tie(self, *others):
        self.kept = after(self.kept, *others)

    def advance(self):
        self.stage += 1
        stage = self.stage
        kept, come = self.kept, self.come
        rows = kept.shape[0]
        if stage < 4:
            half = rows // 2
            bit = self.place[COL + stage]

            def half_at(value, which):
                return lax.dynamic_slice_in_dim(value, which * half, half, 0)

            self.sent = add_low(half_at(kept, 1 - bit), half_at(come, 1 - bit))
            self.kept = add_low(half_at(kept, bit), half_at(come, bit))
            self.come = exchange(self.sent, stage)
            return
        if stage == 4 and self.across:
            start = rows // 4 * 3
            self.sent = add_low(kept[start:], come[start:])
            self.kept = add_low(kept[:start], come[:start])
            self.come = swap_head(self.sent)
            return
        if self.across:
            stage -= 1
            if stage == 4:
                start = rows - come.shape[0]
                self.kept = jnp.concatenate([kept[:start], add_low(kept[start:], come)], axis=0)
        elif stage == 4:
            self.kept = add_low(kept, come)
        if stage > 4:
            bit = self.place[COL + 8 - stage]
            whole = jnp.zeros((2 * rows, 256), BF16)
            whole = lax.dynamic_update_slice_in_dim(whole, kept, bit * rows, 0)
            self.kept = lax.dynamic_update_slice_in_dim(whole, come, (1 - bit) * rows, 0)
        self.sent = self.kept
        self.come = exchange(self.sent, 7 - stage)

    @property
    def halves(self):
        return self.kept, self.come


def both_halves(place_ref, mine, come):
    return (place_ref[COL], mine), (1 - place_ref[COL], come)


def unpack_att(whole, qkv, proj):
    for part in range(3):
        qkv[0, :, 256 * part : 256 * (part + 1)] = whole[512 * part : 512 * (part + 1), :].astype(F32)
    for part in range(2):
        start = ROWS_QKV + 256 * part
        proj[0, :, 256 * part : 256 * (part + 1)] = whole[start : start + 256, :].astype(F32)


def unpack_mlp(whole, fc1, fc2):
    for part in range(4):
        fc1[0, :, 256 * part : 256 * (part + 1)] = whole[512 * part : 512 * (part + 1), :].astype(F32)
    for part in range(2):
        start = 2048 + 1024 * part
        fc2[0, :, 256 * part : 256 * (part + 1)] = whole[start : start + 1024, :].astype(F32)


def unpack_layer_kernel(place_ref, mine, come, qkv, proj, fc1, fc2, att_whole, mlp_whole):
    for which, value in both_halves(place_ref, mine, come):
        for block in range(GROUP):
            first = 3 * EIGHTH * block
            start = pl.multiple_of(which * (ROWS_MLP // 2), 16) + 2 * EIGHTH * block
            mlp_whole[pl.ds(start, 2 * EIGHTH), :] = value[first : first + 2 * EIGHTH, :]
            start = pl.multiple_of(which * HALF_ATT, 16) + EIGHTH * block
            att_whole[pl.ds(start, EIGHTH), :] = value[first + 2 * EIGHTH : first + 3 * EIGHTH, :]
    unpack_att(att_whole, qkv, proj)
    unpack_mlp(mlp_whole, fc1, fc2)


def unpack_mlp_kernel(place_ref, mine, come, *refs):
    fc1, fc2, whole = refs[-3:]
    for which, value in both_halves(place_ref, mine, come):
        whole[pl.ds(pl.multiple_of(which * (ROWS_MLP // 2), 16), ROWS_MLP // 2), :] = value[...]
    unpack_mlp(whole, fc1, fc2)


SMALLS = 256
TABLE_ROWS = (40, 56)


def unpack_last_kernel(
    place_ref, mine, come, order_qv, qkv_in, proj_in,
    qkv, proj, gain, bias, b_qv, table, b_proj, b_fc1, b_fc2, whole, sums,
):
    for which, value in both_halves(place_ref, mine, come):
        whole[pl.ds(pl.multiple_of(which * HALF_ATT, 16), HALF_ATT), :] = value[:HALF_ATT, :]
        start = pl.multiple_of(which * (SMALLS // 2), 16)
        sums[pl.ds(start, SMALLS // 2), :] = value[HALF_ATT:, :].astype(F32)
    unpack_att(whole, qkv, proj)

    for layer, (norm1, norm2) in enumerate(((8, 0), (20, 12))):
        for which, row in enumerate((norm1, norm2)):
            for part in range(2):
                lanes = slice(256 * part, 256 * (part + 1))
                gain[layer, which : which + 1, lanes] = sums[row + part : row + part + 1, :]
                bias[layer, which : which + 1, lanes] = sums[row + 2 + part : row + 3 + part, :]
    for layer, base in enumerate((0, 12)):
        for part in range(2):
            lanes = slice(256 * part, 256 * (part + 1))
            b_fc2[layer : layer + 1, lanes] = sums[base + 4 + part : base + 5 + part, :]
            b_proj[layer : layer + 1, lanes] = sums[base + 6 + part : base + 7 + part, :]
    for layer, base in enumerate((32, 36)):
        for part in range(4):
            b_fc1[layer : layer + 1, 256 * part : 256 * (part + 1)] = sums[base + part : base + part + 1, :]
    for layer, base in enumerate((28, 24)):
        row = jnp.concatenate([sums[base : base + 1, :], sums[base + 2 : base + 3, :]], axis=1)
        b_qv[layer : layer + 1, :] = mm(row.astype(BF16), order_qv[...])
    for layer, base in enumerate(TABLE_ROWS):
        rows = jnp.concatenate(
            [sums[base : base + GROUP, :], sums[base + GROUP : base + 2 * GROUP, :128]], axis=1
        )
        table[layer] = rows[:, : table.shape[2]]


def swap_head(value):
    return lax.ppermute(value, "head", [(0, 1), (1, 0)])


def fast_device(
    act_in, ln_gain, ln_bias, w_qkv, b_qv, rel_table, w_proj, b_proj, w_fc1, b_fc1, w_fc2, b_fc2, grad_out
):
    row_map, row_back, col_map, base, order, heads, order_qv, token_row, token_col = constants()
    band = lax.axis_index("band")
    col = lax.axis_index("col")
    head = lax.axis_index("head")
    bands = lax.axis_size("band")
    cols = lax.axis_size("col")
    digit = [(band >> power) & 1 for power in range(3)]
    place = jnp.stack(
        [
            head,
            col,
            jnp.where(col == 0, digit[0], digit[1]),
            jnp.where(col == 0, digit[1], digit[0]),
            digit[2],
            digit[0],
        ]
    ).astype(jnp.int32)
    band_up = [(here, (here - 1) % bands) for here in range(bands)]
    band_down = [(here, (here + 1) % bands) for here in range(bands)]
    col_left = [(here, (here - 1) % cols) for here in range(cols)]
    edge_left = [(here * 2 + 1, (here - 1) % cols * 2 + 1) for here in range(cols)]
    edge_right = [(here * 2 + 1, (here + 1) % cols * 2 + 1) for here in range(cols)]
    gain = [[ln_gain[layer, which][None] for which in range(2)] for layer in range(2)]
    bias = [[ln_bias[layer, which][None] for which in range(2)] for layer in range(2)]
    row_proj = [b_proj[layer][None] for layer in range(2)]
    row_fc1 = [b_fc1[layer][None] for layer in range(2)]
    row_fc2 = [b_fc2[layer][None] for layer in range(2)]
    qv = b_qv.reshape(2, GROUP, 2, HEAD_DIM).transpose(0, 2, 1, 3).reshape(2, 2, SPAN)
    tables = jnp.pad(rel_table, ((0, 0), (0, ENTRIES - rel_table.shape[1]), (0, 0))).transpose(0, 2, 1)

    def rows_bf(count, width=WIDTH):
        return shape_of((count, width), BF16)

    def rows_f32(count, width=WIDTH):
        return shape_of((count, width), F32)

    def saved(count, width=WIDTH, kind=BF16):
        return pltpu.HBM((count, width), kind)

    def far(value):
        return pltpu.with_memory_space_constraint(value, pltpu.HBM)

    x_other = swap_head(act_in)
    pack0, pack1, pack1_part = pack_weights(place, far(w_qkv), far(w_proj), order)
    pack1_part = swap_head(pack1_part)
    small1 = jnp.concatenate([tables[1], jnp.pad(qv[1], ((0, 6), (0, ENTRIES - SPAN)))], axis=0)
    small1_other = swap_head(small1)
    off0 = bias_of(tables[0], base, row_map, col_map)
    whole, normed0, qkv0, probs0, context0, part0 = run_kernel(
        attention_plain_kernel,
        [place, act_in, x_other, gain[0][0], bias[0][0], far(pack0), qv[0], off0, heads],
        [
            rows_bf(PAIR), saved(PAIR), saved(PAIR, 768), saved(4 * KEYS, TOK), saved(PAIR, SPAN), rows_bf(PAIR),
        ],
        ATTEND_SCRATCH + (pltpu.VMEM((PAIR, WIDTH), F32),),
        specs={0: SMEM},
    )
    part0_other = swap_head(part0)

    off1 = bias_of(after(tables[1], part0), base, row_map, col_map)
    grad_send, grad_stay = run_kernel(
        grad_enter_kernel, [after(grad_out, part0)], [rows_bf(4 * QUAD)] * 2, [pltpu.VMEM((TILE, WIDTH), F32)]
    )
    grad_come = lax.ppermute(grad_send, "band", band_up)
    (grad_own,) = run_kernel(grad_join_kernel, [grad_stay, grad_come], [rows_bf(TILE)])
    pack1_part = after(pack1_part, part0)
    near = [(here, here ^ 1) for here in range(bands)]
    pack1_mine = double(place, pack1_part, lax.ppermute(pack1_part, "band", near), NEAR - COL)
    pack1_theirs = lax.ppermute(pack1_mine, "col", [(0, 1), (1, 0)])
    part0 = after(part0, pack1_mine, grad_own, off1)

    middle0, second0, active0, slope0, x1_keep, x1_send = run_kernel(
        mlp_plain_kernel,
        [
            place, whole, part0, part0_other, row_proj[0], gain[0][1], bias[0][1], far(w_fc1), row_fc1[0],
            far(w_fc2), row_fc2[0],
        ],
        [
            saved(PAIR, WIDTH, F32), saved(PAIR), saved(PAIR, 1024), saved(PAIR, 1024), rows_f32(TILE),
            rows_bf(TILE),
        ],
        [pltpu.VMEM((PAIR, WIDTH), F32)],
        specs={0: SMEM, 7: layer_spec(w_fc1, 0), 9: layer_spec(w_fc2, 0)},
    )
    x1_come = swap_head(x1_send)
    off1_other = bias_of(after(small1_other[:GROUP], x1_send), base, row_map, col_map)
    qv1_other = small1_other[GROUP : GROUP + 2, :SPAN]
    tile, edge = run_kernel(enter_entry_kernel, [x1_keep, x1_come], [rows_bf(TILE), rows_bf(UNIT)])
    edge = lax.ppermute(edge, ("col", "head"), edge_left)
    send, stay = run_kernel(roll_ahead_kernel, [place, tile, edge], [rows_bf(4 * QUAD)] * 2, specs={0: SMEM})
    come = lax.ppermute(send, "band", band_up)
    grad_other = swap_head(after(grad_own, tile))

    rows_id = region_ids(WIN * band + jnp.asarray(token_row), WIN * bands)
    cols_id = region_ids(
        2 * WIN * (2 * col + head) + WIN * jnp.arange(2, dtype=jnp.int32)[:, None] + jnp.asarray(token_col)[None],
        4 * WIN * cols,
    )
    ids = (3 * rows_id[None] + cols_id).astype(F32)
    x1, normed1, qkv1a, qkv1b, probs1a, probs1b, context1a, context1b, middle1, second1_own = run_kernel(
        attention_shifted_kernel,
        [
            place, stay, come, gain[1][0], bias[1][0], gain[1][1], bias[1][1], far(pack1),
            pack1_mine, pack1_theirs, qv[1], qv1_other, off1, off1_other, ids.reshape(TILE, 1), ids.reshape(2, 1, TOK), heads,
            row_proj[1],
        ],
        [
            saved(TILE), saved(TILE), saved(TILE, 768), saved(TILE, 768), saved(2 * KEYS, TOK),
            saved(2 * KEYS, TOK), saved(TILE, SPAN), saved(TILE, SPAN), saved(TILE, WIDTH, F32), rows_bf(TILE),
        ],
        ATTEND_SCRATCH + (pltpu.VMEM((ROWS_ATT, 256), BF16),),
        specs={0: SMEM},
    )
    second1_other = swap_head(second1_own)
    grad_far = jnp.where(head == 0, grad_own[:UNIT], grad_other[:UNIT])
    grad_far = lax.ppermute(after(grad_far, second1_own), "col", col_left)
    second1, grad_all, active1, inner1, x2_keep, x2_send, back1_keep, back1_send, small_mlp1 = run_kernel(
        mlp_shifted_kernel,
        [place, second1_own, second1_other, grad_own, grad_other, grad_far, far(w_fc1), row_fc1[1], far(w_fc2)],
        [
            rows_bf(PAIR), rows_bf(PAIR), rows_bf(PAIR, 1024), rows_bf(PAIR, 1024), saved(TILE, WIDTH, F32),
            rows_bf(TILE), rows_f32(TILE), rows_bf(TILE), rows_f32(8, 256),
        ],
        [pltpu.VMEM((PAIR, 1024), BF16), pltpu.VMEM((PAIR, WIDTH), BF16)],
        specs={0: SMEM, 6: layer_spec(w_fc1, 1), 8: layer_spec(w_fc2, 1)},
    )
    back1_other = swap_head(back1_send)
    mlp1_keep, mlp1_send = mlp_weights(place, second1, active1, grad_all, inner1)
    back1_keep = after(back1_keep, mlp1_send)
    grad_low1, mixed1a, mixed1b, total1a, total1b, stay_main, send_main, edge, small_att1 = run_kernel(
        attention_shifted_back_kernel,
        [
            place, grad_all, back1_keep, back1_other, far(middle1), far(x1), gain[1][0], gain[1][1], far(qkv1a),
            far(qkv1b), far(probs1a), far(probs1b), far(pack1), pack1_mine, pack1_theirs, heads,
        ],
        [
            rows_bf(TILE), rows_bf(TILE, 768), rows_bf(TILE, 768), saved(TOK, KEYS, F32), saved(TOK, KEYS, F32),
            rows_bf(3 * QUAD), rows_bf(3 * QUAD), rows_bf(UNIT), rows_f32(24, 256),
        ],
        ATTEND_SCRATCH
        + (
            pltpu.VMEM((KEYS, TOK), BF16),
            pltpu.VMEM((TILE, SPAN), BF16),
            pltpu.VMEM((TILE, WIDTH), F32),
            pltpu.VMEM((ROWS_ATT, 256), BF16),
        ),
        specs={0: SMEM},
    )

    edge_come = lax.ppermute(edge, ("col", "head"), edge_right)
    send, stay = run_kernel(
        roll_back_kernel, [place, stay_main, send_main, edge, edge_come], [rows_bf(4 * QUAD)] * 2, specs={0: SMEM}
    )
    come = lax.ppermute(send, "band", band_down)
    layer1_keep, layer1_send = run_kernel(
        attention_weights_shifted_kernel,
        [
            place, far(after(normed1, send)), mixed1a, mixed1b, far(context1a), far(context1b), grad_low1, order,
            mlp1_keep, mlp1_send,
        ],
        [rows_bf(2 * ROWS_ATT, 256)] * 2,
        [pltpu.VMEM((2 * ROWS_ATT, 256), BF16)],
        specs={0: SMEM},
    )
    own = jnp.concatenate([stay, after(come, layer1_send)], axis=0)
    own_other = swap_head(own)
    come = own
    layer1 = PageSum(place, layer1_keep, after(layer1_send, come), across=True)
    layer1.advance()
    slope0 = after(slope0, layer1.sent)
    grad0, inner0, back0 = run_kernel(
        mlp_plain_back_kernel,
        [
            place, own, own_other, far(slope0), far(w_fc1), far(w_fc2),
        ],
        [rows_bf(PAIR), rows_bf(PAIR, 1024), rows_bf(PAIR)],
        [pltpu.VMEM((PAIR, WIDTH), BF16)],
        specs={0: SMEM, 4: layer_spec(w_fc1, 0), 5: layer_spec(w_fc2, 0)},
    )
    back0_other = swap_head(back0)
    mlp0_keep, mlp0_send = mlp_weights(place, far(second0), far(active0), grad0, inner0)
    table1_send = table_of(far(after(total1b, back0)), base, row_back, col_map)
    table1 = table_of(far(after(total1a, back0)), base, row_back, col_map)
    mlp0 = PageSum(place, mlp0_keep, after(mlp0_send, back0_other))
    layer1.tie(mlp0_send)
    layer1.advance()
    layer1.tie(back0_other, table1, table1_send)
    layer1.advance()
    back0 = after(back0, layer1.sent, mlp0.sent)
    grad_low0, mixed0, total0, first_keep, first_send, kept0, small_att0 = run_kernel(
        attention_plain_back_kernel,
        [
            place, grad0, back0, back0_other, far(middle0), whole, gain[0][0], gain[0][1], far(qkv0), far(probs0),
            far(pack0), heads, inner0,
        ],
        [
            rows_bf(PAIR), rows_bf(PAIR, 768), saved(TOK, KEYS, F32), saved(TILE, WIDTH, F32), rows_bf(TILE),
            saved(TILE, WIDTH, F32),
            rows_f32(24, 256),
        ],
        ATTEND_SCRATCH
        + (pltpu.VMEM((KEYS, TOK), BF16), pltpu.VMEM((PAIR, SPAN), BF16), pltpu.VMEM((PAIR, WIDTH), F32)),
        specs={0: SMEM},
    )
    att0 = PageSum(
        place,
        *run_kernel(
            attention_weights_plain_kernel,
            [place, far(normed0), mixed0, far(context0), grad_low0, order],
            [rows_bf(HALF_ATT, 256)] * 2,
            [pltpu.VMEM((ROWS_ATT, 256), BF16)],
            specs={0: SMEM},
        ),
    )
    shared = after(jnp.concatenate([small_att0[:12], small_att1[:12]], axis=0), att0.sent)
    come = swap_head(jnp.concatenate([shared, small_att1[16:24], table1_send], axis=0))
    table0 = table_of(far(after(total0, shared)), base, row_back, col_map)
    turn = att0.sent

    def take(chain):
        chain.tie(turn)
        chain.advance()
        return chain.sent

    turn = take(mlp0)
    sums = jnp.concatenate(
        [
            shared + come[:24],
            small_att1[12:16] + come[24:28],
            small_att0[12:20],
            small_mlp1[:4],
            table0,
            table1 + come[32:48],
        ],
        axis=0,
    )
    sums = jnp.pad(after(sums, turn).astype(BF16), ((0, SMALLS - sums.shape[0]), (0, 0)))
    sums_keep = lax.dynamic_slice_in_dim(sums, col * (SMALLS // 2), SMALLS // 2, 0)
    sums_send = lax.dynamic_slice_in_dim(sums, (1 - col) * (SMALLS // 2), SMALLS // 2, 0)
    sums_come = exchange(sums_send, 0)
    att0.kept = jnp.concatenate([att0.kept, after(sums_keep, sums_send)], axis=0)
    att0.come = jnp.concatenate([att0.come, sums_come], axis=0)
    turn = take(att0)
    turn = take(layer1)
    turn = take(mlp0)
    x2_come = swap_head(after(x2_send, turn))
    turn = take(layer1)
    turn = take(att0)
    turn = take(mlp0)
    x2_move, x2_stay = run_kernel(
        last_entry_kernel,
        [far(x2_keep), after(x2_come, turn), far(middle1), row_fc2[1]],
        [rows_bf(4 * QUAD)] * 2,
        [pltpu.VMEM((TILE, WIDTH), F32)],
    )
    x2_come = lax.ppermute(x2_move, "band", band_down)
    layer1.tie(x2_move)
    turn = take(layer1)
    turn = take(att0)
    turn = take(mlp0)
    x2_edge = jnp.concatenate([after(x2_come, turn)[3 * QUAD :], x2_stay[3 * QUAD :]], axis=0)
    x2_far = lax.ppermute(x2_edge, ("col", "head"), edge_right)
    turn = take(layer1)
    turn = take(att0)
    turn = take(mlp0)
    x2_edge = jnp.where(head == 1, x2_far, x2_edge)
    other = swap_head(jnp.concatenate([first_send, after(x2_edge, turn)], axis=0))
    turn = take(layer1)
    turn = take(att0)
    turn = take(mlp0)
    grad_in = run_kernel(
        last_kernel,
        [place, whole, gain[0][0], far(first_keep), after(other, turn), far(kept0)],
        [shape_of((WIN, 2 * WIN, WIDTH), F32)],
        [pltpu.VMEM((TILE, WIDTH), F32)],
        specs={0: SMEM},
    )[0]
    act_out = run_kernel(
        leave_kernel,
        [after(other, turn), x2_stay, x2_come],
        [shape_of((WIN, 2 * WIN, WIDTH), F32)],
        [pltpu.VMEM((TILE, WIDTH), F32)],
    )[0]
    att0.tie(grad_in, act_out)
    turn = take(att0)
    turn = take(mlp0)
    shapes = [(2, 512, 768), (2, 256, 512), (2, 512, 1024), (2, 1024, 512)]
    outs = [shape_of(shape, F32) for shape in shapes]
    anywhere = pl.BlockSpec(memory_space=pl.ANY)
    layer1.tie(turn)
    g_qkv, g_proj, g_fc1, g_fc2 = run_kernel(
        unpack_layer_kernel,
        [place, *layer1.halves],
        outs,
        [pltpu.VMEM((ROWS_ATT, 256), BF16), pltpu.VMEM((ROWS_MLP, 256), BF16)],
        specs={0: SMEM},
        out_specs=[layer_spec(out, 1) for out in outs],
    )
    att0.tie(g_proj)
    turn = take(att0)
    g_fc1, g_fc2 = run_kernel(
        unpack_mlp_kernel,
        [place, *mlp0.halves, g_fc1, g_fc2],
        outs[2:],
        [pltpu.VMEM((ROWS_MLP, 256), BF16)],
        specs={0: SMEM, 3: anywhere, 4: anywhere},
        out_specs=[layer_spec(out, 0) for out in outs[2:]],
        aliases={3: 0, 4: 1},
    )
    g_qkv, g_proj, g_gain, g_bias, g_qv, g_table, g_bproj, g_bfc1, g_bfc2 = run_kernel(
        unpack_last_kernel,
        [place, *att0.halves, order_qv, g_qkv, g_proj],
        outs[:2]
        + [
            shape_of(array.shape, F32)
            for array in (ln_gain, ln_bias, b_qv, rel_table.transpose(0, 2, 1), b_proj, b_fc1, b_fc2)
        ],
        [pltpu.VMEM((ROWS_ATT, 256), BF16), pltpu.VMEM((SMALLS, 256), F32)],
        specs={0: SMEM, 4: pl.BlockSpec(memory_space=pl.ANY), 5: pl.BlockSpec(memory_space=pl.ANY)},
        out_specs=[layer_spec(out, 0) for out in outs[:2]] + [VMEM] * 7,
        aliases={4: 0, 5: 1},
    )
    g_table = g_table.transpose(0, 2, 1)
    return (
        act_out, grad_in, g_gain, g_bias, g_qkv, g_qv, g_table, g_proj, g_bproj, g_fc1, g_bfc1, g_fc2, g_bfc2,
    )


def fits(mesh):
    return dict(mesh.shape) == {"band": 8, "col": 2, "head": 2}


def solution(mesh):
    placed = (
        P("band", ("col", "head"), None),
        P(),
        P(),
        P(None, None, "head"),
        P(None, "head"),
        P(None, None, "head"),
        P(None, "head", None),
        P(),
        P(None, None, "head"),
        P(None, "head"),
        P(None, "head", None),
        P(),
        P("band", ("col", "head"), None),
    )
    return jax.shard_map(
        fast_device if fits(mesh) else on_device,
        mesh=mesh,
        in_specs=placed,
        out_specs=(
            P("band", ("col", "head"), None),
            P("band", ("col", "head"), None),
            P(),
            P(),
            P(None, None, "head"),
            P(None, "head"),
            P(None, None, "head"),
            P(None, "head", None),
            P(),
            P(None, None, "head"),
            P(None, "head"),
            P(None, "head", None),
            P(),
        ),
        check_vma=False,
    )
```
